128 devices in a mesh: gx: 16 (over y, z), gy: 8 (over x, core).
Axes of the slice: x: 4, y: 4, z: 4, core: 2. Of those that a mesh axis runs over, the one named last changes fastest.
Arguments:
- tokens: bfloat16 [1024, 18432], P('gy', 'gx'), may hold values from -125 to 125
- norm_gain: bfloat16 [18432], P('gx'), may hold values from 0.099609375 to 1.8984375
- w_query: bfloat16 [18432, 12288], P('gx', 'gy'), may hold values from -0.046875 to 0.046875
- w_keyvalue: bfloat16 [18432, 512], P('gx', 'gy'), may hold values from -0.109375 to 0.109375
- w_out: bfloat16 [12288, 18432], P('gy', 'gx'), may hold values from -0.21875 to 0.21875
- cache_keys: bfloat16 [512, 2048, 256], P(('gx', 'gy')), may hold values from -250 to 250
- cache_values: bfloat16 [512, 2048, 256], P(('gx', 'gy')), may hold values from -15 to 15
- lengths: int32 [512], P(('gx', 'gy')), may hold values from 1024 to 2048, as said below
Outputs:
- mixed: bfloat16 [1024, 18432], P('gy', 'gx')
The draws below stay inside these ranges and needn't reach their ends.
Inputs may be any that keep to these rules, and one draw needn't show every extreme that they name: `lengths`: some request has exactly 2048 live slots and some has exactly 1024.
All inputs are finite; a program needn't handle non-finite values.
Results may differ from the reference program's by a relative error of at most 0.035.
Values may be sent and summed in bfloat16 or wider, within the bound.
No kernel may reach another device: no remote copies, remote signals or barrier semaphores. Data moves between devices by JAX's collectives and lax.ppermute only.
A program may use at most 64 MiB of HBM per device.

```python
import math
import jax
import jax.numpy as jnp
from jax import lax

D = 18432
HEADS = 48
HD = 256
L = 2048
STEPS = 2
HQ = 12288
REQUESTS = 512
TOKENS = 1024
N_GX = 16
N_GY = 8


def draw_tokens(key, part):
    key = jax.random.fold_in(key, 11)
    first_key, second_key = jax.random.split(key, 2)
    rising = 3.0 ** (0.5 * jnp.arange(D, dtype=jnp.float32) / D)
    jitter = jnp.exp(jax.random.uniform(second_key, (D,), jnp.float32, math.log(0.7), math.log(1.4)))
    base = jnp.clip(jax.random.normal(first_key, (TOKENS, D), jnp.float32), -5.0, 5.0)
    values = base * rising * jitter
    return values.astype(jnp.bfloat16)


def draw_cache_keys(key, part):
    key = jax.random.fold_in(key, 23)
    first_key = jax.random.fold_in(key, 0)
    shape = (REQUESTS, L, HD)
    values = jnp.clip(jax.random.normal(first_key, shape, jnp.float32), -6.0, 6.0)
    return values.astype(jnp.bfloat16)


def draw_lengths(key, part):
    key = jax.random.fold_in(key, 37)
    first_key, second_key, third_key = jax.random.split(key, 3)
    counts = jax.random.randint(first_key, (REQUESTS,), L // 2, L + 1)
    longest = jax.random.randint(second_key, (), 0, REQUESTS)
    shortest = (longest + 1 + jax.random.randint(third_key, (), 0, REQUESTS - 1)) % REQUESTS
    counts = counts.at[longest].set(L)
    counts = counts.at[shortest].set(L // 2)
    return counts.astype(jnp.int32)


def steps_of(stream_key, shape, cuts, low, top_value):
    def one(axis_at, shards_of):
        steps = jax.random.uniform(jax.random.fold_in(jax.random.fold_in(stream_key, 6), axis_at), (shards_of,), jnp.float32, low / len(cuts), top_value / len(cuts))
        return jnp.repeat(jnp.exp(steps), shape[axis_at] // shards_of).reshape((-1,) + (1,) * (len(shape) - axis_at - 1))

    gain = one(*cuts[0])
    for cut in cuts[1:]:
        gain = gain * one(*cut)
    return gain


def noise(stream_key, extent, spread, bound, pieces=(), kind=jnp.bfloat16):
    entries = jax.random.normal(stream_key, extent, jnp.float32) * spread
    if len(pieces) > 0:
        entries = steps_of(stream_key, extent, pieces, -0.22, 0.18) * entries
    return jnp.clip(entries, min=-bound, max=bound).astype(kind)


def setup_inputs(seed: int = 0) -> dict:
    seeds = jax.random.split(jax.random.key(seed), 9)
    tokens = draw_tokens(jax.random.fold_in(seeds[8], 71), 0)
    norm_gain = jnp.clip(1.0 + 0.18 * jax.random.normal(seeds[1], (D,), jnp.float32), 0.099609375, 1.8984375).astype(jnp.bfloat16)
    w_query = noise(seeds[2], (D, HQ), D ** -0.5, 0.046875, ((0, 16), (1, 8)))
    w_keyvalue = noise(seeds[3], (D, 2 * HD), (D // 6) ** -0.5, 0.109375, ((0, 16), (1, 8)))
    w_out = noise(seeds[4], (HQ, D), (HQ // 16) ** -0.5, 0.21875, ((0, 8), (1, 16)))
    cache_keys = draw_cache_keys(jax.random.fold_in(seeds[8], 71), 0)
    cache_values = noise(seeds[6], (REQUESTS, L, HD), 2.5, 15.0, ((0, 128),))
    lengths = draw_lengths(jax.random.fold_in(seeds[8], 71), 0)
    return {"tokens": tokens, "norm_gain": norm_gain, "w_query": w_query, "w_keyvalue": w_keyvalue, "w_out": w_out, "cache_keys": cache_keys, "cache_values": cache_values, "lengths": lengths}


def rotate(values, positions):
    half_dim = values.shape[-1] // 2
    freqs = 10000.0 ** (-jnp.arange(half_dim, dtype=jnp.float32) / half_dim)
    angles = positions.astype(jnp.float32)[..., None] * freqs
    cosine = jnp.cos(angles)
    sine = jnp.sin(angles)
    first = values[..., :half_dim]
    second = values[..., half_dim:]
    return jnp.concatenate([first * cosine - second * sine, second * cosine + first * sine], axis=-1)

def attend(query, new_keys, new_values, cache_keys, cache_values, lengths):
    scale = query.shape[-1] ** (-0.5)
    cached = jnp.einsum('rshd,rld->rshl', query.astype(jnp.float32), cache_keys.astype(jnp.float32)) * scale
    valid = jnp.arange(cache_keys.shape[1], dtype=jnp.int32)[None, :] < lengths[:, None]
    cached = jnp.where(valid[:, None, None, :], cached, -jnp.inf)
    fresh = jnp.einsum('rshd,rtd->rsht', query.astype(jnp.float32), new_keys.astype(jnp.float32)) * scale
    count = query.shape[1]
    causal = jnp.arange(count)[None, :] <= jnp.arange(count)[:, None]
    fresh = jnp.where(causal[None, :, None, :], fresh, -jnp.inf)
    top_score = jnp.maximum(lax.optimization_barrier(jnp.max(cached, axis=-1)), lax.optimization_barrier(jnp.max(fresh, axis=-1)))
    cache_weight = jnp.exp(cached - top_score[..., None])
    fresh_weight = jnp.exp(fresh - top_score[..., None])
    denom = lax.optimization_barrier(jnp.sum(cache_weight, axis=-1)) + lax.optimization_barrier(jnp.sum(fresh_weight, axis=-1))
    cache_share = (cache_weight / denom[..., None]).astype(jnp.bfloat16)
    fresh_share = (fresh_weight / denom[..., None]).astype(jnp.bfloat16)
    result = jnp.einsum('rshl,rld->rshd', cache_share.astype(jnp.float32), cache_values.astype(jnp.float32))
    result = result + jnp.einsum('rsht,rtd->rshd', fresh_share.astype(jnp.float32), new_values.astype(jnp.float32))
    return result.astype(jnp.bfloat16)

def reference(tokens, norm_gain, w_query, w_keyvalue, w_out, cache_keys, cache_values, lengths):
    floated = tokens.astype(jnp.float32)
    row_mean = lax.optimization_barrier(jnp.sum(floated, axis=1)) / D
    row_square = lax.optimization_barrier(jnp.sum(floated * floated, axis=1)) / D
    variance = row_square - row_mean * row_mean
    normed = ((floated - row_mean[:, None]) * lax.rsqrt(variance + 1e-05)[:, None] * norm_gain.astype(jnp.float32)).astype(jnp.bfloat16)
    span = D // N_GX
    query_sum = jnp.zeros((TOKENS, HQ), jnp.float32)
    pair_sum = jnp.zeros((TOKENS, 2 * HD), jnp.float32)
    for block_index in range(N_GX):
        block_rows = normed[:, block_index * span:(block_index + 1) * span]
        query_sum = query_sum + jnp.dot(block_rows, w_query[block_index * span:(block_index + 1) * span], preferred_element_type=jnp.float32).astype(jnp.bfloat16).astype(jnp.float32)
        pair_sum = pair_sum + jnp.dot(block_rows, w_keyvalue[block_index * span:(block_index + 1) * span], preferred_element_type=jnp.float32).astype(jnp.bfloat16).astype(jnp.float32)
    query = query_sum.astype(jnp.bfloat16).reshape(REQUESTS, STEPS, HEADS, HD)
    keyvalue = pair_sum.astype(jnp.bfloat16).reshape(REQUESTS, STEPS, 2 * HD)
    positions = lengths[:, None] + jnp.arange(STEPS, dtype=jnp.int32)[None, :]
    rotated_query = rotate(query.astype(jnp.float32), positions[:, :, None]).astype(jnp.bfloat16)
    rotated_key = rotate(keyvalue[..., :HD].astype(jnp.float32), positions).astype(jnp.bfloat16)
    new_value = keyvalue[..., HD:]
    group = 8
    blocks = REQUESTS // group

    def one_block(operands):
        return attend(*operands)
    attended = lax.map(one_block, (rotated_query.reshape(blocks, group, STEPS, HEADS, HD), rotated_key.reshape(blocks, group, STEPS, HD), new_value.reshape(blocks, group, STEPS, HD), cache_keys.reshape(blocks, group, L, HD), cache_values.reshape(blocks, group, L, HD), lengths.reshape(blocks, group)))
    attended = attended.reshape(TOKENS, HQ)
    width_block = HQ // N_GY
    out_sum = jnp.zeros((TOKENS, D), jnp.float32)
    for block_index in range(N_GY):
        out_sum = out_sum + jnp.dot(attended[:, block_index * width_block:(block_index + 1) * width_block], w_out[block_index * width_block:(block_index + 1) * width_block], preferred_element_type=jnp.float32).astype(jnp.bfloat16).astype(jnp.float32)
    return out_sum.astype(jnp.bfloat16)
```

```python
import functools

import jax
import jax.numpy as jnp
from jax import lax
from jax.experimental import pallas as pl
from jax.experimental.pallas import tpu as pltpu
from jax.sharding import PartitionSpec as P

D = 18432
HD = 256
STEPS = 2
VMEM = pl.BlockSpec(memory_space=pltpu.VMEM)
SMEM = pl.BlockSpec(memory_space=pltpu.SMEM)
ANY = pl.BlockSpec(memory_space=pl.ANY)
F32 = jnp.float32
BF16 = jnp.bfloat16


def params():
    return pltpu.CompilerParams(vmem_limit_bytes=50 * 1024 * 1024)


def along_y(value, m):
    return lax.ppermute(value, "gx", [(g, (g // 4 + m) % 4 * 4 + g % 4) for g in range(16)])


def along_z(value, m):
    return lax.ppermute(value, "gx", [(g, g // 4 * 4 + (g + m) % 4) for g in range(16)])


def along_x(value, m):
    return lax.ppermute(value, "gy", [(g, (g // 2 + m) % 4 * 2 + g % 2) for g in range(8)])


def other_core(value):
    return lax.ppermute(value, "gy", [(g, g ^ 1) for g in range(8)])


def project_kernel(place, stats, gain, *refs):
    pieces, (w_query, w_pair), outs = refs[:8], refs[8:10], refs[10:18]
    normed, mean_of, scale_of, weights, sems = refs[18:]
    tiles = w_query.shape[1] // 256
    loads = []
    for t in range(tiles):
        load = pltpu.make_async_copy(
            w_query.at[:, pl.ds(t * 256, 256)], weights.at[t], sems.at[t]
        )
        load.start()
        loads.append(load)
    y, z, x, c = place[0], place[1], place[2], place[3]
    total = stats[0:8, :]
    for g in range(1, 16):
        total = total + stats[g * 8 : g * 8 + 8, :]
    mean = total[:, :128] / D
    variance = total[:, 128:] / D - mean * mean
    mean_columns = mean.T
    scale_columns = lax.rsqrt(variance + 1e-05).T
    for s in range(8):
        mean_of[s] = mean_columns[:, s : s + 1]
        scale_of[s] = scale_columns[:, s : s + 1]
    gains = gain[...].astype(F32)
    for m in range(4):
        source_x = lax.rem(x + 4 - m, 4)
        to_y = lax.rem(source_x + 4 - y, 4)
        for j in range(2):
            source_c = lax.rem(c + j, 2)
            s = source_x * 2 + source_c
            rows = pieces[m * 2 + j][...].astype(F32)
            rows = ((rows - mean_of[s]) * scale_of[s] * gains).astype(BF16)
            for b in range(2):
                to_z = lax.rem(source_c * 2 + b + 4 - z, 4)
                normed[0, to_y, to_z] = rows[b * 64 : b * 64 + 32]
                normed[1, to_z, to_y] = rows[b * 64 + 32 : b * 64 + 64]
    for h in range(2):
        left = normed[h].reshape(512, normed.shape[-1])
        pair = jnp.dot(left, w_pair[...], preferred_element_type=F32).astype(BF16)
        for k in range(4):
            outs[h * 4 + k][:, tiles * 256 :] = pair[k * 128 : k * 128 + 128]
    for t in range(tiles):
        loads[t].wait()
        for h in range(2):
            left = normed[h].reshape(512, normed.shape[-1])
            part = jnp.dot(left, weights[t], preferred_element_type=F32).astype(BF16)
            for k in range(4):
                outs[h * 4 + k][:, t * 256 : t * 256 + 256] = part[k * 128 : k * 128 + 128]


def project(place, stats, gain, pieces, w_query, w_pair):
    depth, width = w_query.shape
    out = jax.ShapeDtypeStruct((128, width + w_pair.shape[1]), BF16)
    return pl.pallas_call(
        project_kernel,
        out_shape=[out] * 8,
        in_specs=[SMEM] + [VMEM] * 10 + [ANY, VMEM],
        out_specs=[VMEM] * 8,
        scratch_shapes=[
            pltpu.VMEM((2, 4, 4, 32, depth), BF16),
            pltpu.VMEM((8, 128, 1), F32),
            pltpu.VMEM((8, 128, 1), F32),
            pltpu.VMEM((width // 256, depth, 256), BF16),
            pltpu.SemaphoreType.DMA((width // 256,)),
        ],
        compiler_params=params(),
        name="project",
    )(place, stats, gain, *pieces, w_query, w_pair)


def add_kernel(pieces, *refs):
    groups = len(refs) // (2 * pieces)
    ins, outs = refs[: groups * pieces], refs[groups * pieces :]
    for g in range(groups):
        total = ins[g * pieces][...].astype(F32)
        for k in range(1, pieces):
            total = total + ins[g * pieces + k][...].astype(F32)
        total = total.astype(BF16)
        rows = total.shape[0] // pieces
        for k in range(pieces):
            outs[g * pieces + k][...] = total[k * rows : k * rows + rows]


def add_and_cut(values, pieces):
    rows, width = values[0].shape
    out = jax.ShapeDtypeStruct((rows // pieces, width), BF16)
    return pl.pallas_call(
        functools.partial(add_kernel, pieces),
        out_shape=[out] * len(values),
        in_specs=[VMEM] * len(values),
        out_specs=[VMEM] * len(values),
        compiler_params=params(),
        name="add_and_cut",
    )(*values)


def attend_kernel(lengths, packed, cosine, sine, keys, values, out, query_rows, new_kv, result):
    request = pl.program_id(0)
    heads = out.shape[1] // HD
    count = 8 * heads

    @pl.when(request == 0)
    def _():
        rows = packed[...].astype(F32)
        cos, sin = cosine[...], sine[...]

        def rotated(first, second):
            return first * cos - second * sin, second * cos + first * sin

        for n in range(count):
            g, h = n // heads, n % heads
            head = rows[g * 8 : g * 8 + 8, h * HD : h * HD + HD]
            for i, half in enumerate(rotated(head[:, :128], head[:, 128:])):
                query_rows[i, pl.ds(n, 8, stride=count), :] = half
        parts = [rows[g * 8 : g * 8 + 8, heads * HD :] for g in range(8)]
        halves = [jnp.concatenate(parts[i : i + 2], axis=-1) for i in range(0, 8, 2)]
        new_kv[0] = jnp.concatenate(rotated(halves[0], halves[1]), axis=-1).astype(BF16)
        new_kv[1] = jnp.concatenate(halves[2:], axis=-1).astype(BF16)

    per = STEPS * count
    start = pl.multiple_of(request * per, per)
    query = jnp.concatenate([query_rows[i, pl.ds(start, per), :] for i in range(2)], axis=-1)
    query = (query.astype(BF16).astype(F32) * HD ** (-0.5)).astype(BF16)
    dims = (((1,), (1,)), ((), ()))
    cached = lax.dot_general(query, keys[0], dims, preferred_element_type=F32)
    slots = lax.broadcasted_iota(jnp.int32, cached.shape, 1)
    cached = jnp.where(slots < lengths[request], cached, -jnp.inf)
    fresh = lax.dot_general(query, new_kv[0], dims, preferred_element_type=F32)
    row_step = lax.broadcasted_iota(jnp.int32, fresh.shape, 0) // count
    key_step = lax.broadcasted_iota(jnp.int32, fresh.shape, 1) - request * STEPS
    fresh = jnp.where((key_step >= 0) & (key_step <= row_step), fresh, -jnp.inf)
    top = jnp.maximum(
        jnp.max(cached, axis=-1, keepdims=True), jnp.max(fresh, axis=-1, keepdims=True)
    )
    cached = jnp.exp(cached - top)
    fresh = jnp.exp(fresh - top)
    denom = jnp.sum(cached, axis=-1, keepdims=True) + jnp.sum(fresh, axis=-1, keepdims=True)
    mixed = jnp.dot(cached.astype(BF16), values[0], preferred_element_type=F32)
    mixed = mixed + jnp.dot(fresh.astype(BF16), new_kv[1], preferred_element_type=F32)
    mixed = mixed / denom
    for i in range(2):
        result[i, pl.ds(start, per), :] = mixed[:, i * 128 : i * 128 + 128]

    @pl.when(request == pl.num_programs(0) - 1)
    def _():
        for g in range(8):
            line = jnp.concatenate(
                [
                    result[i, pl.ds(g * heads + h, 8, stride=count), :]
                    for h in range(heads)
                    for i in range(2)
                ],
                axis=-1,
            )
            out[g * 8 : g * 8 + 8, :] = line


def attend(packed, cosine, sine, cache_keys, cache_values, lengths):
    requests, slots, _ = cache_keys.shape
    width = packed.shape[1] // HD * HD
    count = 8 * (width // HD)
    whole = lambda *shape: pl.BlockSpec(shape, lambda r, *_: (0,) * len(shape))
    cache = pl.BlockSpec((1, slots, HD), lambda r, *_: (r, 0, 0))
    return pl.pallas_call(
        attend_kernel,
        out_shape=jax.ShapeDtypeStruct((64, width), F32),
        grid_spec=pltpu.PrefetchScalarGridSpec(
            num_scalar_prefetch=1,
            grid=(requests,),
            in_specs=[whole(*packed.shape), whole(8, 128), whole(8, 128), cache, cache],
            out_specs=whole(64, width),
            scratch_shapes=[
                pltpu.VMEM((2, 8 * count, 128), F32),
                pltpu.VMEM((2, 8, HD), BF16),
                pltpu.VMEM((2, 8 * count, 128), F32),
            ],
        ),
        compiler_params=params(),
        name="attend",
    )(lengths, packed, cosine, sine, cache_keys, cache_values).astype(BF16)


def mix_kernel(want, place, *refs):
    first, second = refs[:4], refs[4:8]
    w_out, out, rows = refs[8], refs[9], refs[10]
    y, z, x, c = place[0], place[1], place[2], place[3]
    core = lax.rem(c + want, 2)
    for m_z in range(4):
        token_z = lax.rem(z + 4 - m_z, 4)

        @pl.when(token_z // 2 == core)
        def _():
            for m_y in range(4):
                to_x = lax.rem(y + 8 - m_y - x, 4)
                b = lax.rem(token_z, 2)
                rows[to_x, b, 0] = first[m_z][m_y * 32 : m_y * 32 + 32, :]
                rows[to_x, b, 1] = second[m_y][m_z * 32 : m_z * 32 + 32, :]

    left = rows[...].reshape(512, rows.shape[-1])
    width = w_out.shape[1]
    for t in range(0, width, 256):
        n = min(256, width - t)
        part = jnp.dot(left, w_out[:, t : t + n], preferred_element_type=F32)
        out[:, t : t + n] = part.astype(BF16)


def mix(want, place, first, second, w_out):
    depth, width = w_out.shape
    return pl.pallas_call(
        functools.partial(mix_kernel, want),
        out_shape=jax.ShapeDtypeStruct((512, width), BF16),
        in_specs=[SMEM] + [VMEM] * 9,
        out_specs=VMEM,
        scratch_shapes=[pltpu.VMEM((4, 2, 2, 32, depth), BF16)],
        compiler_params=params(),
        name="mix",
    )(place, *first, *second, w_out)


def pair_add_kernel(mine, theirs, *outs):
    for k in range(4):
        rows = slice(k * 128, k * 128 + 128)
        outs[k][...] = (mine[rows, :].astype(F32) + theirs[rows, :].astype(F32)).astype(BF16)


def pair_add(mine, theirs):
    out = jax.ShapeDtypeStruct((128, mine.shape[1]), BF16)
    return pl.pallas_call(
        pair_add_kernel,
        out_shape=[out] * 4,
        in_specs=[VMEM] * 2,
        out_specs=[VMEM] * 4,
        compiler_params=params(),
        name="pair_add",
    )(mine, theirs)


def total(values):
    result = values[0].astype(F32)
    for value in values[1:]:
        result = result + value.astype(F32)
    return result.astype(BF16)


def per_device(tokens, norm_gain, w_query, w_keyvalue, w_out, cache_keys, cache_values, lengths):
    gx, gy = lax.axis_index("gx"), lax.axis_index("gy")
    place = jnp.stack([gx // 4, gx % 4, gy // 2, gy % 2]).astype(jnp.int32)

    arrived = [tokens] + [along_x(tokens, m) for m in range(1, 4)]
    pieces = []
    for piece in arrived:
        pieces += [piece, other_core(piece)]
    floated = tokens.astype(F32)
    sums = jnp.concatenate([jnp.sum(floated, axis=1), jnp.sum(floated * floated, axis=1)])
    stats = lax.all_to_all(
        jnp.broadcast_to(sums[None], (128, 256)), ("gx", "gy"), 0, 0, tiled=True
    )

    parts = project(place, stats, norm_gain[None], pieces, w_query, w_keyvalue)
    by_y = [parts[0]] + [along_y(parts[m], m) for m in range(1, 4)]
    by_z = [parts[4]] + [along_z(parts[4 + m], m) for m in range(1, 4)]
    parts = add_and_cut(by_y + by_z, 4)
    by_z = [parts[0]] + [along_z(parts[m], m) for m in range(1, 4)]
    by_y = [parts[4]] + [along_y(parts[4 + m], m) for m in range(1, 4)]
    query = jnp.concatenate([total(by_z), total(by_y)], axis=0)
    packed = lax.all_to_all(query, "gy", 0, 0, tiled=True)

    half_dim = HD // 2
    freqs = 10000.0 ** (-jnp.arange(half_dim, dtype=F32) / half_dim)
    positions = lengths[:, None] + jnp.arange(STEPS, dtype=jnp.int32)[None, :]
    angles = positions.reshape(-1).astype(F32)[:, None] * freqs
    attended = attend(packed, jnp.cos(angles), jnp.sin(angles), cache_keys, cache_values, lengths)

    returned = lax.all_to_all(attended, "gy", 0, 0, tiled=True)
    halves = [returned[:32], returned[32:]]
    first = jnp.concatenate([halves[0]] + [along_y(halves[0], m) for m in range(1, 4)], axis=0)
    second = jnp.concatenate([halves[1]] + [along_z(halves[1], m) for m in range(1, 4)], axis=0)
    first = [first] + [along_z(first, m) for m in range(1, 4)]
    second = [second] + [along_y(second, m) for m in range(1, 4)]

    theirs = other_core(mix(1, place, first, second, w_out))
    mine = mix(0, place, first, second, w_out)
    parts = pair_add(mine, theirs)
    return total([parts[0]] + [along_x(parts[m], m) for m in range(1, 4)])


def solution(mesh):
    return jax.shard_map(
        per_device,
        mesh=mesh,
        in_specs=(
            P("gy", "gx"),
            P("gx"),
            P("gx", "gy"),
            P("gx", "gy"),
            P("gy", "gx"),
            P(("gx", "gy"), None, None),
            P(("gx", "gy"), None, None),
            P(("gx", "gy")),
        ),
        out_specs=P("gy", "gx"),
        check_vma=False,
    )
```

```python
import functools

import jax
import jax.numpy as jnp
from jax import lax
from jax.experimental import pallas as pl
from jax.experimental.pallas import tpu as pltpu
from jax.sharding import PartitionSpec as P

D = 18432
HD = 256
STEPS = 2
VMEM = pl.BlockSpec(memory_space=pltpu.VMEM)
SMEM = pl.BlockSpec(memory_space=pltpu.SMEM)
ANY = pl.BlockSpec(memory_space=pl.ANY)
F32 = jnp.float32
BF16 = jnp.bfloat16


def params(mib):
    return pltpu.CompilerParams(vmem_limit_bytes=mib * 1024 * 1024)


def along_y(value, m):
    return lax.ppermute(value, "gx", [(g, g ^ (4 * m)) for g in range(16)])


def along_z(value, m):
    return lax.ppermute(value, "gx", [(g, g ^ m) for g in range(16)])


def along_x(value, m):
    return lax.ppermute(value, "gy", [(g, g ^ (2 * m)) for g in range(8)])


def other_core(value):
    return lax.ppermute(value, "gy", [(g, g ^ 1) for g in range(8)])


def load_tiles(source, tiles, sems):
    loads = []
    wide = tiles.shape[2]
    for t in range(tiles.shape[0]):
        load = pltpu.make_async_copy(source.at[:, pl.ds(t * wide, wide)], tiles.at[t], sems.at[t])
        load.start()
        loads.append(load)
    return loads


def multiply(left, w_pair, tiles, loads, outs):
    width = tiles.shape[0] * 256

    def put(part, at, size):
        for k, out in enumerate(outs):
            out[:, at : at + size] = part[k * 128 : k * 128 + 128]

    pair = jnp.dot(left, w_pair[...], preferred_element_type=F32).astype(BF16)
    put(pair, width, w_pair.shape[1])
    for t in range(tiles.shape[0]):
        loads[t].wait()
        put(jnp.dot(left, tiles[t], preferred_element_type=F32).astype(BF16), t * 256, 256)


def project_kernel(place, stats, gain, *refs):
    pieces, (w_query, w_pair), outs, rest = refs[:8], refs[8:10], refs[10:14], refs[14]
    normed, mean_of, scale_of, tiles, sems = refs[15:]
    loads = load_tiles(w_query, tiles, sems)
    y, z, x, c = place[0], place[1], place[2], place[3]
    total = stats[0:8, :]
    for g in range(1, 16):
        total = total + stats[g * 8 : g * 8 + 8, :]
    mean = total[:, :128] / D
    variance = total[:, 128:] / D - mean * mean
    mean_columns = mean.T
    scale_columns = lax.rsqrt(variance + 1e-05).T
    for s in range(8):
        mean_of[s] = mean_columns[:, s : s + 1]
        scale_of[s] = scale_columns[:, s : s + 1]
    gains = gain[...].astype(F32)
    for m in range(4):
        for j in range(2):
            source_c = c ^ j
            s = (x ^ m) * 2 + source_c
            rows = pieces[m * 2 + j][...].astype(F32)
            rows = ((rows - mean_of[s]) * scale_of[s] * gains).astype(BF16)
            to_y = x ^ m ^ y
            for b in range(2):
                to_z = (source_c * 2 + b) ^ z
                normed[0, to_y, to_z] = rows[b * 64 : b * 64 + 32]
                normed[1, to_z, to_y] = rows[b * 64 + 32 : b * 64 + 64]
    depth = normed.shape[-1]
    for h in range(2):
        for i, k in enumerate((0, 3)):
            at = (h * 2 + i) * 128
            rest[at : at + 128, :] = normed[h, k].reshape(128, depth)
    left = normed[:, 1:3].reshape(512, depth)
    multiply(left, w_pair, tiles, loads, outs)


def project(place, stats, gain, pieces, w_query, w_pair):
    depth, width = w_query.shape
    out = jax.ShapeDtypeStruct((128, width + w_pair.shape[1]), BF16)
    return pl.pallas_call(
        project_kernel,
        out_shape=[out] * 4 + [jax.ShapeDtypeStruct((512, depth), BF16)],
        in_specs=[SMEM] + [VMEM] * 10 + [ANY, VMEM],
        out_specs=[VMEM] * 5,
        scratch_shapes=[
            pltpu.VMEM((2, 4, 4, 32, depth), BF16),
            pltpu.VMEM((8, 128, 1), F32),
            pltpu.VMEM((8, 128, 1), F32),
            pltpu.VMEM((width // 256, depth, 256), BF16),
            pltpu.SemaphoreType.DMA((width // 256,)),
        ],
        compiler_params=params(28),
        name="project",
    )(place, stats, gain, *pieces, w_query, w_pair)


def project_rest_kernel(left, w_query, w_pair, *refs):
    outs, tiles, sems = refs[:4], refs[4], refs[5]
    multiply(left[...], w_pair, tiles, load_tiles(w_query, tiles, sems), outs)


def project_rest(left, w_query, w_pair):
    depth, width = w_query.shape
    out = jax.ShapeDtypeStruct((128, width + w_pair.shape[1]), BF16)
    return pl.pallas_call(
        project_rest_kernel,
        out_shape=[out] * 4,
        in_specs=[VMEM, ANY, VMEM],
        out_specs=[VMEM] * 4,
        scratch_shapes=[
            pltpu.VMEM((width // 256, depth, 256), BF16),
            pltpu.SemaphoreType.DMA((width // 256,)),
        ],
        compiler_params=params(20),
        name="project_rest",
    )(left, w_query, w_pair)


def add_kernel(pieces, *refs):
    groups = len(refs) // (2 * pieces)
    ins, outs = refs[: groups * pieces], refs[groups * pieces :]
    for g in range(groups):
        total = ins[g * pieces][...].astype(F32)
        for k in range(1, pieces):
            total = total + ins[g * pieces + k][...].astype(F32)
        total = total.astype(BF16)
        rows = total.shape[0] // pieces
        for k in range(pieces):
            outs[g * pieces + k][...] = total[k * rows : k * rows + rows]


def add_and_cut(values, pieces):
    rows, width = values[0].shape
    out = jax.ShapeDtypeStruct((rows // pieces, width), BF16)
    return pl.pallas_call(
        functools.partial(add_kernel, pieces),
        out_shape=[out] * len(values),
        in_specs=[VMEM] * len(values),
        out_specs=[VMEM] * len(values),
        compiler_params=params(16),
        name="add_and_cut",
    )(*values)


def finish_kernel(place, *refs):
    ins, (mine, theirs), blocks = refs[:8], refs[8:10], refs[10]
    x, c = place[2], place[3]
    for h in range(2):
        total = ins[h * 4][...].astype(F32)
        for k in range(1, 4):
            total = total + ins[h * 4 + k][...].astype(F32)
        for i in range(4):
            blocks[c ^ (i % 2), x ^ (h * 2 + i // 2)] = total[i * 8 : i * 8 + 8]
    width = blocks.shape[-1]
    mine[...] = blocks[0].reshape(32, width).astype(BF16)
    theirs[...] = blocks[1].reshape(32, width).astype(BF16)


def finish(place, values):
    shape = values[0].shape
    return pl.pallas_call(
        finish_kernel,
        out_shape=[jax.ShapeDtypeStruct(shape, BF16)] * 2,
        in_specs=[SMEM] + [VMEM] * 8,
        out_specs=[VMEM] * 2,
        scratch_shapes=[pltpu.VMEM((2, 4, 8, shape[1]), F32)],
        compiler_params=params(8),
        name="finish",
    )(place, *values)


def pair_kernel(by_core, place, mine, theirs, *outs):
    first, second = mine[...].astype(F32), theirs[...].astype(F32)
    if by_core:
        swap = place[3] == 1
        first, second = jnp.where(swap, second, first), jnp.where(swap, first, second)
    for m, out in enumerate(outs):
        rows = slice(m * 8, m * 8 + 8)
        out[...] = jnp.concatenate([first[rows], second[rows]], axis=0).astype(BF16)


def pair(by_core, place, mine, theirs):
    out = jax.ShapeDtypeStruct((16, mine.shape[1]), BF16)
    return pl.pallas_call(
        functools.partial(pair_kernel, by_core),
        out_shape=[out] * 4,
        in_specs=[SMEM] + [VMEM] * 2,
        out_specs=[VMEM] * 4,
        compiler_params=params(8),
        name="pair",
    )(place, mine, theirs)


def attend_kernel(lengths, place, *refs):
    packed, (cosine, sine, keys, values, mine, theirs) = refs[:4], refs[4:10]
    query_rows, new_pieces, new_kv, result = refs[10:]
    request = pl.program_id(0)
    heads = mine.shape[1] // HD
    count = 8 * heads

    @pl.when(request == 0)
    def _():
        x, c = place[2], place[3]
        cos, sin = cosine[...], sine[...]

        def rotated(first, second):
            return first * cos - second * sin, second * cos + first * sin

        for m in range(4):
            rows = packed[m][...].astype(F32)
            for j in range(2):
                block = rows[j * 8 : j * 8 + 8]
                for h in range(heads):
                    head = block[:, h * HD : h * HD + HD]
                    at = (m * 2 + j) * heads + h
                    for i, half in enumerate(rotated(head[:, :128], head[:, 128:])):
                        query_rows[i, pl.ds(at, 8, stride=count), :] = half
                new_pieces[(x ^ m) * 2 + (c ^ j)] = block[:, heads * HD :]
        halves = [
            jnp.concatenate([new_pieces[i], new_pieces[i + 1]], axis=-1) for i in range(0, 8, 2)
        ]
        new_kv[0] = jnp.concatenate(rotated(halves[0], halves[1]), axis=-1).astype(BF16)
        new_kv[1] = jnp.concatenate(halves[2:], axis=-1).astype(BF16)

    per = STEPS * count
    start = pl.multiple_of(request * per, per)
    query = jnp.concatenate([query_rows[i, pl.ds(start, per), :] for i in range(2)], axis=-1)
    query = (query.astype(BF16).astype(F32) * HD ** (-0.5)).astype(BF16)
    dims = (((1,), (1,)), ((), ()))
    cached = lax.dot_general(query, keys[0], dims, preferred_element_type=F32)
    slots = lax.broadcasted_iota(jnp.int32, cached.shape, 1)
    cached = jnp.where(slots < lengths[request], cached, -jnp.inf)
    fresh = lax.dot_general(query, new_kv[0], dims, preferred_element_type=F32)
    row_step = lax.broadcasted_iota(jnp.int32, fresh.shape, 0) // count
    key_step = lax.broadcasted_iota(jnp.int32, fresh.shape, 1) - request * STEPS
    fresh = jnp.where((key_step >= 0) & (key_step <= row_step), fresh, -jnp.inf)
    top = jnp.maximum(
        jnp.max(cached, axis=-1, keepdims=True), jnp.max(fresh, axis=-1, keepdims=True)
    )
    cached = jnp.exp(cached - top)
    fresh = jnp.exp(fresh - top)
    denom = jnp.sum(cached, axis=-1, keepdims=True) + jnp.sum(fresh, axis=-1, keepdims=True)
    mixed = jnp.dot(cached.astype(BF16), values[0], preferred_element_type=F32)
    mixed = mixed + jnp.dot(fresh.astype(BF16), new_kv[1], preferred_element_type=F32)
    mixed = mixed / denom
    for i in range(2):
        result[i, pl.ds(start, per), :] = mixed[:, i * 128 : i * 128 + 128]

    @pl.when(request == pl.num_programs(0) - 1)
    def _():
        for j, out in enumerate((mine, theirs)):
            lines = []
            for m in range(4):
                at = (m * 2 + j) * heads
                halves = [
                    result[i, pl.ds(at + h, 8, stride=count), :]
                    for h in range(heads)
                    for i in range(2)
                ]
                lines.append(jnp.concatenate(halves, axis=-1))
            out[...] = jnp.concatenate(lines, axis=0).astype(BF16)


def attend(place, packed, cosine, sine, cache_keys, cache_values, lengths):
    requests, slots, _ = cache_keys.shape
    total = packed[0].shape[1]
    width = total // HD * HD
    count = 8 * (width // HD)
    whole = lambda *shape: pl.BlockSpec(shape, lambda r, *_: (0,) * len(shape))
    cache = pl.BlockSpec((1, slots, HD), lambda r, *_: (r, 0, 0))
    return pl.pallas_call(
        attend_kernel,
        out_shape=[jax.ShapeDtypeStruct((32, width), BF16)] * 2,
        grid_spec=pltpu.PrefetchScalarGridSpec(
            num_scalar_prefetch=2,
            grid=(requests,),
            in_specs=[whole(16, total)] * 4 + [whole(8, 128)] * 2 + [cache] * 2,
            out_specs=[whole(32, width)] * 2,
            scratch_shapes=[
                pltpu.VMEM((2, 8 * count, 128), F32),
                pltpu.VMEM((8, 8, total - width), F32),
                pltpu.VMEM((2, 8, HD), BF16),
                pltpu.VMEM((2, 8 * count, 128), F32),
            ],
        ),
        compiler_params=params(20),
        name="attend",
    )(lengths, place, *packed, cosine, sine, cache_keys, cache_values)


def mix_kernel(place, *refs):
    first, second, (w_out, mine, theirs) = refs[:2], refs[2:6], refs[6:9]
    rows, tiles, sems = refs[9:]
    loads = load_tiles(w_out, tiles, sems)
    y, z, x, c = place[0], place[1], place[2], place[3]
    for i in range(2):
        core = z // 2 ^ i ^ c
        for m_y in range(4):
            to_x = y ^ m_y ^ x
            for k in range(2):
                at = m_y * 32 + k * 16
                rows[core, to_x, x ^ k] = first[i][at : at + 16, :]
                at = i * 32 + k * 16
                rows[core, to_x, x ^ (k + 2)] = second[m_y][at : at + 16, :]
    left = rows[...].reshape(512, rows.shape[-1])
    for t, load in enumerate(loads):
        load.wait()
        part = jnp.dot(left, tiles[t], preferred_element_type=F32).astype(BF16)
        wide = tiles.shape[2]
        mine[:, t * wide : t * wide + wide] = part[:256]
        theirs[:, t * wide : t * wide + wide] = part[256:]


def mix(place, first, second, w_out):
    depth, width = w_out.shape
    return pl.pallas_call(
        mix_kernel,
        out_shape=[jax.ShapeDtypeStruct((256, width), BF16)] * 2,
        in_specs=[SMEM] + [VMEM] * 6 + [ANY],
        out_specs=[VMEM] * 2,
        scratch_shapes=[
            pltpu.VMEM((2, 4, 4, 16, depth), BF16),
            pltpu.VMEM((3, depth, width // 3), BF16),
            pltpu.SemaphoreType.DMA((3,)),
        ],
        compiler_params=params(20),
        name="mix",
    )(place, *first, *second, w_out)


def pair_add_kernel(mine, theirs, *outs):
    for k in range(4):
        rows = slice(k * 64, k * 64 + 64)
        outs[k][...] = (mine[rows, :].astype(F32) + theirs[rows, :].astype(F32)).astype(BF16)


def pair_add(mine, theirs):
    out = jax.ShapeDtypeStruct((64, mine.shape[1]), BF16)
    return pl.pallas_call(
        pair_add_kernel,
        out_shape=[out] * 4,
        in_specs=[VMEM] * 2,
        out_specs=[VMEM] * 4,
        compiler_params=params(8),
        name="pair_add",
    )(mine, theirs)


def sum_of(values):
    result = values[0].astype(F32)
    for value in values[1:]:
        result = result + value.astype(F32)
    return result.astype(BF16)


def exchanged(along, parts):
    return [parts[0]] + [along(parts[m], m) for m in range(1, 4)]


def per_device(tokens, norm_gain, w_query, w_keyvalue, w_out, cache_keys, cache_values, lengths):
    gx, gy = lax.axis_index("gx"), lax.axis_index("gy")
    place = jnp.stack([gx // 4, gx % 4, gy // 2, gy % 2]).astype(jnp.int32)

    floated = tokens.astype(F32)
    sums = jnp.concatenate([jnp.sum(floated, axis=1), jnp.sum(floated * floated, axis=1)])
    stats = jnp.broadcast_to(sums[None], (128, 256))
    tokens, stats = lax.optimization_barrier((tokens, stats))
    arrived = exchanged(along_x, [tokens] * 4)
    stats = lax.all_to_all(stats, ("gx", "gy"), 0, 0, tiled=True)
    arrived[1:], stats = lax.optimization_barrier((arrived[1:], stats))
    pieces = []
    for piece in arrived:
        pieces += [piece, other_core(piece)]

    *sent, rest = project(place, stats, norm_gain[None], pieces, w_query, w_keyvalue)
    kept = project_rest(rest, w_query, w_keyvalue)
    by_y = exchanged(along_y, [kept[0], sent[0], sent[1], kept[1]])
    by_z = exchanged(along_z, [kept[2], sent[2], sent[3], kept[3]])
    parts = add_and_cut(by_y + by_z, 4)
    parts = exchanged(along_z, parts[:4]) + exchanged(along_y, parts[4:])
    mine, theirs = finish(place, parts)
    packed = exchanged(along_x, pair(False, place, mine, other_core(theirs)))

    half_dim = HD // 2
    freqs = 10000.0 ** (-jnp.arange(half_dim, dtype=F32) / half_dim)
    positions = lengths[:, None] + jnp.arange(STEPS, dtype=jnp.int32)[None, :]
    angles = positions.reshape(-1).astype(F32)[:, None] * freqs
    mine, theirs = attend(
        place, packed, jnp.cos(angles), jnp.sin(angles), cache_keys, cache_values, lengths
    )

    returned = exchanged(along_x, pair(True, place, mine, other_core(theirs)))
    first = jnp.concatenate(returned[:2], axis=0)
    second = jnp.concatenate(returned[2:], axis=0)
    first = jnp.concatenate(exchanged(along_y, [first] * 4), axis=0)
    second = exchanged(along_z, [second] * 4)

    halves = []
    for k in range(2):
        left = [first if k == 0 else along_z(first, 1), along_z(first, 2 + k)]
        right = jnp.concatenate([second[k], second[k + 2]], axis=0)
        mine, theirs = mix(place, left, exchanged(along_y, [right] * 4), w_out)
        halves.append(sum_of(exchanged(along_x, pair_add(mine, other_core(theirs)))))
    odd = place[1] % 2 == 1
    return jnp.concatenate(
        [jnp.where(odd, halves[1], halves[0]), jnp.where(odd, halves[0], halves[1])], axis=0
    )


def solution(mesh):
    return jax.shard_map(
        per_device,
        mesh=mesh,
        in_specs=(
            P("gy", "gx"),
            P("gx"),
            P("gx", "gy"),
            P("gx", "gy"),
            P("gy", "gx"),
            P(("gx", "gy"), None, None),
            P(("gx", "gy"), None, None),
            P(("gx", "gy")),
        ),
        out_specs=P("gy", "gx"),
        check_vma=False,
    )
```

```python
import functools

import jax
import jax.numpy as jnp
from jax import lax
from jax.experimental import pallas as pl
from jax.experimental.pallas import tpu as pltpu
from jax.sharding import PartitionSpec as P

D = 18432
HD = 256
STEPS = 2
VMEM = pl.BlockSpec(memory_space=pltpu.VMEM)
SMEM = pl.BlockSpec(memory_space=pltpu.SMEM)
HBM = pl.BlockSpec(memory_space=pltpu.HBM)
F32 = jnp.float32
BF16 = jnp.bfloat16


def params(mib):
    return pltpu.CompilerParams(vmem_limit_bytes=mib * 1024 * 1024)


def cost(flops, size):
    return pl.CostEstimate(flops=int(flops), bytes_accessed=int(size), transcendentals=0)


def along_y(value, m):
    return lax.ppermute(value, "gx", [(g, g ^ (4 * m)) for g in range(16)])


def along_z(value, m):
    return lax.ppermute(value, "gx", [(g, g ^ m) for g in range(16)])


def along_x(value, m):
    return lax.ppermute(value, "gy", [(g, g ^ (2 * m)) for g in range(8)])


def other_core(value):
    return lax.ppermute(value, "gy", [(g, g ^ 1) for g in range(8)])


def load_tiles(source, tiles, sems):
    loads = []
    wide = tiles.shape[2]
    for t in range(tiles.shape[0]):
        load = pltpu.make_async_copy(source.at[:, pl.ds(t * wide, wide)], tiles.at[t], sems.at[t])
        load.start()
        loads.append(load)
    return loads


def multiply(left, w_pair, tiles, loads, outs):
    wide = tiles.shape[2]
    width = tiles.shape[0] * wide

    def put(part, at, size):
        for k, out in enumerate(outs):
            out[:, at : at + size] = part[k * 128 : k * 128 + 128]

    dims = (((1,), (1,)), ((), ()))
    pair = lax.dot_general(left, w_pair[...], dims, preferred_element_type=F32).astype(BF16)
    put(pair, width, w_pair.shape[0])
    for t in range(tiles.shape[0]):
        loads[t].wait()
        put(jnp.dot(left, tiles[t], preferred_element_type=F32).astype(BF16), t * wide, wide)


def project_kernel(place, stats, gain, *refs):
    pieces, (w_query, w_pair), outs, rest = list(refs[:8]), refs[8:10], refs[10:14], refs[14]
    normed, own, mean_of, scale_of, tiles, sems, own_sem = refs[15:]
    own_load = pltpu.make_async_copy(pieces[0], own, own_sem)
    own_load.start()
    pieces[0] = own
    loads = load_tiles(w_query, tiles, sems)
    y, z, x, c = place[0], place[1], place[2], place[3]
    total = stats[0:8, :]
    for g in range(1, 16):
        total = total + stats[g * 8 : g * 8 + 8, :]
    mean = total[:, :128] / D
    variance = total[:, 128:] / D - mean * mean
    mean_columns = mean.T
    scale_columns = lax.rsqrt(variance + 1e-05).T
    for s in range(8):
        mean_of[s] = mean_columns[:, s : s + 1]
        scale_of[s] = scale_columns[:, s : s + 1]
    gains = gain[...].astype(F32)
    own_load.wait()
    for m in range(4):
        for j in range(2):
            source_c = c ^ j
            s = (x ^ m) * 2 + source_c
            rows = pieces[m * 2 + j][...].astype(F32)
            rows = ((rows - mean_of[s]) * scale_of[s] * gains).astype(BF16)
            to_y = x ^ m ^ y
            for b in range(2):
                to_z = (source_c * 2 + b) ^ z
                normed[0, to_y, to_z] = rows[b * 64 : b * 64 + 32]
                normed[1, to_z, to_y] = rows[b * 64 + 32 : b * 64 + 64]
    depth = normed.shape[-1]
    for h in range(2):
        for i, k in enumerate((0, 3)):
            at = (h * 2 + i) * 128
            rest[at : at + 128, :] = normed[h, k].reshape(128, depth)
    left = normed[:, 1:3].reshape(512, depth)
    multiply(left, w_pair, tiles, loads, outs)


def project(place, stats, gain, pieces, w_query, w_pair):
    depth, width = w_query.shape
    out = jax.ShapeDtypeStruct((128, width + w_pair.shape[0]), BF16)
    return pl.pallas_call(
        project_kernel,
        out_shape=[out] * 4 + [jax.ShapeDtypeStruct((512, depth), BF16)],
        in_specs=[SMEM] + [VMEM] * 2 + [HBM] + [VMEM] * 7 + [HBM, VMEM],
        out_specs=[VMEM] * 5,
        scratch_shapes=[
            pltpu.VMEM((2, 4, 4, 32, depth), BF16),
            pltpu.VMEM((128, depth), BF16),
            pltpu.VMEM((8, 128, 1), F32),
            pltpu.VMEM((8, 128, 1), F32),
            pltpu.VMEM((width // 512, depth, 512), BF16),
            pltpu.SemaphoreType.DMA((width // 512,)),
            pltpu.SemaphoreType.DMA,
        ],
        compiler_params=params(50),
        cost_estimate=cost(6e9, 1.2e7),
        name="project",
    )(place, stats, gain, *pieces, w_query, w_pair)


def project_rest_kernel(left, w_query, w_pair, *refs):
    outs, tiles, sems = refs[:4], refs[4], refs[5]
    multiply(left[...], w_pair, tiles, load_tiles(w_query, tiles, sems), outs)


def project_rest(left, w_query, w_pair):
    depth, width = w_query.shape
    out = jax.ShapeDtypeStruct((128, width + w_pair.shape[0]), BF16)
    return pl.pallas_call(
        project_rest_kernel,
        out_shape=[out] * 4,
        in_specs=[VMEM, HBM, VMEM],
        out_specs=[VMEM] * 4,
        scratch_shapes=[
            pltpu.VMEM((width // 512, depth, 512), BF16),
            pltpu.SemaphoreType.DMA((width // 512,)),
        ],
        compiler_params=params(50),
        cost_estimate=cost(6e9, 9e6),
        name="project_rest",
    )(left, w_query, w_pair)


def add_kernel(*refs):
    for g in range(2):
        first, second, third = refs[g * 3 : g * 3 + 3]
        total = first[...].astype(F32) + second[...].astype(F32)
        refs[6 + g][...] = total + third[...].astype(F32)


def add_three(values):
    out = jax.ShapeDtypeStruct(values[0].shape, F32)
    return pl.pallas_call(
        add_kernel,
        out_shape=[out] * 2,
        in_specs=[VMEM] * 6,
        out_specs=[VMEM] * 2,
        compiler_params=params(16),
        cost_estimate=cost(1e9, 4e6),
        name="add_three",
    )(*values)


def add_and_cut_kernel(*refs):
    for g in range(2):
        total = (refs[g][...] + refs[2 + g][...].astype(F32)).astype(BF16)
        rows = total.shape[0] // 4
        for k in range(4):
            refs[4 + g * 4 + k][...] = total[k * rows : k * rows + rows]


def add_and_cut(values):
    rows, width = values[0].shape
    out = jax.ShapeDtypeStruct((rows // 4, width), BF16)
    return pl.pallas_call(
        add_and_cut_kernel,
        out_shape=[out] * 8,
        in_specs=[VMEM] * 4,
        out_specs=[VMEM] * 8,
        compiler_params=params(16),
        cost_estimate=cost(1e8, 3e6),
        name="add_and_cut",
    )(*values)


def finish_kernel(place, *refs):
    ins, (mine, theirs), blocks = refs[:8], refs[8:10], refs[10]
    x, c = place[2], place[3]
    for h in range(2):
        total = ins[h * 4][...].astype(F32)
        for k in range(1, 4):
            total = total + ins[h * 4 + k][...].astype(F32)
        for i in range(4):
            blocks[c ^ (i % 2), x ^ (h * 2 + i // 2)] = total[i * 8 : i * 8 + 8]
    width = blocks.shape[-1]
    mine[...] = blocks[0].reshape(32, width).astype(BF16)
    theirs[...] = blocks[1].reshape(32, width).astype(BF16)


def finish(place, values):
    shape = values[0].shape
    return pl.pallas_call(
        finish_kernel,
        out_shape=[jax.ShapeDtypeStruct(shape, BF16)] * 2,
        in_specs=[SMEM] + [VMEM] * 8,
        out_specs=[VMEM] * 2,
        scratch_shapes=[pltpu.VMEM((2, 4, 8, shape[1]), F32)],
        compiler_params=params(8),
        cost_estimate=cost(1e8, 1e6),
        name="finish",
    )(place, *values)


def pair_kernel(by_core, place, mine, theirs, *outs):
    first, second = mine[...].astype(F32), theirs[...].astype(F32)
    if by_core:
        swap = place[3] == 1
        first, second = jnp.where(swap, second, first), jnp.where(swap, first, second)
    for m, out in enumerate(outs):
        rows = slice(m * 8, m * 8 + 8)
        out[...] = jnp.concatenate([first[rows], second[rows]], axis=0).astype(BF16)


def pair(by_core, place, mine, theirs):
    out = jax.ShapeDtypeStruct((16, mine.shape[1]), BF16)
    return pl.pallas_call(
        functools.partial(pair_kernel, by_core),
        out_shape=[out] * 4,
        in_specs=[SMEM] + [VMEM] * 2,
        out_specs=[VMEM] * 4,
        compiler_params=params(8),
        cost_estimate=cost(1e8, 4e5),
        name="pair",
    )(place, mine, theirs)


def attend_kernel(lengths, place, *refs):
    packed, (cosine, sine, keys, values, mine, theirs) = refs[:4], refs[4:10]
    query_rows, new_pieces, new_kv, result = refs[10:]
    request = pl.program_id(0)
    heads = mine.shape[1] // HD
    count = 8 * heads

    @pl.when(request == 0)
    def _():
        x, c = place[2], place[3]
        cos, sin = cosine[...], sine[...]

        def rotated(first, second):
            return first * cos - second * sin, second * cos + first * sin

        for m in range(4):
            rows = packed[m][...].astype(F32)
            for j in range(2):
                block = rows[j * 8 : j * 8 + 8]
                for h in range(heads):
                    head = block[:, h * HD : h * HD + HD]
                    at = (m * 2 + j) * heads + h
                    for i, half in enumerate(rotated(head[:, :128], head[:, 128:])):
                        query_rows[i, pl.ds(at, 8, stride=count), :] = half
                new_pieces[(x ^ m) * 2 + (c ^ j)] = block[:, heads * HD :]
        halves = [
            jnp.concatenate([new_pieces[i], new_pieces[i + 1]], axis=-1) for i in range(0, 8, 2)
        ]
        new_kv[0] = jnp.concatenate(rotated(halves[0], halves[1]), axis=-1).astype(BF16)
        new_kv[1] = jnp.concatenate(halves[2:], axis=-1).astype(BF16)

    per = STEPS * count
    start = pl.multiple_of(request * per, per)
    query = jnp.concatenate([query_rows[i, pl.ds(start, per), :] for i in range(2)], axis=-1)
    query = (query.astype(BF16).astype(F32) * HD ** (-0.5)).astype(BF16)
    dims = (((1,), (1,)), ((), ()))
    cached = lax.dot_general(query, keys[0], dims, preferred_element_type=F32)
    slots = lax.broadcasted_iota(jnp.int32, cached.shape, 1)
    cached = jnp.where(slots < lengths[request], cached, -jnp.inf)
    fresh = lax.dot_general(query, new_kv[0], dims, preferred_element_type=F32)
    row_step = lax.broadcasted_iota(jnp.int32, fresh.shape, 0) // count
    key_step = lax.broadcasted_iota(jnp.int32, fresh.shape, 1) - request * STEPS
    fresh = jnp.where((key_step >= 0) & (key_step <= row_step), fresh, -jnp.inf)
    top = jnp.maximum(
        jnp.max(cached, axis=-1, keepdims=True), jnp.max(fresh, axis=-1, keepdims=True)
    )
    cached = jnp.exp(cached - top)
    fresh = jnp.exp(fresh - top)
    denom = jnp.sum(cached, axis=-1, keepdims=True) + jnp.sum(fresh, axis=-1, keepdims=True)
    mixed = jnp.dot(cached.astype(BF16), values[0], preferred_element_type=F32)
    mixed = mixed + jnp.dot(fresh.astype(BF16), new_kv[1], preferred_element_type=F32)
    mixed = mixed / denom
    for i in range(2):
        result[i, pl.ds(start, per), :] = mixed[:, i * 128 : i * 128 + 128]

    @pl.when(request == pl.num_programs(0) - 1)
    def _():
        for j, out in enumerate((mine, theirs)):
            lines = []
            for m in range(4):
                at = (m * 2 + j) * heads
                halves = [
                    result[i, pl.ds(at + h, 8, stride=count), :]
                    for h in range(heads)
                    for i in range(2)
                ]
                lines.append(jnp.concatenate(halves, axis=-1))
            out[...] = jnp.concatenate(lines, axis=0).astype(BF16)


def attend(place, packed, cosine, sine, cache_keys, cache_values, lengths):
    requests, slots, _ = cache_keys.shape
    total = packed[0].shape[1]
    width = total // HD * HD
    count = 8 * (width // HD)
    whole = lambda *shape: pl.BlockSpec(shape, lambda r, *_: (0,) * len(shape))
    cache = pl.BlockSpec((1, slots, HD), lambda r, *_: (r, 0, 0))
    return pl.pallas_call(
        attend_kernel,
        out_shape=[jax.ShapeDtypeStruct((32, width), BF16)] * 2,
        grid_spec=pltpu.PrefetchScalarGridSpec(
            num_scalar_prefetch=2,
            grid=(requests,),
            in_specs=[whole(16, total)] * 4 + [whole(8, 128)] * 2 + [cache] * 2,
            out_specs=[whole(32, width)] * 2,
            scratch_shapes=[
                pltpu.VMEM((2, 8 * count, 128), F32),
                pltpu.VMEM((8, 8, total - width), F32),
                pltpu.VMEM((2, 8, HD), BF16),
                pltpu.VMEM((2, 8 * count, 128), F32),
            ],
        ),
        compiler_params=params(52),
        cost_estimate=cost(6e9, 1.8e7),
        name="attend",
    )(lengths, place, *packed, cosine, sine, cache_keys, cache_values)


def mix_kernel(place, *refs):
    first, second, (w_out, mine, theirs) = refs[:2], refs[2:6], refs[6:9]
    rows, tiles, sems = refs[9:]
    loads = load_tiles(w_out, tiles, sems)
    y, z, x, c = place[0], place[1], place[2], place[3]
    for i in range(2):
        core = z // 2 ^ i ^ c
        for m_y in range(4):
            to_x = y ^ m_y ^ x
            for k in range(2):
                at = m_y * 32 + k * 16
                rows[core, to_x, x ^ k] = first[i][at : at + 16, :]
                at = i * 32 + k * 16
                rows[core, to_x, x ^ (k + 2)] = second[m_y][at : at + 16, :]
    left = rows[...].reshape(512, rows.shape[-1])
    for t, load in enumerate(loads):
        load.wait()
        part = jnp.dot(left, tiles[t], preferred_element_type=F32).astype(BF16)
        wide = tiles.shape[2]
        mine[:, t * wide : t * wide + wide] = part[:256]
        theirs[:, t * wide : t * wide + wide] = part[256:]


def mix(place, first, second, w_out):
    depth, width = w_out.shape
    return pl.pallas_call(
        mix_kernel,
        out_shape=[jax.ShapeDtypeStruct((256, width), BF16)] * 2,
        in_specs=[SMEM] + [VMEM] * 6 + [HBM],
        out_specs=[VMEM] * 2,
        scratch_shapes=[
            pltpu.VMEM((2, 4, 4, 16, depth), BF16),
            pltpu.VMEM((3, depth, width // 3), BF16),
            pltpu.SemaphoreType.DMA((3,)),
        ],
        compiler_params=params(20),
        cost_estimate=cost(4e9, 8e6),
        name="mix",
    )(place, *first, *second, w_out)


def pair_add_kernel(mine, theirs, *outs):
    for k in range(4):
        rows = slice(k * 64, k * 64 + 64)
        outs[k][...] = (mine[rows, :].astype(F32) + theirs[rows, :].astype(F32)).astype(BF16)


def pair_add(mine, theirs):
    out = jax.ShapeDtypeStruct((64, mine.shape[1]), BF16)
    return pl.pallas_call(
        pair_add_kernel,
        out_shape=[out] * 4,
        in_specs=[VMEM] * 2,
        out_specs=[VMEM] * 4,
        compiler_params=params(8),
        cost_estimate=cost(1e8, 1e6),
        name="pair_add",
    )(mine, theirs)


def sum_of(values):
    result = values[0].astype(F32)
    for value in values[1:]:
        result = result + value.astype(F32)
    return result.astype(BF16)


def exchanged(along, parts):
    return [parts[0]] + [along(parts[m], m) for m in range(1, 4)]


def per_device(tokens, norm_gain, w_query, w_keyvalue, w_out, cache_keys, cache_values, lengths):
    gx, gy = lax.axis_index("gx"), lax.axis_index("gy")
    place = jnp.stack([gx // 4, gx % 4, gy // 2, gy % 2]).astype(jnp.int32)

    floated = tokens.astype(F32)
    sums = jnp.concatenate([jnp.sum(floated, axis=1), jnp.sum(floated * floated, axis=1)])
    stats = jnp.broadcast_to(sums[None], (128, 256))
    tokens, stats = lax.optimization_barrier((tokens, stats))
    arrived = exchanged(along_x, [tokens] * 4)
    stats = lax.all_to_all(stats, ("gx", "gy"), 0, 0, tiled=True)
    arrived[1:], stats = lax.optimization_barrier((arrived[1:], stats))
    pieces = []
    for piece in arrived:
        pieces += [piece, other_core(piece)]

    w_pair = w_keyvalue.T
    *sent, rest = project(place, stats, norm_gain[None], pieces, w_query, w_pair)
    kept = project_rest(rest, w_query, w_pair)
    by_y = exchanged(along_y, [kept[0], sent[0], sent[1], kept[1]])
    by_z = exchanged(along_z, [kept[2], sent[2], sent[3], kept[3]])
    parts = add_and_cut([*add_three(by_y[:3] + by_z[:3]), by_y[3], by_z[3]])
    parts = exchanged(along_z, parts[:4]) + exchanged(along_y, parts[4:])
    mine, theirs = finish(place, parts)
    packed = exchanged(along_x, pair(False, place, mine, other_core(theirs)))

    half_dim = HD // 2
    freqs = 10000.0 ** (-jnp.arange(half_dim, dtype=F32) / half_dim)
    positions = lengths[:, None] + jnp.arange(STEPS, dtype=jnp.int32)[None, :]
    angles = positions.reshape(-1).astype(F32)[:, None] * freqs
    mine, theirs = attend(
        place, packed, jnp.cos(angles), jnp.sin(angles), cache_keys, cache_values, lengths
    )

    returned = exchanged(along_x, pair(True, place, mine, other_core(theirs)))
    first = jnp.concatenate(returned[:2], axis=0)
    second = jnp.concatenate(returned[2:], axis=0)
    first, second = exchanged(along_y, [first] * 4), exchanged(along_z, [second] * 4)
    first, second = lax.optimization_barrier((first, second))
    first = jnp.concatenate(first, axis=0)

    lefts = [first, along_z(first, 2)], [along_z(first, 1), along_z(first, 3)]
    rights = [
        exchanged(along_y, [jnp.concatenate([second[k], second[k + 2]], axis=0)] * 4)
        for k in range(2)
    ]
    lefts[0][1], lefts[1][0] = lax.optimization_barrier((lefts[0][1], lefts[1][0]))
    mine, theirs = mix(place, lefts[0], rights[0], w_out)
    theirs = other_core(theirs)
    mine, rights[1][1:], lefts[1][1] = lax.optimization_barrier(
        (mine, rights[1][1:], lefts[1][1])
    )
    half = sum_of(exchanged(along_x, pair_add(mine, theirs)))
    mine, theirs = mix(place, lefts[1], rights[1], w_out)
    theirs = other_core(theirs)
    mine, half = lax.optimization_barrier((mine, half))
    halves = [half, sum_of(exchanged(along_x, pair_add(mine, theirs)))]
    odd = place[1] % 2 == 1
    return jnp.concatenate(
        [jnp.where(odd, halves[1], halves[0]), jnp.where(odd, halves[0], halves[1])], axis=0
    )


def solution(mesh):
    return jax.shard_map(
        per_device,
        mesh=mesh,
        in_specs=(
            P("gy", "gx"),
            P("gx"),
            P("gx", "gy"),
            P("gx", "gy"),
            P("gy", "gx"),
            P(("gx", "gy"), None, None),
            P(("gx", "gy"), None, None),
            P(("gx", "gy")),
        ),
        out_specs=P("gy", "gx"),
        check_vma=False,
    )
```

```python
import jax
import jax.numpy as jnp
from jax import lax
from jax.experimental import pallas as pl
from jax.experimental.pallas import tpu as pltpu
from jax.sharding import PartitionSpec as P

D = 18432
HD = 256
STEPS = 2
VMEM = pl.BlockSpec(memory_space=pltpu.VMEM)
SMEM = pl.BlockSpec(memory_space=pltpu.SMEM)
ANY = pl.BlockSpec(memory_space=pl.ANY)
F32 = jnp.float32
BF16 = jnp.bfloat16


def params(mib):
    return pltpu.CompilerParams(vmem_limit_bytes=mib * 1024 * 1024)


def cost(flops, size):
    return pl.CostEstimate(flops=int(flops), bytes_accessed=int(size), transcendentals=0)


def exchange_pairs(core_along_y, m):
    pairs = []
    for d in range(128):
        far = 32 * m if d % 2 == core_along_y else 8 * m
        pairs.append((d, d ^ far))
    return pairs


def along_first(value, m):
    return lax.ppermute(value, ("gx", "gy"), exchange_pairs(0, m))


def along_second(value, m):
    return lax.ppermute(value, ("gx", "gy"), exchange_pairs(1, m))


def along_x(value, m):
    return lax.ppermute(value, "gy", [(g, g ^ (2 * m)) for g in range(8)])


def other_core(value):
    return lax.ppermute(value, "gy", [(g, g ^ 1) for g in range(8)])


def exchanged(along, parts):
    return [parts[0]] + [along(parts[m], m) for m in range(1, 4)]


def groups_of(rows, first, count):
    return jnp.concatenate([rows[16 * i + first : 16 * i + first + 8] for i in range(count)], axis=0)


def prepare_kernel(place, tokens, stats, mine, theirs):
    rows = tokens[...].astype(F32)
    by_core = [groups_of(rows, 0, 8), groups_of(rows, 8, 8)]
    swap = place[3] == 1
    mine[...] = jnp.where(swap, by_core[1], by_core[0]).astype(BF16)
    theirs[...] = jnp.where(swap, by_core[0], by_core[1]).astype(BF16)
    lines = []
    for power in range(2):
        sums = [
            jnp.sum(part if power == 0 else part * part, axis=1, keepdims=True) for part in by_core
        ]
        column = jnp.broadcast_to(jnp.concatenate(sums, axis=0), (128, 128))
        lines.append(column.T[0:1])
    line = jnp.concatenate(lines, axis=1)
    stats[...] = jnp.broadcast_to(line[:, None, :], stats.shape)


def prepare(place, tokens):
    half = jax.ShapeDtypeStruct((64, tokens.shape[1]), BF16)
    return pl.pallas_call(
        prepare_kernel,
        out_shape=[jax.ShapeDtypeStruct((128, 1, 256), F32), half, half],
        in_specs=[SMEM, VMEM],
        out_specs=[VMEM] * 3,
        compiler_params=params(8),
        cost_estimate=cost(1e8, 1e6),
        name="prepare",
    )(place, tokens)


def load_tiles(source, tiles, sems, at):
    loads = []
    wide = tiles.shape[2]
    for t in range(source.shape[1] // wide):
        load = pltpu.make_async_copy(
            source.at[:, pl.ds(t * wide, wide)], tiles.at[at + t], sems.at[at + t]
        )
        load.start()
        loads.append(load)
    return loads


def project_kernel(place, stats, gain, *refs):
    pieces, weights, pairs, outs = refs[:4], refs[4:6], refs[6:8], refs[8:12]
    normed, mean_of, scale_of, tiles, sems = refs[12:]
    count = tiles.shape[0] // 2
    loads = load_tiles(weights[0], tiles, sems, 0) + load_tiles(weights[1], tiles, sems, count)
    y, z, x, c = place[0], place[1], place[2], place[3]
    total = stats[0:8, :]
    for g in range(1, 16):
        total = total + stats[g * 8 : g * 8 + 8, :]
    mean = total[:, :128] / D
    variance = total[:, 128:] / D - mean * mean
    mean_columns = mean.T
    scale_columns = lax.rsqrt(variance + 1e-05).T
    for s in range(8):
        mean_of[s] = mean_columns[:, s : s + 1]
        scale_of[s] = scale_columns[:, s : s + 1]
    gains = gain[...].astype(F32)
    along_y = c == 0
    for m in range(4):
        to_y = x ^ m ^ y
        for j in range(2):
            source_c = c ^ j
            s = (x ^ m) * 2 + source_c
            rows = pieces[m][j * 64 : j * 64 + 64, :].astype(F32)
            of_core = pl.ds(pl.multiple_of(c * 64, 64), 64)
            rows = ((rows - mean_of[s, of_core]) * scale_of[s, of_core] * gains).astype(BF16)
            for b in range(2):
                to_z = (source_c * 2 + b) ^ z
                first = jnp.where(along_y, to_y, to_z)
                second = jnp.where(along_y, to_z, to_y)
                normed[first, second] = rows[b * 32 : b * 32 + 32]
    left = normed[...].reshape(512, normed.shape[-1])

    def put(part, at, size):
        for k, out in enumerate(outs):
            out[:, at : at + size] = part[k * 128 : k * 128 + 128]

    dims = (((1,), (1,)), ((), ()))
    wide = tiles.shape[2]
    width = tiles.shape[0] * wide
    pair = jnp.concatenate([pairs[0][...], pairs[1][...]], axis=0)
    pair = lax.dot_general(left, pair, dims, preferred_element_type=F32).astype(BF16)
    put(pair, width, pair.shape[1])
    for t, load in enumerate(loads):
        load.wait()
        put(jnp.dot(left, tiles[t], preferred_element_type=F32).astype(BF16), t * wide, wide)


def project(place, stats, gain, pieces, weights, pairs):
    depth, width = weights[0].shape
    out = jax.ShapeDtypeStruct((128, 2 * (width + pairs[0].shape[0])), BF16)
    count = 2 * width // 512
    return pl.pallas_call(
        project_kernel,
        out_shape=[out] * 4,
        in_specs=[SMEM] + [VMEM] * 6 + [ANY] * 2 + [VMEM] * 2,
        out_specs=[VMEM] * 4,
        scratch_shapes=[
            pltpu.VMEM((4, 4, 32, depth), BF16),
            pltpu.VMEM((8, 128, 1), F32),
            pltpu.VMEM((8, 128, 1), F32),
            pltpu.VMEM((count, depth, 512), BF16),
            pltpu.SemaphoreType.DMA((count,)),
        ],
        compiler_params=params(32),
        cost_estimate=cost(8e9, 1.2e7),
        name="project",
    )(place, stats, gain, *pieces, *weights, *pairs)


def sum_of(refs):
    total = refs[0][...].astype(F32)
    for ref in refs[1:]:
        total = total + ref[...].astype(F32)
    return total


def add_and_cut_kernel(*refs):
    total = sum_of(refs[:4]).astype(BF16)
    rows = total.shape[0] // 4
    for k in range(4):
        refs[4 + k][...] = total[k * rows : k * rows + rows]


def add_and_cut(values):
    rows, width = values[0].shape
    out = jax.ShapeDtypeStruct((rows // 4, width), BF16)
    return pl.pallas_call(
        add_and_cut_kernel,
        out_shape=[out] * 4,
        in_specs=[VMEM] * 4,
        out_specs=[VMEM] * 4,
        compiler_params=params(12),
        cost_estimate=cost(1e8, 1e6),
        name="add_and_cut",
    )(*values)


def finish_kernel(place, *refs):
    ins, outs, blocks = refs[:4], refs[4:8], refs[8]
    total = sum_of(ins)
    for i in range(4):
        blocks[place[2] ^ i] = total[i * 8 : i * 8 + 8]
    for m in range(4):
        outs[m][...] = blocks[m].astype(BF16)


def finish(place, values):
    rows, width = values[0].shape
    out = jax.ShapeDtypeStruct((rows // 4, width), BF16)
    return pl.pallas_call(
        finish_kernel,
        out_shape=[out] * 4,
        in_specs=[SMEM] + [VMEM] * 4,
        out_specs=[VMEM] * 4,
        scratch_shapes=[pltpu.VMEM((4, rows // 4, width), F32)],
        compiler_params=params(8),
        cost_estimate=cost(1e8, 1e6),
        name="finish",
    )(place, *values)


def line_up_kernel(place, *refs):
    ins, out, blocks = refs[:4], refs[4], refs[5]
    for m in range(4):
        blocks[place[2] ^ m] = ins[m][...].astype(F32)
    out[...] = blocks[...].reshape(out.shape).astype(BF16)


def line_up(place, values):
    rows, width = values[0].shape
    return pl.pallas_call(
        line_up_kernel,
        out_shape=jax.ShapeDtypeStruct((4 * rows, width), BF16),
        in_specs=[SMEM] + [VMEM] * 4,
        out_specs=VMEM,
        scratch_shapes=[pltpu.VMEM((4, rows, width), F32)],
        compiler_params=params(8),
        cost_estimate=cost(1e8, 1e6),
        name="line_up",
    )(place, *values)


def attend_kernel(lengths, place, *refs):
    packed, (cosine, sine, keys, values), outs = refs[:4], refs[4:8], refs[8:12]
    query_rows, new_pieces, new_kv, result = refs[12:]
    request = pl.program_id(0)
    width = outs[0].shape[1]
    heads = width // HD
    count = 4 * heads

    @pl.when(request == 0)
    def _():
        x, c = place[2], place[3]
        cos, sin = cosine[...], sine[...]

        def rotated(first, second):
            return first * cos - second * sin, second * cos + first * sin

        for m in range(4):
            rows = packed[m][...].astype(F32)
            for h in range(heads):
                head = rows[:, h * HD : h * HD + HD]
                for i, half in enumerate(rotated(head[:, :128], head[:, 128:])):
                    query_rows[i, pl.ds(m * heads + h, 8, stride=count), :] = half
            size = (rows.shape[1] - width) // 2
            for j in range(2):
                at = width + j * size
                new_pieces[(x ^ m) * 2 + (c ^ j)] = rows[:, at : at + size]
        halves = [
            jnp.concatenate([new_pieces[i], new_pieces[i + 1]], axis=-1) for i in range(0, 8, 2)
        ]
        new_kv[0] = jnp.concatenate(rotated(halves[0], halves[1]), axis=-1).astype(BF16)
        new_kv[1] = jnp.concatenate(halves[2:], axis=-1).astype(BF16)

    per = STEPS * count
    start = pl.multiple_of(request * per, per)
    query = jnp.concatenate([query_rows[i, pl.ds(start, per), :] for i in range(2)], axis=-1)
    query = (query.astype(BF16).astype(F32) * HD ** (-0.5)).astype(BF16)
    dims = (((1,), (1,)), ((), ()))
    cached = lax.dot_general(query, keys[0], dims, preferred_element_type=F32)
    slots = lax.broadcasted_iota(jnp.int32, cached.shape, 1)
    cached = jnp.where(slots < lengths[request], cached, -jnp.inf)
    fresh = lax.dot_general(query, new_kv[0], dims, preferred_element_type=F32)
    row_step = lax.broadcasted_iota(jnp.int32, fresh.shape, 0) // count
    key_step = lax.broadcasted_iota(jnp.int32, fresh.shape, 1) - request * STEPS
    fresh = jnp.where((key_step >= 0) & (key_step <= row_step), fresh, -jnp.inf)
    top = jnp.maximum(
        jnp.max(cached, axis=-1, keepdims=True), jnp.max(fresh, axis=-1, keepdims=True)
    )
    cached = jnp.exp(cached - top)
    fresh = jnp.exp(fresh - top)
    denom = jnp.sum(cached, axis=-1, keepdims=True) + jnp.sum(fresh, axis=-1, keepdims=True)
    mixed = jnp.dot(cached.astype(BF16), values[0], preferred_element_type=F32)
    mixed = mixed + jnp.dot(fresh.astype(BF16), new_kv[1], preferred_element_type=F32)
    mixed = mixed / denom
    for i in range(2):
        result[i, pl.ds(start, per), :] = mixed[:, i * 128 : i * 128 + 128]

    @pl.when(request == pl.num_programs(0) - 1)
    def _():
        for m, out in enumerate(outs):
            halves = [
                result[i, pl.ds(m * heads + h, 8, stride=count), :]
                for h in range(heads)
                for i in range(2)
            ]
            out[...] = jnp.concatenate(halves, axis=-1).astype(BF16)


def attend(place, packed, cosine, sine, cache_keys, cache_values, lengths, width):
    requests, slots, _ = cache_keys.shape
    total = packed[0].shape[1]
    count = 4 * (width // HD)
    whole = lambda *shape: pl.BlockSpec(shape, lambda r, *_: (0,) * len(shape))
    cache = pl.BlockSpec((1, slots, HD), lambda r, *_: (r, 0, 0))
    return pl.pallas_call(
        attend_kernel,
        out_shape=[jax.ShapeDtypeStruct((8, width), BF16)] * 4,
        grid_spec=pltpu.PrefetchScalarGridSpec(
            num_scalar_prefetch=2,
            grid=(requests,),
            in_specs=[whole(8, total)] * 4 + [whole(8, 128)] * 2 + [cache] * 2,
            out_specs=[whole(8, width)] * 4,
            scratch_shapes=[
                pltpu.VMEM((2, 8 * count, 128), F32),
                pltpu.VMEM((8, 8, (total - width) // 2), F32),
                pltpu.VMEM((2, 8, HD), BF16),
                pltpu.VMEM((2, 8 * count, 128), F32),
            ],
        ),
        compiler_params=params(52),
        cost_estimate=cost(6e9, 1.8e7),
        name="attend",
    )(lengths, place, *packed, cosine, sine, cache_keys, cache_values)


def mix_kernel(place, *refs):
    lefts, weights, outs = refs[:4], refs[4:6], refs[6:10]
    rows, tiles, sems = refs[10:]
    count = tiles.shape[0] // 2
    loads = load_tiles(weights[0], tiles, sems, 0) + load_tiles(weights[1], tiles, sems, count)
    y, z, x, c = place[0], place[1], place[2], place[3]
    along_y = c == 0
    for second in range(4):
        for first in range(4):
            to_x = y ^ x ^ jnp.where(along_y, first, second)
            token_z = z ^ jnp.where(along_y, second, first)
            slot = (token_z // 2 ^ c) * 2 + token_z % 2
            rows[to_x, slot] = lefts[second][first * 32 : first * 32 + 32, :]
    left = rows[...].reshape(512, rows.shape[-1])
    depth = left.shape[1] // 2
    wide = tiles.shape[2]
    for t in range(count):
        loads[t].wait()
        part = jnp.dot(left[:, :depth], tiles[t], preferred_element_type=F32)
        loads[count + t].wait()
        part = part + jnp.dot(left[:, depth:], tiles[count + t], preferred_element_type=F32)
        part = part.astype(BF16)
        for k, out in enumerate(outs):
            out[:, t * wide : t * wide + wide] = part[k * 128 : k * 128 + 128]


def mix(place, lefts, weights):
    depth, width = weights[0].shape
    return pl.pallas_call(
        mix_kernel,
        out_shape=[jax.ShapeDtypeStruct((128, width), BF16)] * 4,
        in_specs=[SMEM] + [VMEM] * 4 + [ANY] * 2,
        out_specs=[VMEM] * 4,
        scratch_shapes=[
            pltpu.VMEM((4, 4, 32, 2 * depth), BF16),
            pltpu.VMEM((6, depth, width // 3), BF16),
            pltpu.SemaphoreType.DMA((6,)),
        ],
        compiler_params=params(32),
        cost_estimate=cost(8e9, 1.2e7),
        name="mix",
    )(place, *lefts, *weights)


def last_sum_kernel(*refs):
    total = sum_of(refs[:4]).astype(BF16)
    refs[4][...] = total[:64]
    refs[5][...] = total[64:]


def last_sum(values):
    half = jax.ShapeDtypeStruct((64, values[0].shape[1]), BF16)
    return pl.pallas_call(
        last_sum_kernel,
        out_shape=[half] * 2,
        in_specs=[VMEM] * 4,
        out_specs=[VMEM] * 2,
        compiler_params=params(8),
        cost_estimate=cost(1e8, 1e6),
        name="last_sum",
    )(*values)


def interleave_kernel(place, mine, theirs, out):
    first, second = mine[...].astype(F32), theirs[...].astype(F32)
    swap = place[3] == 1
    first, second = jnp.where(swap, second, first), jnp.where(swap, first, second)
    groups = []
    for i in range(8):
        groups += [first[i * 8 : i * 8 + 8], second[i * 8 : i * 8 + 8]]
    out[...] = jnp.concatenate(groups, axis=0).astype(BF16)


def interleave(place, mine, theirs):
    rows, width = mine.shape
    return pl.pallas_call(
        interleave_kernel,
        out_shape=jax.ShapeDtypeStruct((2 * rows, width), BF16),
        in_specs=[SMEM] + [VMEM] * 2,
        out_specs=VMEM,
        compiler_params=params(8),
        cost_estimate=cost(1e8, 1e6),
        name="interleave",
    )(place, mine, theirs)


def per_device(tokens, norm_gain, w_query, w_keyvalue, w_out, cache_keys, cache_values, lengths):
    gx, gy = lax.axis_index("gx"), lax.axis_index("gy")
    place = jnp.stack([gx // 4, gx % 4, gy // 2, gy % 2]).astype(jnp.int32)

    stats, mine, theirs = prepare(place, tokens)
    piece = jnp.concatenate([mine, other_core(theirs)], axis=0)
    piece, stats = lax.optimization_barrier((piece, stats))
    pieces = exchanged(along_x, [piece] * 4)
    stats = lax.all_to_all(stats, ("gx", "gy"), 0, 0, tiled=True).reshape(128, 256)
    w_pair = w_keyvalue.T
    weights = [w_query, other_core(w_query)]
    parts = project(
        place, stats, norm_gain[None], pieces, weights, [w_pair, other_core(w_pair)]
    )

    parts = add_and_cut(exchanged(along_first, parts))
    parts = finish(place, exchanged(along_second, parts))
    packed = exchanged(along_x, parts)

    half_dim = HD // 2
    freqs = 10000.0 ** (-jnp.arange(half_dim, dtype=F32) / half_dim)
    positions = lengths[:, None] + jnp.arange(STEPS, dtype=jnp.int32)[None, :]
    angles = positions.reshape(-1).astype(F32)[:, None] * freqs
    attended = attend(
        place,
        packed,
        jnp.cos(angles),
        jnp.sin(angles),
        cache_keys,
        cache_values,
        lengths,
        2 * w_query.shape[1],
    )

    rows = line_up(place, exchanged(along_x, attended))
    rows = jnp.concatenate(exchanged(along_first, [rows] * 4), axis=0)
    parts = mix(place, exchanged(along_second, [rows] * 4), [w_out, other_core(w_out)])
    mine, theirs = last_sum(exchanged(along_x, parts))
    return interleave(place, mine, other_core(theirs))


def solution(mesh):
    return jax.shard_map(
        per_device,
        mesh=mesh,
        in_specs=(
            P("gy", "gx"),
            P("gx"),
            P("gx", "gy"),
            P("gx", "gy"),
            P("gy", "gx"),
            P(("gx", "gy"), None, None),
            P(("gx", "gy"), None, None),
            P(("gx", "gy")),
        ),
        out_specs=P("gy", "gx"),
        check_vma=False,
    )
```

```python
import functools

import jax
import jax.numpy as jnp
from jax import lax
from jax.experimental import pallas as pl
from jax.experimental.pallas import tpu as pltpu
from jax.sharding import PartitionSpec as P

D = 18432
HD = 256
STEPS = 2
VMEM = pl.BlockSpec(memory_space=pltpu.VMEM)
SMEM = pl.BlockSpec(memory_space=pltpu.SMEM)
ANY = pl.BlockSpec(memory_space=pl.ANY)
F32 = jnp.float32
BF16 = jnp.bfloat16


def params(mib):
    return pltpu.CompilerParams(vmem_limit_bytes=mib * 1024 * 1024)


def cost(flops, size):
    return pl.CostEstimate(flops=int(flops), bytes_accessed=int(size), transcendentals=0)


def exchange_pairs(core_along_y, m):
    pairs = []
    for d in range(128):
        far = 32 * m if d % 2 == core_along_y else 8 * m
        pairs.append((d, d ^ far))
    return pairs


def along_first(value, m):
    return lax.ppermute(value, ("gx", "gy"), exchange_pairs(0, m))


def along_second(value, m):
    return lax.ppermute(value, ("gx", "gy"), exchange_pairs(1, m))


def along_x(value, m):
    return lax.ppermute(value, "gy", [(g, g ^ (2 * m)) for g in range(8)])


def other_core(value):
    return lax.ppermute(value, "gy", [(g, g ^ 1) for g in range(8)])


def exchanged(along, parts):
    return [parts[0]] + [along(parts[m], m) for m in range(1, 4)]


def groups_of(rows, first):
    groups = [rows[at + first : at + first + 8] for at in range(0, rows.shape[0], 16)]
    return jnp.concatenate(groups, axis=0)


def prepare_kernel(place, tokens, theirs, stats, piece):
    rows, others = tokens[...].astype(F32), theirs[...].astype(F32)
    by_core = [groups_of(rows, 0), groups_of(rows, 8)]
    swap = place[3] == 1
    piece[:64] = jnp.where(swap, by_core[1], by_core[0]).astype(BF16)
    piece[64:] = jnp.where(swap, groups_of(others, 8), groups_of(others, 0)).astype(BF16)
    lines = []
    for power in range(2):
        sums = [
            jnp.sum(part if power == 0 else part * part, axis=1, keepdims=True) for part in by_core
        ]
        column = jnp.broadcast_to(jnp.concatenate(sums, axis=0), (128, 128))
        lines.append(column.T[0:1])
    line = jnp.concatenate(lines, axis=1)
    stats[...] = jnp.broadcast_to(line[:, None, :], stats.shape)


def prepare(place, tokens, theirs):
    return pl.pallas_call(
        prepare_kernel,
        out_shape=[
            jax.ShapeDtypeStruct((128, 1, 256), F32),
            jax.ShapeDtypeStruct(tokens.shape, BF16),
        ],
        in_specs=[SMEM, VMEM, VMEM],
        out_specs=[VMEM] * 2,
        compiler_params=params(8),
        cost_estimate=cost(1e8, 1e6),
        name="prepare",
    )(place, tokens, theirs)


def load_tiles(source, tiles, sems, at):
    loads = []
    wide = tiles.shape[2]
    for t in range(source.shape[1] // wide):
        load = pltpu.make_async_copy(
            source.at[:, pl.ds(t * wide, wide)], tiles.at[at + t], sems.at[at + t]
        )
        load.start()
        loads.append(load)
    return loads


def fill_left(blocks, place, gain, pieces, left):
    y, z, x, c = place[0], place[1], place[2], place[3]
    gains = gain[...].astype(F32)
    along_y = c == 0
    for m in range(4):
        to_y = x ^ m ^ y
        for j in range(2):
            for b in range(2):
                to_z = ((c ^ j) * 2 + b) ^ z
                first = jnp.where(along_y, to_y, to_z)
                second = jnp.where(along_y, to_z, to_y)

                @pl.when((first == blocks[0]) | (first == blocks[1]))
                def _():
                    at = j * 64 + b * 32
                    rows = pieces[m][at : at + 32, :].astype(F32)
                    rows = rows - jnp.sum(rows, axis=1, keepdims=True) / rows.shape[1]
                    slot = jnp.where(first == blocks[0], 0, 4) + second
                    left[pl.ds(pl.multiple_of(slot * 32, 32), 32)] = (rows * gains).astype(BF16)


def multiply(left, tiles, loads, pairs, put):
    wide = tiles.shape[2]
    width = tiles.shape[0] * wide
    pair = jnp.concatenate([pairs[0][...], pairs[1][...]], axis=0)
    dims = (((1,), (1,)), ((), ()))
    put(lax.dot_general(left[...], pair, dims, preferred_element_type=F32), width, pair.shape[0])
    for t, load in enumerate(loads):
        load.wait()
        put(jnp.dot(left[...], tiles[t], preferred_element_type=F32), t * wide, wide)


def load_both(weights, tiles, sems):
    count = tiles.shape[0] // 2
    return load_tiles(weights[0], tiles, sems, 0) + load_tiles(weights[1], tiles, sems, count)


def project_kernel(blocks, place, gain, *refs):
    pieces, weights, pairs = refs[:4], refs[4:6], refs[6:8]
    out, gain_row, left, tiles, sems = refs[8:]
    loads = load_both(weights, tiles, sems)
    left[256:] = jnp.broadcast_to(gain[...], (16, gain.shape[1]))
    fill_left(blocks, place, gain, pieces, left)

    def put(part, at, size):
        out[:, at : at + size] = part[:256].astype(BF16)
        gain_row[:, at : at + size] = part[256:264]

    multiply(left, tiles, loads, pairs, put)


def project_scratch(rows, weights):
    depth, width = weights[0].shape
    count = 2 * width // 512
    return [
        pltpu.VMEM((rows, depth), BF16),
        pltpu.VMEM((count, depth, 512), BF16),
        pltpu.SemaphoreType.DMA((count,)),
    ]


def project(blocks, place, gain, pieces, weights, pairs):
    total = 2 * (weights[0].shape[1] + pairs[0].shape[0])
    return pl.pallas_call(
        functools.partial(project_kernel, blocks),
        out_shape=[
            jax.ShapeDtypeStruct((256, total), BF16),
            jax.ShapeDtypeStruct((8, total), F32),
        ],
        in_specs=[SMEM] + [VMEM] * 5 + [ANY] * 2 + [VMEM] * 2,
        out_specs=[VMEM] * 2,
        scratch_shapes=project_scratch(272, weights),
        compiler_params=params(48),
        cost_estimate=cost(4e9, 1e7),
        name="project",
    )(place, gain, *pieces, *weights, *pairs)


def fill_columns(place, stats, shift_of, scale_of):
    y, z = place[0], place[1]
    total = stats[0:8, :]
    for g in range(1, 16):
        total = total + stats[g * 8 : g * 8 + 8, :]
    mean = total[:, :128] / D
    variance = total[:, 128:] / D - mean * mean
    here = stats[pl.ds(pl.multiple_of((y * 4 + z) * 8, 8), 8), :]
    shift_columns = (here[:, :128] / (D // 16) - mean).T
    scale_columns = lax.rsqrt(variance + 1e-05).T
    for s in range(8):
        shift_of[s] = shift_columns[:, s : s + 1]
        scale_of[s] = scale_columns[:, s : s + 1]


def columns_of(place, block, second):
    y, z, c = place[0], place[1], place[3]
    token_y = y ^ jnp.where(c == 0, block, second)
    token_z = z ^ jnp.where(c == 0, second, block)
    rows = pl.ds(pl.multiple_of(c * 64 + token_z % 2 * 32, 32), 32)
    return token_y * 2 + token_z // 2, rows


def scale_kernel(blocks, place, stats, gain_row, parts, *refs):
    outs, shift_of, scale_of = refs[:2], refs[2], refs[3]
    fill_columns(place, stats, shift_of, scale_of)
    line = gain_row[0:1, :]
    for i, out in enumerate(outs):
        for second in range(4):
            s, at = columns_of(place, blocks[i], second)
            rows = parts[i * 128 + second * 32 : i * 128 + second * 32 + 32, :]
            rows = (rows.astype(F32) + shift_of[s, at] * line) * scale_of[s, at]
            out[second * 32 : second * 32 + 32, :] = rows.astype(BF16)


def scale(blocks, place, stats, gain_row, parts):
    out = jax.ShapeDtypeStruct((128, parts.shape[1]), BF16)
    return pl.pallas_call(
        functools.partial(scale_kernel, blocks),
        out_shape=[out] * 2,
        in_specs=[SMEM] + [VMEM] * 3,
        out_specs=[VMEM] * 2,
        scratch_shapes=[pltpu.VMEM((8, 128, 1), F32)] * 2,
        compiler_params=params(12),
        cost_estimate=cost(1e9, 2e6),
        name="scale",
    )(place, stats, gain_row, parts)


def project_rest_kernel(blocks, place, stats, gain_row, gain, *refs):
    pieces, weights, pairs = refs[:4], refs[4:6], refs[6:8]
    outs, (left, tiles, sems, shift_of, scale_of, shift, factor) = refs[8:10], refs[10:]
    loads = load_both(weights, tiles, sems)
    fill_columns(place, stats, shift_of, scale_of)
    for k in range(8):
        s, at = columns_of(place, blocks[k // 4], k % 4)
        shift[k * 32 : k * 32 + 32] = shift_of[s, at]
        factor[k * 32 : k * 32 + 32] = scale_of[s, at]
    fill_left(blocks, place, gain, pieces, left)

    def put(part, at, size):
        line = gain_row[0:1, at : at + size]
        part = ((part + shift[...] * line) * factor[...]).astype(BF16)
        for i, out in enumerate(outs):
            out[:, at : at + size] = part[i * 128 : i * 128 + 128]

    multiply(left, tiles, loads, pairs, put)


def project_rest(blocks, place, stats, gain_row, gain, pieces, weights, pairs):
    out = jax.ShapeDtypeStruct((128, gain_row.shape[1]), BF16)
    return pl.pallas_call(
        functools.partial(project_rest_kernel, blocks),
        out_shape=[out] * 2,
        in_specs=[SMEM] + [VMEM] * 7 + [ANY] * 2 + [VMEM] * 2,
        out_specs=[VMEM] * 2,
        scratch_shapes=project_scratch(256, weights)
        + [pltpu.VMEM((8, 128, 1), F32)] * 2
        + [pltpu.VMEM((256, 1), F32)] * 2,
        compiler_params=params(48),
        cost_estimate=cost(5e9, 1e7),
        name="project_rest",
    )(place, stats, gain_row, gain, *pieces, *weights, *pairs)


def sum_of(refs):
    total = refs[0][...].astype(F32)
    for ref in refs[1:]:
        total = total + ref[...].astype(F32)
    return total


def add_and_cut_kernel(*refs):
    total = sum_of(refs[:4]).astype(BF16)
    rows = total.shape[0] // 4
    for k in range(4):
        refs[4 + k][...] = total[k * rows : k * rows + rows]


def add_and_cut(values):
    rows, width = values[0].shape
    out = jax.ShapeDtypeStruct((rows // 4, width), BF16)
    return pl.pallas_call(
        add_and_cut_kernel,
        out_shape=[out] * 4,
        in_specs=[VMEM] * 4,
        out_specs=[VMEM] * 4,
        compiler_params=params(12),
        cost_estimate=cost(1e8, 1e6),
        name="add_and_cut",
    )(*values)


def finish_kernel(place, *refs):
    ins, outs, blocks = refs[:4], refs[4:8], refs[8]
    total = sum_of(ins)
    for i in range(4):
        blocks[place[2] ^ i] = total[i * 8 : i * 8 + 8]
    for m in range(4):
        outs[m][...] = blocks[m].astype(BF16)


def finish(place, values):
    rows, width = values[0].shape
    out = jax.ShapeDtypeStruct((rows // 4, width), BF16)
    return pl.pallas_call(
        finish_kernel,
        out_shape=[out] * 4,
        in_specs=[SMEM] + [VMEM] * 4,
        out_specs=[VMEM] * 4,
        scratch_shapes=[pltpu.VMEM((4, rows // 4, width), F32)],
        compiler_params=params(8),
        cost_estimate=cost(1e8, 1e6),
        name="finish",
    )(place, *values)


def line_up_kernel(place, *refs):
    ins, out, blocks = refs[:4], refs[4], refs[5]
    for m in range(4):
        blocks[place[2] ^ m] = ins[m][...].astype(F32)
    out[...] = blocks[...].reshape(out.shape).astype(BF16)


def line_up(place, values):
    rows, width = values[0].shape
    return pl.pallas_call(
        line_up_kernel,
        out_shape=jax.ShapeDtypeStruct((4 * rows, width), BF16),
        in_specs=[SMEM] + [VMEM] * 4,
        out_specs=VMEM,
        scratch_shapes=[pltpu.VMEM((4, rows, width), F32)],
        compiler_params=params(8),
        cost_estimate=cost(1e8, 1e6),
        name="line_up",
    )(place, *values)


def attend_kernel(lengths, place, *refs):
    packed, (cosine, sine, keys, values), outs = refs[:4], refs[4:8], refs[8:12]
    query_rows, new_pieces, new_kv, result = refs[12:]
    request = pl.program_id(0)
    width = outs[0].shape[1]
    heads = width // HD
    count = 4 * heads

    @pl.when(request == 0)
    def _():
        x, c = place[2], place[3]
        cos, sin = cosine[...], sine[...]

        def rotated(first, second):
            return first * cos - second * sin, second * cos + first * sin

        for m in range(4):
            rows = packed[m][...].astype(F32)
            for h in range(heads):
                head = rows[:, h * HD : h * HD + HD]
                for i, half in enumerate(rotated(head[:, :128], head[:, 128:])):
                    query_rows[i, pl.ds(m * heads + h, 8, stride=count), :] = half
            size = (rows.shape[1] - width) // 2
            for j in range(2):
                at = width + j * size
                new_pieces[(x ^ m) * 2 + (c ^ j)] = rows[:, at : at + size]
        halves = [
            jnp.concatenate([new_pieces[i], new_pieces[i + 1]], axis=-1) for i in range(0, 8, 2)
        ]
        new_kv[0] = jnp.concatenate(rotated(halves[0], halves[1]), axis=-1).astype(BF16)
        new_kv[1] = jnp.concatenate(halves[2:], axis=-1).astype(BF16)

    per = STEPS * count
    start = pl.multiple_of(request * per, per)
    query = jnp.concatenate([query_rows[i, pl.ds(start, per), :] for i in range(2)], axis=-1)
    query = (query.astype(BF16).astype(F32) * HD ** (-0.5)).astype(BF16)
    dims = (((1,), (1,)), ((), ()))
    cached = lax.dot_general(query, keys[0], dims, preferred_element_type=F32)
    slots = lax.broadcasted_iota(jnp.int32, cached.shape, 1)
    cached = jnp.where(slots < lengths[request], cached, -jnp.inf)
    fresh = lax.dot_general(query, new_kv[0], dims, preferred_element_type=F32)
    row_step = lax.broadcasted_iota(jnp.int32, fresh.shape, 0) // count
    key_step = lax.broadcasted_iota(jnp.int32, fresh.shape, 1) - request * STEPS
    fresh = jnp.where((key_step >= 0) & (key_step <= row_step), fresh, -jnp.inf)
    top = jnp.maximum(
        jnp.max(cached, axis=-1, keepdims=True), jnp.max(fresh, axis=-1, keepdims=True)
    )
    cached = jnp.exp(cached - top)
    fresh = jnp.exp(fresh - top)
    denom = jnp.sum(cached, axis=-1, keepdims=True) + jnp.sum(fresh, axis=-1, keepdims=True)
    mixed = jnp.dot(cached.astype(BF16), values[0], preferred_element_type=F32)
    mixed = mixed + jnp.dot(fresh.astype(BF16), new_kv[1], preferred_element_type=F32)
    mixed = mixed / denom
    for i in range(2):
        result[i, pl.ds(start, per), :] = mixed[:, i * 128 : i * 128 + 128]

    @pl.when(request == pl.num_programs(0) - 1)
    def _():
        for m, out in enumerate(outs):
            halves = [
                result[i, pl.ds(m * heads + h, 8, stride=count), :]
                for h in range(heads)
                for i in range(2)
            ]
            out[...] = jnp.concatenate(halves, axis=-1).astype(BF16)


def attend(place, packed, cosine, sine, cache_keys, cache_values, lengths, width):
    requests, slots, _ = cache_keys.shape
    total = packed[0].shape[1]
    count = 4 * (width // HD)
    whole = lambda *shape: pl.BlockSpec(shape, lambda r, *_: (0,) * len(shape))
    cache = pl.BlockSpec((1, slots, HD), lambda r, *_: (r, 0, 0))
    return pl.pallas_call(
        attend_kernel,
        out_shape=[jax.ShapeDtypeStruct((8, width), BF16)] * 4,
        grid_spec=pltpu.PrefetchScalarGridSpec(
            num_scalar_prefetch=2,
            grid=(requests,),
            in_specs=[whole(8, total)] * 4 + [whole(8, 128)] * 2 + [cache] * 2,
            out_specs=[whole(8, width)] * 4,
            scratch_shapes=[
                pltpu.VMEM((2, 8 * count, 128), F32),
                pltpu.VMEM((8, 8, (total - width) // 2), F32),
                pltpu.VMEM((2, 8, HD), BF16),
                pltpu.VMEM((2, 8 * count, 128), F32),
            ],
        ),
        compiler_params=params(52),
        cost_estimate=cost(6e9, 1.8e7),
        name="attend",
    )(lengths, place, *packed, cosine, sine, cache_keys, cache_values)


def multiply_rows(lefts, tiles, loads, put):
    left = jnp.concatenate([ref[...] for ref in lefts], axis=0)
    depth = left.shape[1] // 2
    count = tiles.shape[0] // 2
    wide = tiles.shape[2]
    for t in range(count):
        loads[t].wait()
        part = jnp.dot(left[:, :depth], tiles[t], preferred_element_type=F32)
        loads[count + t].wait()
        part = part + jnp.dot(left[:, depth:], tiles[count + t], preferred_element_type=F32)
        put(part.astype(BF16), t * wide, wide)


def mix_kernel(*refs):
    lefts, weights, out, tiles, sems = refs[:3], refs[3:5], refs[5], refs[6], refs[7]
    loads = load_tiles(weights[0], tiles, sems, 0) + load_tiles(weights[1], tiles, sems, 3)

    def put(part, at, size):
        out[:, at : at + size] = part

    multiply_rows(lefts, tiles, loads, put)


def mix_rest_kernel(place, done, last, *refs):
    weights, outs = refs[:2], refs[2:6]
    result, tiles, sems = refs[6:]
    loads = load_tiles(weights[0], tiles, sems, 0) + load_tiles(weights[1], tiles, sems, 3)
    y, z, x, c = place[0], place[1], place[2], place[3]
    along_y = c == 0

    def slots(second, first):
        to_x = y ^ x ^ jnp.where(along_y, first, second)
        token_z = z ^ jnp.where(along_y, second, first)
        return to_x, (token_z // 2 ^ c) * 2 + token_z % 2

    for k in range(12):
        result[slots((0, 1, 3)[k // 4], k % 4)] = done[k * 32 : k * 32 + 32, :]

    def put(part, at, size):
        for k in range(4):
            to_x, slot = slots(2, k)
            result[to_x, slot, :, at : at + size] = part[k * 32 : k * 32 + 32]

    multiply_rows([last], tiles, loads, put)
    for k, out in enumerate(outs):
        out[...] = result[k].reshape(out.shape)


def mix_scratch(depth, width):
    return [pltpu.VMEM((6, depth, width // 3), BF16), pltpu.SemaphoreType.DMA((6,))]


def mix(lefts, weights):
    depth, width = weights[0].shape
    return pl.pallas_call(
        mix_kernel,
        out_shape=jax.ShapeDtypeStruct((384, width), BF16),
        in_specs=[VMEM] * 3 + [ANY] * 2,
        out_specs=VMEM,
        scratch_shapes=mix_scratch(depth, width),
        compiler_params=params(24),
        cost_estimate=cost(4e9, 8e6),
        name="mix",
    )(*lefts, *weights)


def mix_rest(place, done, last, weights):
    depth, width = weights[0].shape
    return pl.pallas_call(
        mix_rest_kernel,
        out_shape=[jax.ShapeDtypeStruct((128, width), BF16)] * 4,
        in_specs=[SMEM] + [VMEM] * 2 + [ANY] * 2,
        out_specs=[VMEM] * 4,
        scratch_shapes=[pltpu.VMEM((4, 4, 32, width), BF16)] + mix_scratch(depth, width),
        compiler_params=params(24),
        cost_estimate=cost(4e9, 8e6),
        name="mix_rest",
    )(place, done, last, *weights)


def last_sum_kernel(*refs):
    total = sum_of(refs[:4]).astype(BF16)
    refs[4][...] = total[:64]
    refs[5][...] = total[64:]


def last_sum(values):
    half = jax.ShapeDtypeStruct((64, values[0].shape[1]), BF16)
    return pl.pallas_call(
        last_sum_kernel,
        out_shape=[half] * 2,
        in_specs=[VMEM] * 4,
        out_specs=[VMEM] * 2,
        compiler_params=params(8),
        cost_estimate=cost(1e8, 1e6),
        name="last_sum",
    )(*values)


def interleave_kernel(place, mine, theirs, out):
    first, second = mine[...].astype(F32), theirs[...].astype(F32)
    swap = place[3] == 1
    first, second = jnp.where(swap, second, first), jnp.where(swap, first, second)
    groups = []
    for i in range(8):
        groups += [first[i * 8 : i * 8 + 8], second[i * 8 : i * 8 + 8]]
    out[...] = jnp.concatenate(groups, axis=0).astype(BF16)


def interleave(place, mine, theirs):
    rows, width = mine.shape
    return pl.pallas_call(
        interleave_kernel,
        out_shape=jax.ShapeDtypeStruct((2 * rows, width), BF16),
        in_specs=[SMEM] + [VMEM] * 2,
        out_specs=VMEM,
        compiler_params=params(8),
        cost_estimate=cost(1e8, 1e6),
        name="interleave",
    )(place, mine, theirs)


def per_device(tokens, norm_gain, w_query, w_keyvalue, w_out, cache_keys, cache_values, lengths):
    gx, gy = lax.axis_index("gx"), lax.axis_index("gy")
    place = jnp.stack([gx // 4, gx % 4, gy // 2, gy % 2]).astype(jnp.int32)

    stats, piece = prepare(place, tokens, other_core(tokens))
    pieces = exchanged(along_x, [piece] * 4)
    stats = lax.all_to_all(stats, ("gx", "gy"), 0, 0, tiled=True)
    w_pair = w_keyvalue.T
    w_query, w_pair, piece = lax.optimization_barrier((w_query, w_pair, piece))
    weights, pairs = [w_query, other_core(w_query)], [w_pair, other_core(w_pair)]
    gain = norm_gain[None]
    parts, gain_row = project((1, 3), place, gain, pieces, weights, pairs)
    parts, stats = lax.optimization_barrier((parts, stats))
    stats = stats.reshape(128, 256)
    sent = scale((1, 3), place, stats, gain_row, parts)
    kept = project_rest((2, 0), place, stats, gain_row, gain, pieces, weights, pairs)
    parts = [kept[1], sent[0], kept[0], sent[1]]

    parts = add_and_cut(exchanged(along_first, parts))
    parts = finish(place, exchanged(along_second, parts))
    packed = exchanged(along_x, parts)

    half_dim = HD // 2
    freqs = 10000.0 ** (-jnp.arange(half_dim, dtype=F32) / half_dim)
    positions = lengths[:, None] + jnp.arange(STEPS, dtype=jnp.int32)[None, :]
    angles = positions.reshape(-1).astype(F32)[:, None] * freqs
    attended = attend(
        place,
        packed,
        jnp.cos(angles),
        jnp.sin(angles),
        cache_keys,
        cache_values,
        lengths,
        2 * w_query.shape[1],
    )

    rows = line_up(place, exchanged(along_x, attended))
    rows = jnp.concatenate(exchanged(along_first, [rows] * 4), axis=0)
    near = [along_second(rows, 1), along_second(rows, 3)]
    late, *near = lax.optimization_barrier((rows, *near))
    blocks = [rows, near[0], along_second(late, 2), near[1]]
    weights = [w_out, other_core(w_out)]
    done = mix([blocks[0], blocks[1], blocks[3]], weights)
    parts = mix_rest(place, done, blocks[2], weights)
    mine, theirs = last_sum(exchanged(along_x, parts))
    return interleave(place, mine, other_core(theirs))


def solution(mesh):
    return jax.shard_map(
        per_device,
        mesh=mesh,
        in_specs=(
            P("gy", "gx"),
            P("gx"),
            P("gx", "gy"),
            P("gx", "gy"),
            P("gy", "gx"),
            P(("gx", "gy"), None, None),
            P(("gx", "gy"), None, None),
            P(("gx", "gy")),
        ),
        out_specs=P("gy", "gx"),
        check_vma=False,
    )
```

```python
import functools

import jax
import jax.numpy as jnp
from jax import lax
from jax.experimental import pallas as pl
from jax.experimental.pallas import tpu as pltpu
from jax.sharding import PartitionSpec as P

D = 18432
HD = 256
GROUP = 2
STEPS = 2
VMEM = pl.BlockSpec(memory_space=pltpu.VMEM)
SMEM = pl.BlockSpec(memory_space=pltpu.SMEM)
ANY = pl.BlockSpec(memory_space=pl.ANY)
F32 = jnp.float32
BF16 = jnp.bfloat16


def params(mib):
    return pltpu.CompilerParams(vmem_limit_bytes=mib * 1024 * 1024)


def cost(flops, size):
    return pl.CostEstimate(flops=int(flops), bytes_accessed=int(size), transcendentals=0)


def exchange_pairs(core_along_y, m):
    pairs = []
    for d in range(128):
        far = 32 * m if d % 2 == core_along_y else 8 * m
        pairs.append((d, d ^ far))
    return pairs


def along_first(value, m):
    return lax.ppermute(value, ("gx", "gy"), exchange_pairs(0, m))


def along_second(value, m):
    return lax.ppermute(value, ("gx", "gy"), exchange_pairs(1, m))


def along_x(value, m):
    return lax.ppermute(value, "gy", [(g, g ^ (2 * m)) for g in range(8)])


def other_core(value):
    return lax.ppermute(value, "gy", [(g, g ^ 1) for g in range(8)])


ORDER = (0, 2, 1, 3)


def exchanged(along, parts, order=ORDER):
    return [along(parts[m], m) if m else parts[0] for m in order]


def groups_of(rows, first):
    groups = [rows[at + first : at + first + 8] for at in range(0, rows.shape[0], 16)]
    return jnp.concatenate(groups, axis=0)


def prepare_kernel(place, tokens, theirs, stats, piece):
    rows, others = tokens[...].astype(F32), theirs[...].astype(F32)
    by_core = [groups_of(rows, 0), groups_of(rows, 8)]
    swap = place[3] == 1
    piece[:64] = jnp.where(swap, by_core[1], by_core[0]).astype(BF16)
    piece[64:] = jnp.where(swap, groups_of(others, 8), groups_of(others, 0)).astype(BF16)
    lines = []
    for power in range(2):
        sums = [
            jnp.sum(part if power == 0 else part * part, axis=1, keepdims=True) for part in by_core
        ]
        column = jnp.broadcast_to(jnp.concatenate(sums, axis=0), (128, 128))
        lines.append(column.T[0:1])
    line = jnp.concatenate(lines, axis=1)
    stats[...] = jnp.broadcast_to(line[:, None, :], stats.shape)


def prepare(place, tokens, theirs):
    return pl.pallas_call(
        prepare_kernel,
        out_shape=[
            jax.ShapeDtypeStruct((128, 1, 256), F32),
            jax.ShapeDtypeStruct(tokens.shape, BF16),
        ],
        in_specs=[SMEM, VMEM, VMEM],
        out_specs=[VMEM] * 2,
        compiler_params=params(8),
        cost_estimate=cost(1e8, 1e6),
        name="prepare",
    )(place, tokens, theirs)


def load_tiles(source, tiles, sems, at):
    loads = []
    wide = tiles.shape[2]
    for t in range(source.shape[1] // wide):
        load = pltpu.make_async_copy(
            source.at[:, pl.ds(t * wide, wide)], tiles.at[at + t], sems.at[at + t]
        )
        load.start()
        loads.append(load)
    return loads


def fill_left(blocks, place, gain, pieces, left):
    y, z, x, c = place[0], place[1], place[2], place[3]
    gains = gain[...].astype(F32)
    along_y = c == 0
    for m, piece in zip(ORDER, pieces):
        to_y = x ^ m ^ y
        for j in range(2):
            for b in range(2):
                to_z = ((c ^ j) * 2 + b) ^ z
                first = jnp.where(along_y, to_y, to_z)
                second = jnp.where(along_y, to_z, to_y)

                @pl.when((first == blocks[0]) | (first == blocks[1]))
                def _():
                    at = j * 64 + b * 32
                    rows = piece[at : at + 32, :].astype(F32)
                    rows = rows - jnp.sum(rows, axis=1, keepdims=True) / rows.shape[1]
                    slot = jnp.where(first == blocks[0], 0, 4) + second
                    left[pl.ds(pl.multiple_of(slot * 32, 32), 32)] = (rows * gains).astype(BF16)


def multiply(left, tiles, loads, pairs, put):
    wide = tiles.shape[2]
    width = tiles.shape[0] * wide
    pair = jnp.concatenate([pairs[0][...], pairs[1][...]], axis=0)
    dims = (((1,), (1,)), ((), ()))
    put(lax.dot_general(left[...], pair, dims, preferred_element_type=F32), width, pair.shape[0])
    for t, load in enumerate(loads):
        load.wait()
        put(jnp.dot(left[...], tiles[t], preferred_element_type=F32), t * wide, wide)


def load_both(weights, tiles, sems):
    count = tiles.shape[0] // 2
    return load_tiles(weights[0], tiles, sems, 0) + load_tiles(weights[1], tiles, sems, count)


def project_kernel(blocks, place, gain, *refs):
    pieces, weights, pairs = refs[:4], refs[4:6], refs[6:8]
    out, gain_row, left, tiles, sems = refs[8:]
    loads = load_both(weights, tiles, sems)
    left[256:] = jnp.broadcast_to(gain[...], (16, gain.shape[1]))
    fill_left(blocks, place, gain, pieces, left)

    def put(part, at, size):
        out[:, at : at + size] = part[:256].astype(BF16)
        gain_row[:, at : at + size] = part[256:264]

    multiply(left, tiles, loads, pairs, put)


def project_scratch(rows, weights):
    depth, width = weights[0].shape
    count = 2 * width // 512
    return [
        pltpu.VMEM((rows, depth), BF16),
        pltpu.VMEM((count, depth, 512), BF16),
        pltpu.SemaphoreType.DMA((count,)),
    ]


def project(blocks, place, gain, pieces, weights, pairs):
    total = 2 * (weights[0].shape[1] + pairs[0].shape[0])
    return pl.pallas_call(
        functools.partial(project_kernel, blocks),
        out_shape=[
            jax.ShapeDtypeStruct((256, total), BF16),
            jax.ShapeDtypeStruct((8, total), F32),
        ],
        in_specs=[SMEM] + [VMEM] * 5 + [ANY] * 2 + [VMEM] * 2,
        out_specs=[VMEM] * 2,
        scratch_shapes=project_scratch(272, weights),
        compiler_params=params(48),
        cost_estimate=cost(4e9, 1e7),
        name="project",
    )(place, gain, *pieces, *weights, *pairs)


def fill_columns(place, stats, shift_of, scale_of):
    y, z = place[0], place[1]
    total = stats[0:8, :]
    for g in range(1, 16):
        total = total + stats[g * 8 : g * 8 + 8, :]
    mean = total[:, :128] / D
    variance = total[:, 128:] / D - mean * mean
    here = stats[pl.ds(pl.multiple_of((y * 4 + z) * 8, 8), 8), :]
    shift_columns = (here[:, :128] / (D // 16) - mean).T
    scale_columns = lax.rsqrt(variance + 1e-05).T
    for s in range(8):
        shift_of[s] = shift_columns[:, s : s + 1]
        scale_of[s] = scale_columns[:, s : s + 1]


def columns_of(place, block, second):
    y, z, c = place[0], place[1], place[3]
    token_y = y ^ jnp.where(c == 0, block, second)
    token_z = z ^ jnp.where(c == 0, second, block)
    rows = pl.ds(pl.multiple_of(c * 64 + token_z % 2 * 32, 32), 32)
    return token_y * 2 + token_z // 2, rows


def scale_kernel(blocks, place, stats, gain_row, parts, *refs):
    outs, shift_of, scale_of = refs[:2], refs[2], refs[3]
    fill_columns(place, stats, shift_of, scale_of)
    line = gain_row[0:1, :]
    for i, out in enumerate(outs):
        for second in range(4):
            s, at = columns_of(place, blocks[i], second)
            rows = parts[i * 128 + second * 32 : i * 128 + second * 32 + 32, :]
            rows = (rows.astype(F32) + shift_of[s, at] * line) * scale_of[s, at]
            out[second * 32 : second * 32 + 32, :] = rows.astype(BF16)


def scale(blocks, place, stats, gain_row, parts):
    out = jax.ShapeDtypeStruct((128, parts.shape[1]), BF16)
    return pl.pallas_call(
        functools.partial(scale_kernel, blocks),
        out_shape=[out] * 2,
        in_specs=[SMEM] + [VMEM] * 3,
        out_specs=[VMEM] * 2,
        scratch_shapes=[pltpu.VMEM((8, 128, 1), F32)] * 2,
        compiler_params=params(12),
        cost_estimate=cost(1e9, 2e6),
        name="scale",
    )(place, stats, gain_row, parts)


def project_rest_kernel(blocks, place, stats, gain_row, gain, *refs):
    pieces, weights, pairs = refs[:4], refs[4:6], refs[6:8]
    outs, (left, tiles, sems, shift_of, scale_of, shift, factor) = refs[8:10], refs[10:]
    loads = load_both(weights, tiles, sems)
    fill_columns(place, stats, shift_of, scale_of)
    for k in range(8):
        s, at = columns_of(place, blocks[k // 4], k % 4)
        shift[k * 32 : k * 32 + 32] = shift_of[s, at]
        factor[k * 32 : k * 32 + 32] = scale_of[s, at]
    fill_left(blocks, place, gain, pieces, left)

    def put(part, at, size):
        line = gain_row[0:1, at : at + size]
        part = ((part + shift[...] * line) * factor[...]).astype(BF16)
        for i, out in enumerate(outs):
            out[:, at : at + size] = part[i * 128 : i * 128 + 128]

    multiply(left, tiles, loads, pairs, put)


def project_rest(blocks, place, stats, gain_row, gain, pieces, weights, pairs):
    out = jax.ShapeDtypeStruct((128, gain_row.shape[1]), BF16)
    return pl.pallas_call(
        functools.partial(project_rest_kernel, blocks),
        out_shape=[out] * 2,
        in_specs=[SMEM] + [VMEM] * 7 + [ANY] * 2 + [VMEM] * 2,
        out_specs=[VMEM] * 2,
        scratch_shapes=project_scratch(256, weights)
        + [pltpu.VMEM((8, 128, 1), F32)] * 2
        + [pltpu.VMEM((256, 1), F32)] * 2,
        compiler_params=params(48),
        cost_estimate=cost(5e9, 1e7),
        name="project_rest",
    )(place, stats, gain_row, gain, *pieces, *weights, *pairs)


def sum_of(refs):
    total = refs[0][...].astype(F32)
    for ref in refs[1:]:
        total = total + ref[...].astype(F32)
    return total


def add_and_cut_kernel(*refs):
    total = sum_of(refs[:4]).astype(BF16)
    rows = total.shape[0] // 4
    for k in range(4):
        refs[4 + k][...] = total[k * rows : k * rows + rows]


def add_and_cut(values):
    rows, width = values[0].shape
    out = jax.ShapeDtypeStruct((rows // 4, width), BF16)
    return pl.pallas_call(
        add_and_cut_kernel,
        out_shape=[out] * 4,
        in_specs=[VMEM] * 4,
        out_specs=[VMEM] * 4,
        compiler_params=params(12),
        cost_estimate=cost(1e8, 1e6),
        name="add_and_cut",
    )(*values)


def finish_kernel(place, *refs):
    ins, outs, blocks = refs[:4], refs[4:8], refs[8]
    total = sum_of(ins)
    for i in range(4):
        blocks[place[2] ^ i] = total[i * 8 : i * 8 + 8]
    for m in range(4):
        outs[m][...] = blocks[m].astype(BF16)


def finish(place, values):
    rows, width = values[0].shape
    out = jax.ShapeDtypeStruct((rows // 4, width), BF16)
    return pl.pallas_call(
        finish_kernel,
        out_shape=[out] * 4,
        in_specs=[SMEM] + [VMEM] * 4,
        out_specs=[VMEM] * 4,
        scratch_shapes=[pltpu.VMEM((4, rows // 4, width), F32)],
        compiler_params=params(8),
        cost_estimate=cost(1e8, 1e6),
        name="finish",
    )(place, *values)


def line_up_kernel(place, *refs):
    ins, out, blocks = refs[:4], refs[4], refs[5]
    for m, rows in zip(ORDER, ins):
        blocks[place[2] ^ m] = rows[...].astype(F32)
    out[...] = blocks[...].reshape(out.shape).astype(BF16)


def line_up(place, values):
    rows, width = values[0].shape
    return pl.pallas_call(
        line_up_kernel,
        out_shape=jax.ShapeDtypeStruct((4 * rows, width), BF16),
        in_specs=[SMEM] + [VMEM] * 4,
        out_specs=VMEM,
        scratch_shapes=[pltpu.VMEM((4, rows, width), F32)],
        compiler_params=params(8),
        cost_estimate=cost(1e8, 1e6),
        name="line_up",
    )(place, *values)


def attend_one(request, lengths, keys, values, count, query_rows, new_kv, result):
    per = STEPS * count
    start = pl.multiple_of(request * per, per)
    query = jnp.concatenate([query_rows[i, pl.ds(start, per), :] for i in range(2)], axis=-1)
    query = (query.astype(BF16).astype(F32) * HD ** (-0.5)).astype(BF16)
    dims = (((1,), (1,)), ((), ()))
    cached = lax.dot_general(query, keys[...], dims, preferred_element_type=F32)
    slots = lax.broadcasted_iota(jnp.int32, cached.shape, 1)
    cached = jnp.where(slots < lengths[request], cached, -jnp.inf)
    fresh = lax.dot_general(query, new_kv[0], dims, preferred_element_type=F32)
    row_step = lax.broadcasted_iota(jnp.int32, fresh.shape, 0) // count
    key_step = lax.broadcasted_iota(jnp.int32, fresh.shape, 1) - request * STEPS
    fresh = jnp.where((key_step >= 0) & (key_step <= row_step), fresh, -jnp.inf)
    top = jnp.maximum(
        jnp.max(cached, axis=-1, keepdims=True), jnp.max(fresh, axis=-1, keepdims=True)
    )
    cached = jnp.exp(cached - top)
    fresh = jnp.exp(fresh - top)
    denom = jnp.sum(cached, axis=-1, keepdims=True) + jnp.sum(fresh, axis=-1, keepdims=True)
    mixed = jnp.dot(cached.astype(BF16), values[...], preferred_element_type=F32)
    mixed = mixed + jnp.dot(fresh.astype(BF16), new_kv[1], preferred_element_type=F32)
    mixed = mixed / denom
    for i in range(2):
        result[i, pl.ds(start, per), :] = mixed[:, i * 128 : i * 128 + 128]


def attend_kernel(lengths, place, *refs):
    packed, (cosine, sine, keys, values), outs = refs[:4], refs[4:8], refs[8:12]
    query_rows, new_pieces, new_kv, result = refs[12:]
    request = pl.program_id(0)
    width = outs[0].shape[1]
    heads = width // HD
    count = 4 * heads

    @pl.when(request == 0)
    def _():
        x, c = place[2], place[3]
        cos, sin = cosine[...], sine[...]

        def rotated(first, second):
            return first * cos - second * sin, second * cos + first * sin

        for m, rows in zip(ORDER, packed):
            rows = rows[...].astype(F32)
            for h in range(heads):
                head = rows[:, h * HD : h * HD + HD]
                for i, half in enumerate(rotated(head[:, :128], head[:, 128:])):
                    query_rows[i, pl.ds(m * heads + h, 8, stride=count), :] = half
            size = (rows.shape[1] - width) // 2
            for j in range(2):
                at = width + j * size
                new_pieces[(x ^ m) * 2 + (c ^ j)] = rows[:, at : at + size]
        halves = [
            jnp.concatenate([new_pieces[i], new_pieces[i + 1]], axis=-1) for i in range(0, 8, 2)
        ]
        new_kv[0] = jnp.concatenate(rotated(halves[0], halves[1]), axis=-1).astype(BF16)
        new_kv[1] = jnp.concatenate(halves[2:], axis=-1).astype(BF16)

    for i in range(keys.shape[0]):
        attend_one(request * keys.shape[0] + i, lengths, keys.at[i], values.at[i], count, query_rows, new_kv, result)

    @pl.when(request == pl.num_programs(0) - 1)
    def _():
        for m, out in enumerate(outs):
            halves = [
                result[i, pl.ds(m * heads + h, 8, stride=count), :]
                for h in range(heads)
                for i in range(2)
            ]
            out[...] = jnp.concatenate(halves, axis=-1).astype(BF16)


def attend(place, packed, cosine, sine, cache_keys, cache_values, lengths, width):
    requests, slots, _ = cache_keys.shape
    total = packed[0].shape[1]
    count = 4 * (width // HD)
    whole = lambda *shape: pl.BlockSpec(shape, lambda r, *_: (0,) * len(shape))
    cache = pl.BlockSpec((GROUP, slots, HD), lambda r, *_: (r, 0, 0))
    return pl.pallas_call(
        attend_kernel,
        out_shape=[jax.ShapeDtypeStruct((8, width), BF16)] * 4,
        grid_spec=pltpu.PrefetchScalarGridSpec(
            num_scalar_prefetch=2,
            grid=(requests // GROUP,),
            in_specs=[whole(8, total)] * 4 + [whole(8, 128)] * 2 + [cache] * 2,
            out_specs=[whole(8, width)] * 4,
            scratch_shapes=[
                pltpu.VMEM((2, 8 * count, 128), F32),
                pltpu.VMEM((8, 8, (total - width) // 2), F32),
                pltpu.VMEM((2, 8, HD), BF16),
                pltpu.VMEM((2, 8 * count, 128), F32),
            ],
        ),
        compiler_params=params(52),
        cost_estimate=cost(6e9, 1.8e7),
        name="attend",
    )(lengths, place, *packed, cosine, sine, cache_keys, cache_values)


def multiply_rows(lefts, tiles, loads, put):
    left = jnp.concatenate([ref[...] for ref in lefts], axis=0)
    depth = left.shape[1] // 2
    count = tiles.shape[0] // 2
    wide = tiles.shape[2]
    for t in range(count):
        loads[t].wait()
        part = jnp.dot(left[:, :depth], tiles[t], preferred_element_type=F32)
        loads[count + t].wait()
        part = part + jnp.dot(left[:, depth:], tiles[count + t], preferred_element_type=F32)
        put(part.astype(BF16), t * wide, wide)


def mix_kernel(*refs):
    lefts, weights, out, tiles, sems = refs[:3], refs[3:5], refs[5], refs[6], refs[7]
    loads = load_tiles(weights[0], tiles, sems, 0) + load_tiles(weights[1], tiles, sems, 3)

    def put(part, at, size):
        out[:, at : at + size] = part

    multiply_rows(lefts, tiles, loads, put)


def mix_rest_kernel(place, done, last, *refs):
    weights, outs = refs[:2], refs[2:6]
    result, tiles, sems = refs[6:]
    loads = load_tiles(weights[0], tiles, sems, 0) + load_tiles(weights[1], tiles, sems, 3)
    y, z, x, c = place[0], place[1], place[2], place[3]
    along_y = c == 0

    def slots(second, first):
        to_x = y ^ x ^ jnp.where(along_y, first, second)
        token_z = z ^ jnp.where(along_y, second, first)
        return to_x, (token_z // 2 ^ c) * 2 + token_z % 2

    for k in range(12):
        result[slots((0, 1, 3)[k // 4], ORDER[k % 4])] = done[k * 32 : k * 32 + 32, :]

    def put(part, at, size):
        for k in range(4):
            to_x, slot = slots(2, ORDER[k])
            result[to_x, slot, :, at : at + size] = part[k * 32 : k * 32 + 32]

    multiply_rows([last], tiles, loads, put)
    for k, out in enumerate(outs):
        out[...] = result[k].reshape(out.shape)


def mix_scratch(depth, width):
    return [pltpu.VMEM((6, depth, width // 3), BF16), pltpu.SemaphoreType.DMA((6,))]


def mix(lefts, weights):
    depth, width = weights[0].shape
    return pl.pallas_call(
        mix_kernel,
        out_shape=jax.ShapeDtypeStruct((384, width), BF16),
        in_specs=[VMEM] * 3 + [ANY] * 2,
        out_specs=VMEM,
        scratch_shapes=mix_scratch(depth, width),
        compiler_params=params(24),
        cost_estimate=cost(4e9, 8e6),
        name="mix",
    )(*lefts, *weights)


def mix_rest(place, done, last, weights):
    depth, width = weights[0].shape
    return pl.pallas_call(
        mix_rest_kernel,
        out_shape=[jax.ShapeDtypeStruct((128, width), BF16)] * 4,
        in_specs=[SMEM] + [VMEM] * 2 + [ANY] * 2,
        out_specs=[VMEM] * 4,
        scratch_shapes=[pltpu.VMEM((4, 4, 32, width), BF16)] + mix_scratch(depth, width),
        compiler_params=params(24),
        cost_estimate=cost(4e9, 8e6),
        name="mix_rest",
    )(place, done, last, *weights)


def last_sum_kernel(*refs):
    total = sum_of(refs[:4]).astype(BF16)
    refs[4][...] = total[:64]
    refs[5][...] = total[64:]


def last_sum(values):
    half = jax.ShapeDtypeStruct((64, values[0].shape[1]), BF16)
    return pl.pallas_call(
        last_sum_kernel,
        out_shape=[half] * 2,
        in_specs=[VMEM] * 4,
        out_specs=[VMEM] * 2,
        compiler_params=params(8),
        cost_estimate=cost(1e8, 1e6),
        name="last_sum",
    )(*values)


def interleave_kernel(place, mine, theirs, out):
    first, second = mine[...].astype(F32), theirs[...].astype(F32)
    swap = place[3] == 1
    first, second = jnp.where(swap, second, first), jnp.where(swap, first, second)
    groups = []
    for i in range(8):
        groups += [first[i * 8 : i * 8 + 8], second[i * 8 : i * 8 + 8]]
    out[...] = jnp.concatenate(groups, axis=0).astype(BF16)


def interleave(place, mine, theirs):
    rows, width = mine.shape
    return pl.pallas_call(
        interleave_kernel,
        out_shape=jax.ShapeDtypeStruct((2 * rows, width), BF16),
        in_specs=[SMEM] + [VMEM] * 2,
        out_specs=VMEM,
        compiler_params=params(8),
        cost_estimate=cost(1e8, 1e6),
        name="interleave",
    )(place, mine, theirs)


def per_device(tokens, norm_gain, w_query, w_keyvalue, w_out, cache_keys, cache_values, lengths):
    gx, gy = lax.axis_index("gx"), lax.axis_index("gy")
    place = jnp.stack([gx // 4, gx % 4, gy // 2, gy % 2]).astype(jnp.int32)

    stats, piece = prepare(place, tokens, other_core(tokens))
    pieces = exchanged(along_x, [piece] * 4)
    stats = lax.all_to_all(stats, ("gx", "gy"), 0, 0, tiled=True)
    w_pair = w_keyvalue.T
    w_query, w_pair, piece = lax.optimization_barrier((w_query, w_pair, piece))
    weights, pairs = [w_query, other_core(w_query)], [w_pair, other_core(w_pair)]
    gain = norm_gain[None]
    parts, gain_row = project((1, 3), place, gain, pieces, weights, pairs)
    parts, stats = lax.optimization_barrier((parts, stats))
    stats = stats.reshape(128, 256)
    sent = scale((1, 3), place, stats, gain_row, parts)
    kept = project_rest((2, 0), place, stats, gain_row, gain, pieces, weights, pairs)
    parts = [kept[1], sent[0], kept[0], sent[1]]

    parts = add_and_cut(exchanged(along_first, parts))
    parts = finish(place, exchanged(along_second, parts, range(4)))
    packed = exchanged(along_x, parts)

    half_dim = HD // 2
    freqs = 10000.0 ** (-jnp.arange(half_dim, dtype=F32) / half_dim)
    positions = lengths[:, None] + jnp.arange(STEPS, dtype=jnp.int32)[None, :]
    angles = positions.reshape(-1).astype(F32)[:, None] * freqs
    attended = attend(
        place,
        packed,
        jnp.cos(angles),
        jnp.sin(angles),
        cache_keys,
        cache_values,
        lengths,
        2 * w_query.shape[1],
    )

    rows = line_up(place, exchanged(along_x, attended))
    rows = jnp.concatenate(exchanged(along_first, [rows] * 4), axis=0)
    near = [along_second(rows, 1), along_second(rows, 3)]
    late, *near = lax.optimization_barrier((rows, *near))
    blocks = [rows, near[0], along_second(late, 2), near[1]]
    weights = [w_out, other_core(w_out)]
    done = mix([blocks[0], blocks[1], blocks[3]], weights)
    parts = mix_rest(place, done, blocks[2], weights)
    mine, theirs = last_sum(exchanged(along_x, parts))
    return interleave(place, mine, other_core(theirs))


def solution(mesh):
    return jax.shard_map(
        per_device,
        mesh=mesh,
        in_specs=(
            P("gy", "gx"),
            P("gx"),
            P("gx", "gy"),
            P("gx", "gy"),
            P("gy", "gx"),
            P(("gx", "gy"), None, None),
            P(("gx", "gy"), None, None),
            P(("gx", "gy")),
        ),
        out_specs=P("gy", "gx"),
        check_vma=False,
    )
```

```python
import functools

import jax
import jax.numpy as jnp
from jax import lax
from jax.experimental import pallas as pl
from jax.experimental.pallas import tpu as pltpu
from jax.sharding import PartitionSpec as P

D = 18432
HD = 256
GROUP = 2
STEPS = 2
VMEM = pl.BlockSpec(memory_space=pltpu.VMEM)
SMEM = pl.BlockSpec(memory_space=pltpu.SMEM)
ANY = pl.BlockSpec(memory_space=pl.ANY)
F32 = jnp.float32
BF16 = jnp.bfloat16


def params(mib):
    return pltpu.CompilerParams(vmem_limit_bytes=mib * 1024 * 1024)


def cost(flops, size):
    return pl.CostEstimate(flops=int(flops), bytes_accessed=int(size), transcendentals=0)


def exchange_pairs(core_along_y, m):
    pairs = []
    for d in range(128):
        far = 32 * m if d % 2 == core_along_y else 8 * m
        pairs.append((d, d ^ far))
    return pairs


def along_first(value, m):
    return lax.ppermute(value, ("gx", "gy"), exchange_pairs(0, m))


def along_second(value, m):
    return lax.ppermute(value, ("gx", "gy"), exchange_pairs(1, m))


def along_x(value, m):
    return lax.ppermute(value, "gy", [(g, g ^ (2 * m)) for g in range(8)])


def other_core(value):
    return lax.ppermute(value, "gy", [(g, g ^ 1) for g in range(8)])


ORDER = (0, 2, 1, 3)


def exchanged(along, parts, order=ORDER):
    return [along(parts[m], m) if m else parts[0] for m in order]


def groups_of(rows, first):
    groups = [rows[at + first : at + first + 8] for at in range(0, rows.shape[0], 16)]
    return jnp.concatenate(groups, axis=0)


def prepare_kernel(tokens, stats, copy):
    copy[...] = tokens[...]
    rows = tokens[...].astype(F32)
    by_core = [groups_of(rows, 0), groups_of(rows, 8)]
    lines = []
    for power in range(2):
        sums = [
            jnp.sum(part if power == 0 else part * part, axis=1, keepdims=True) for part in by_core
        ]
        column = jnp.broadcast_to(jnp.concatenate(sums, axis=0), (128, 128))
        lines.append(column.T[0:1])
    line = jnp.concatenate(lines, axis=1)
    stats[...] = jnp.broadcast_to(line[:, None, :], stats.shape)


def prepare(tokens):
    return pl.pallas_call(
        prepare_kernel,
        out_shape=[
            jax.ShapeDtypeStruct((128, 1, 256), F32),
            jax.ShapeDtypeStruct(tokens.shape, tokens.dtype),
        ],
        in_specs=[VMEM],
        out_specs=[VMEM] * 2,
        compiler_params=params(8),
        cost_estimate=cost(1e8, 1e6),
        name="prepare",
    )(tokens)


def load_tiles(source, tiles, sems, at):
    loads = []
    wide = tiles.shape[2]
    for t in range(source.shape[1] // wide):
        load = pltpu.make_async_copy(
            source.at[:, pl.ds(t * wide, wide)], tiles.at[at + t], sems.at[at + t]
        )
        load.start()
        loads.append(load)
    return loads


def fill_left(place, gain, pieces, left):
    y, z, x, c = place[0], place[1], place[2], place[3]
    gains = gain[...].astype(F32)
    left[256:272] = jnp.broadcast_to(gain[...], (16, gain.shape[1]))
    along_y = c == 0
    for i, m in enumerate(ORDER):
        to_y = x ^ m ^ y
        for j in range(2):
            rows = pieces[j * 4 + i][...].astype(F32)
            rows = jnp.where(along_y, groups_of(rows, 0), groups_of(rows, 8))
            rows = rows - jnp.sum(rows, axis=1, keepdims=True) / rows.shape[1]
            rows = (rows * gains).astype(BF16)
            for b in range(2):
                to_z = ((c ^ j) * 2 + b) ^ z
                first = jnp.where(along_y, to_y, to_z)
                second = jnp.where(along_y, to_z, to_y)
                at = jnp.where(first % 2 == 1, first // 2 * 128, 400 - first // 2 * 128)
                at = pl.multiple_of(at + second * 32, 16)
                left[pl.ds(at, 32)] = rows[b * 32 : b * 32 + 32]


def multiply(left, tiles, loads, pairs, put):
    wide = tiles.shape[2]
    width = tiles.shape[0] * wide
    dims = (((1,), (1,)), ((), ()))
    part = lax.dot_general(left, pairs[...], dims, preferred_element_type=F32)
    put(part, width, pairs.shape[0])
    for t, load in enumerate(loads):
        load.wait()
        put(jnp.dot(left, tiles[t], preferred_element_type=F32), t * wide, wide)


def load_both(weights, tiles, sems):
    count = tiles.shape[0] // 2
    return load_tiles(weights[0], tiles, sems, 0) + load_tiles(weights[1], tiles, sems, count)


def project_kernel(place, gain, *refs):
    pieces, weights, pairs = refs[:8], refs[8:10], refs[10]
    out, gain_row, rest, left, tiles, sems = refs[11:]
    loads = load_both(weights, tiles, sems)
    fill_left(place, gain, pieces, left)
    rest[...] = left[272:]

    def put(part, at, size):
        out[:, at : at + size] = part[:256].astype(BF16)
        gain_row[:, at : at + size] = part[256:264]

    multiply(left[:272], tiles, loads, pairs, put)


def project_scratch(weights):
    depth, width = weights[0].shape
    count = 2 * width // 512
    return [
        pltpu.VMEM((count, depth, 512), BF16),
        pltpu.SemaphoreType.DMA((count,)),
    ]


def project(place, gain, pieces, weights, pairs):
    depth = weights[0].shape[0]
    total = 2 * weights[0].shape[1] + pairs.shape[0]
    return pl.pallas_call(
        project_kernel,
        out_shape=[
            jax.ShapeDtypeStruct((256, total), BF16),
            jax.ShapeDtypeStruct((8, total), F32),
            jax.ShapeDtypeStruct((256, depth), BF16),
        ],
        in_specs=[SMEM] + [VMEM] * 9 + [ANY] * 2 + [VMEM],
        out_specs=[VMEM] * 3,
        scratch_shapes=[pltpu.VMEM((528, depth), BF16)] + project_scratch(weights),
        compiler_params=params(48),
        cost_estimate=cost(4e9, 1e7),
        name="project",
    )(place, gain, *pieces, *weights, pairs)


def fill_columns(place, stats, shift_of, scale_of):
    y, z = place[0], place[1]
    total = stats[0:8, :]
    for g in range(1, 16):
        total = total + stats[g * 8 : g * 8 + 8, :]
    mean = total[:, :128] / D
    variance = total[:, 128:] / D - mean * mean
    here = stats[pl.ds(pl.multiple_of((y * 4 + z) * 8, 8), 8), :]
    shift_columns = (here[:, :128] / (D // 16) - mean).T
    scale_columns = lax.rsqrt(variance + 1e-05).T
    for s in range(8):
        shift_of[s] = shift_columns[:, s : s + 1]
        scale_of[s] = scale_columns[:, s : s + 1]


def columns_of(place, block, second):
    y, z, c = place[0], place[1], place[3]
    token_y = y ^ jnp.where(c == 0, block, second)
    token_z = z ^ jnp.where(c == 0, second, block)
    rows = pl.ds(pl.multiple_of(c * 64 + token_z % 2 * 32, 32), 32)
    return token_y * 2 + token_z // 2, rows


def scale_kernel(blocks, place, stats, gain_row, parts, *refs):
    outs, shift_of, scale_of = refs[:2], refs[2], refs[3]
    fill_columns(place, stats, shift_of, scale_of)
    line = gain_row[0:1, :]
    for i, out in enumerate(outs):
        for second in range(4):
            s, at = columns_of(place, blocks[i], second)
            rows = parts[i * 128 + second * 32 : i * 128 + second * 32 + 32, :]
            rows = (rows.astype(F32) + shift_of[s, at] * line) * scale_of[s, at]
            out[second * 32 : second * 32 + 32, :] = rows.astype(BF16)


def scale(blocks, place, stats, gain_row, parts):
    out = jax.ShapeDtypeStruct((128, parts.shape[1]), BF16)
    return pl.pallas_call(
        functools.partial(scale_kernel, blocks),
        out_shape=[out] * 2,
        in_specs=[SMEM] + [VMEM] * 3,
        out_specs=[VMEM] * 2,
        scratch_shapes=[pltpu.VMEM((8, 128, 1), F32)] * 2,
        compiler_params=params(12),
        cost_estimate=cost(1e9, 2e6),
        name="scale",
    )(place, stats, gain_row, parts)


def project_rest_kernel(blocks, place, stats, gain_row, left, *refs):
    weights, pairs, outs = refs[:2], refs[2], refs[3:5]
    tiles, sems, shift_of, scale_of, shift, factor = refs[5:]
    loads = load_both(weights, tiles, sems)
    fill_columns(place, stats, shift_of, scale_of)
    for k in range(8):
        s, at = columns_of(place, blocks[k // 4], k % 4)
        shift[k * 32 : k * 32 + 32] = shift_of[s, at]
        factor[k * 32 : k * 32 + 32] = scale_of[s, at]

    def put(part, at, size):
        line = gain_row[0:1, at : at + size]
        part = ((part + shift[...] * line) * factor[...]).astype(BF16)
        for i, out in enumerate(outs):
            out[:, at : at + size] = part[i * 128 : i * 128 + 128]

    multiply(left[...], tiles, loads, pairs, put)


def project_rest(blocks, place, stats, gain_row, left, weights, pairs):
    out = jax.ShapeDtypeStruct((128, gain_row.shape[1]), BF16)
    return pl.pallas_call(
        functools.partial(project_rest_kernel, blocks),
        out_shape=[out] * 2,
        in_specs=[SMEM] + [VMEM] * 3 + [ANY] * 2 + [VMEM],
        out_specs=[VMEM] * 2,
        scratch_shapes=project_scratch(weights)
        + [pltpu.VMEM((8, 128, 1), F32)] * 2
        + [pltpu.VMEM((256, 1), F32)] * 2,
        compiler_params=params(48),
        cost_estimate=cost(5e9, 1e7),
        name="project_rest",
    )(place, stats, gain_row, left, *weights, pairs)


def sum_of(refs):
    total = refs[0][...].astype(F32)
    for ref in refs[1:]:
        total = total + ref[...].astype(F32)
    return total


def add_and_cut_kernel(*refs):
    total = sum_of(refs[:4]).astype(BF16)
    rows = total.shape[0] // 4
    for k in range(4):
        refs[4 + k][...] = total[k * rows : k * rows + rows]


def add_and_cut(values):
    rows, width = values[0].shape
    out = jax.ShapeDtypeStruct((rows // 4, width), BF16)
    return pl.pallas_call(
        add_and_cut_kernel,
        out_shape=[out] * 4,
        in_specs=[VMEM] * 4,
        out_specs=[VMEM] * 4,
        compiler_params=params(12),
        cost_estimate=cost(1e8, 1e6),
        name="add_and_cut",
    )(*values)


def finish_kernel(place, *refs):
    ins, outs, blocks = refs[:4], refs[4:8], refs[8]
    total = sum_of(ins)
    for i in range(4):
        blocks[place[2] ^ i] = total[i * 8 : i * 8 + 8]
    for m in range(4):
        outs[m][...] = blocks[m].astype(BF16)


def finish(place, values):
    rows, width = values[0].shape
    out = jax.ShapeDtypeStruct((rows // 4, width), BF16)
    return pl.pallas_call(
        finish_kernel,
        out_shape=[out] * 4,
        in_specs=[SMEM] + [VMEM] * 4,
        out_specs=[VMEM] * 4,
        scratch_shapes=[pltpu.VMEM((4, rows // 4, width), F32)],
        compiler_params=params(8),
        cost_estimate=cost(1e8, 1e6),
        name="finish",
    )(place, *values)


def line_up_kernel(place, *refs):
    ins, out, blocks = refs[:4], refs[4], refs[5]
    for m, rows in zip(ORDER, ins):
        blocks[place[2] ^ m] = rows[...].astype(F32)
    out[...] = blocks[...].reshape(out.shape).astype(BF16)


def line_up(place, values):
    rows, width = values[0].shape
    return pl.pallas_call(
        line_up_kernel,
        out_shape=jax.ShapeDtypeStruct((4 * rows, width), BF16),
        in_specs=[SMEM] + [VMEM] * 4,
        out_specs=VMEM,
        scratch_shapes=[pltpu.VMEM((4, rows, width), F32)],
        compiler_params=params(8),
        cost_estimate=cost(1e8, 1e6),
        name="line_up",
    )(place, *values)


def attend_one(request, lengths, keys, values, count, query_rows, new_kv, result):
    per = STEPS * count
    start = pl.multiple_of(request * per, per)
    query = jnp.concatenate([query_rows[i, pl.ds(start, per), :] for i in range(2)], axis=-1)
    query = (query.astype(BF16).astype(F32) * HD ** (-0.5)).astype(BF16)
    dims = (((1,), (1,)), ((), ()))
    cached = lax.dot_general(query, keys[...], dims, preferred_element_type=F32)
    slots = lax.broadcasted_iota(jnp.int32, cached.shape, 1)
    cached = jnp.where(slots < lengths[request], cached, -jnp.inf)
    fresh = lax.dot_general(query, new_kv[0], dims, preferred_element_type=F32)
    row_step = lax.broadcasted_iota(jnp.int32, fresh.shape, 0) // count
    key_step = lax.broadcasted_iota(jnp.int32, fresh.shape, 1) - request * STEPS
    fresh = jnp.where((key_step >= 0) & (key_step <= row_step), fresh, -jnp.inf)
    top = jnp.maximum(
        jnp.max(cached, axis=-1, keepdims=True), jnp.max(fresh, axis=-1, keepdims=True)
    )
    cached = jnp.exp(cached - top)
    fresh = jnp.exp(fresh - top)
    denom = jnp.sum(cached, axis=-1, keepdims=True) + jnp.sum(fresh, axis=-1, keepdims=True)
    mixed = jnp.dot(cached.astype(BF16), values[...], preferred_element_type=F32)
    mixed = mixed + jnp.dot(fresh.astype(BF16), new_kv[1], preferred_element_type=F32)
    mixed = mixed / denom
    for i in range(2):
        result[i, pl.ds(start, per), :] = mixed[:, i * 128 : i * 128 + 128]


def attend_kernel(lengths, place, *refs):
    packed, (cosine, sine, keys, values), outs = refs[:4], refs[4:8], refs[8:12]
    query_rows, new_pieces, new_kv, result = refs[12:]
    request = pl.program_id(0)
    width = outs[0].shape[1]
    heads = width // HD
    count = 4 * heads

    @pl.when(request == 0)
    def _():
        x, c = place[2], place[3]
        cos, sin = cosine[...], sine[...]

        def rotated(first, second):
            return first * cos - second * sin, second * cos + first * sin

        for m, rows in zip(ORDER, packed):
            rows = rows[...].astype(F32)
            for h in range(heads):
                head = rows[:, h * HD : h * HD + HD]
                for i, half in enumerate(rotated(head[:, :128], head[:, 128:])):
                    query_rows[i, pl.ds(m * heads + h, 8, stride=count), :] = half
            size = (rows.shape[1] - width) // 2
            for j in range(2):
                at = width + j * size
                new_pieces[(x ^ m) * 2 + (c ^ j)] = rows[:, at : at + size]
        halves = [
            jnp.concatenate([new_pieces[i], new_pieces[i + 1]], axis=-1) for i in range(0, 8, 2)
        ]
        new_kv[0] = jnp.concatenate(rotated(halves[0], halves[1]), axis=-1).astype(BF16)
        new_kv[1] = jnp.concatenate(halves[2:], axis=-1).astype(BF16)

    for i in range(keys.shape[0]):
        attend_one(request * keys.shape[0] + i, lengths, keys.at[i], values.at[i], count, query_rows, new_kv, result)

    @pl.when(request == pl.num_programs(0) - 1)
    def _():
        for m, out in enumerate(outs):
            halves = [
                result[i, pl.ds(m * heads + h, 8, stride=count), :]
                for h in range(heads)
                for i in range(2)
            ]
            out[...] = jnp.concatenate(halves, axis=-1).astype(BF16)


def attend(place, packed, cosine, sine, cache_keys, cache_values, lengths, width):
    requests, slots, _ = cache_keys.shape
    total = packed[0].shape[1]
    count = 4 * (width // HD)
    whole = lambda *shape: pl.BlockSpec(shape, lambda r, *_: (0,) * len(shape))
    cache = pl.BlockSpec((GROUP, slots, HD), lambda r, *_: (r, 0, 0))
    return pl.pallas_call(
        attend_kernel,
        out_shape=[jax.ShapeDtypeStruct((8, width), BF16)] * 4,
        grid_spec=pltpu.PrefetchScalarGridSpec(
            num_scalar_prefetch=2,
            grid=(requests // GROUP,),
            in_specs=[whole(8, total)] * 4 + [whole(8, 128)] * 2 + [cache] * 2,
            out_specs=[whole(8, width)] * 4,
            scratch_shapes=[
                pltpu.VMEM((2, 8 * count, 128), F32),
                pltpu.VMEM((8, 8, (total - width) // 2), F32),
                pltpu.VMEM((2, 8, HD), BF16),
                pltpu.VMEM((2, 8 * count, 128), F32),
            ],
        ),
        compiler_params=params(52),
        cost_estimate=cost(6e9, 1.8e7),
        name="attend",
    )(lengths, place, *packed, cosine, sine, cache_keys, cache_values)


def multiply_rows(lefts, tiles, put, loads=None):
    left = jnp.concatenate([ref[...] for ref in lefts], axis=0)
    depth = left.shape[1] // 2
    count = tiles.shape[0] // 2
    wide = tiles.shape[2]
    for t in range(count):
        if loads:
            loads[t].wait()
        part = jnp.dot(left[:, :depth], tiles[t], preferred_element_type=F32)
        if loads:
            loads[count + t].wait()
        part = part + jnp.dot(left[:, depth:], tiles[count + t], preferred_element_type=F32)
        put(part.astype(BF16), t * wide, wide)


def mix_kernel(*refs):
    lefts, weights, (out, tiles, sems) = refs[:3], refs[3:5], refs[5:]
    loads = load_tiles(weights[0], tiles, sems, 0) + load_tiles(weights[1], tiles, sems, 3)

    def put(part, at, size):
        out[:, at : at + size] = part

    multiply_rows(lefts, tiles, put, loads)


def mix_rest_kernel(place, done, last, tiles, *refs):
    outs, result = refs[:4], refs[4]
    y, z, x, c = place[0], place[1], place[2], place[3]
    along_y = c == 0

    def slots(second, first):
        to_x = y ^ x ^ jnp.where(along_y, first, second)
        token_z = z ^ jnp.where(along_y, second, first)
        return to_x, (token_z // 2 ^ c) * 2 + token_z % 2

    for k in range(12):
        result[slots((0, 1, 3)[k // 4], ORDER[k % 4])] = done[k * 32 : k * 32 + 32, :]

    def put(part, at, size):
        for k in range(4):
            to_x, slot = slots(2, ORDER[k])
            result[to_x, slot, :, at : at + size] = part[k * 32 : k * 32 + 32]

    multiply_rows([last], tiles, put)
    for k, out in enumerate(outs):
        out[...] = result[k].reshape(out.shape)


def mix(lefts, weights):
    depth, width = weights[0].shape
    return pl.pallas_call(
        mix_kernel,
        out_shape=[
            jax.ShapeDtypeStruct((384, width), BF16),
            jax.ShapeDtypeStruct((6, depth, width // 3), BF16),
        ],
        in_specs=[VMEM] * 3 + [ANY] * 2,
        out_specs=[VMEM] * 2,
        scratch_shapes=[pltpu.SemaphoreType.DMA((6,))],
        compiler_params=params(24),
        cost_estimate=cost(4e9, 8e6),
        name="mix",
    )(*lefts, *weights)


def mix_rest(place, done, last, tiles):
    width = done.shape[1]
    return pl.pallas_call(
        mix_rest_kernel,
        out_shape=[jax.ShapeDtypeStruct((128, width), BF16)] * 4,
        in_specs=[SMEM] + [VMEM] * 3,
        out_specs=[VMEM] * 4,
        scratch_shapes=[pltpu.VMEM((4, 4, 32, width), BF16)],
        compiler_params=params(24),
        cost_estimate=cost(4e9, 8e6),
        name="mix_rest",
    )(place, done, last, tiles)


def last_sum_kernel(*refs):
    total = sum_of(refs[:4]).astype(BF16)
    refs[4][...] = total[:64]
    refs[5][...] = total[64:]


def last_sum(values):
    half = jax.ShapeDtypeStruct((64, values[0].shape[1]), BF16)
    return pl.pallas_call(
        last_sum_kernel,
        out_shape=[half] * 2,
        in_specs=[VMEM] * 4,
        out_specs=[VMEM] * 2,
        compiler_params=params(8),
        cost_estimate=cost(1e8, 1e6),
        name="last_sum",
    )(*values)


def interleave_kernel(place, mine, theirs, out):
    first, second = mine[...].astype(F32), theirs[...].astype(F32)
    swap = place[3] == 1
    first, second = jnp.where(swap, second, first), jnp.where(swap, first, second)
    groups = []
    for i in range(8):
        groups += [first[i * 8 : i * 8 + 8], second[i * 8 : i * 8 + 8]]
    out[...] = jnp.concatenate(groups, axis=0).astype(BF16)


def interleave(place, mine, theirs):
    rows, width = mine.shape
    return pl.pallas_call(
        interleave_kernel,
        out_shape=jax.ShapeDtypeStruct((2 * rows, width), BF16),
        in_specs=[SMEM] + [VMEM] * 2,
        out_specs=VMEM,
        compiler_params=params(8),
        cost_estimate=cost(1e8, 1e6),
        name="interleave",
    )(place, mine, theirs)


def per_device(tokens, norm_gain, w_query, w_keyvalue, w_out, cache_keys, cache_values, lengths):
    gx, gy = lax.axis_index("gx"), lax.axis_index("gy")
    place = jnp.stack([gx // 4, gx % 4, gy // 2, gy % 2]).astype(jnp.int32)

    stats, held = prepare(tokens)
    pieces = exchanged(along_x, [held] + [tokens] * 3)
    pieces += [other_core(piece) for piece in pieces]
    stats = lax.all_to_all(stats, ("gx", "gy"), 0, 0, tiled=True)
    w_pair = w_keyvalue.T
    weights = [w_query, other_core(w_query)]
    pairs = jnp.concatenate([w_pair, other_core(w_pair)], axis=0)
    gain = norm_gain[None]
    parts, gain_row, rest = project(place, gain, pieces, weights, pairs)
    gain_row, stats = lax.optimization_barrier((gain_row, stats))
    stats = stats.reshape(128, 256)
    sent = scale((1, 3), place, stats, gain_row, parts)
    kept = project_rest((2, 0), place, stats, gain_row, rest, weights, pairs)
    parts = [kept[1], sent[0], kept[0], sent[1]]

    parts = add_and_cut(exchanged(along_first, parts))
    parts = finish(place, exchanged(along_second, parts))
    packed = exchanged(along_x, parts)

    half_dim = HD // 2
    freqs = 10000.0 ** (-jnp.arange(half_dim, dtype=F32) / half_dim)
    positions = lengths[:, None] + jnp.arange(STEPS, dtype=jnp.int32)[None, :]
    angles = positions.reshape(-1).astype(F32)[:, None] * freqs
    attended = attend(
        place,
        packed,
        jnp.cos(angles),
        jnp.sin(angles),
        cache_keys,
        cache_values,
        lengths,
        2 * w_query.shape[1],
    )

    rows = line_up(place, exchanged(along_x, attended))
    rows = jnp.concatenate(exchanged(along_first, [rows] * 4), axis=0)
    near = [along_second(rows, 1), along_second(rows, 3)]
    late, *near = lax.optimization_barrier((rows, *near))
    blocks = [rows, near[0], along_second(late, 2), near[1]]
    weights = [w_out, other_core(w_out)]
    done, tiles = mix([blocks[0], blocks[1], blocks[3]], weights)
    parts = mix_rest(place, done, blocks[2], tiles)
    mine, theirs = last_sum(exchanged(along_x, parts))
    return interleave(place, mine, other_core(theirs))


def solution(mesh):
    return jax.shard_map(
        per_device,
        mesh=mesh,
        in_specs=(
            P("gy", "gx"),
            P("gx"),
            P("gx", "gy"),
            P("gx", "gy"),
            P("gy", "gx"),
            P(("gx", "gy"), None, None),
            P(("gx", "gy"), None, None),
            P(("gx", "gy")),
        ),
        out_specs=P("gy", "gx"),
        check_vma=False,
    )
```

```python
import functools

import jax
import jax.numpy as jnp
from jax import lax
from jax.experimental import pallas as pl
from jax.experimental.pallas import tpu as pltpu
from jax.sharding import PartitionSpec as P

D = 18432
HD = 256
GROUP = 2
STEPS = 2
VMEM = pl.BlockSpec(memory_space=pltpu.VMEM)
SMEM = pl.BlockSpec(memory_space=pltpu.SMEM)
ANY = pl.BlockSpec(memory_space=pl.ANY)
F32 = jnp.float32
BF16 = jnp.bfloat16


def params(mib):
    return pltpu.CompilerParams(vmem_limit_bytes=mib * 1024 * 1024)


def cost(flops, size):
    return pl.CostEstimate(flops=int(flops), bytes_accessed=int(size), transcendentals=0)


def exchange_pairs(core_along_y, m):
    pairs = []
    for d in range(128):
        far = 32 * m if d % 2 == core_along_y else 8 * m
        pairs.append((d, d ^ far))
    return pairs


def along_first(value, m):
    return lax.ppermute(value, ("gx", "gy"), exchange_pairs(0, m))


def along_second(value, m):
    return lax.ppermute(value, ("gx", "gy"), exchange_pairs(1, m))


def along_x(value, m):
    return lax.ppermute(value, "gy", [(g, g ^ (2 * m)) for g in range(8)])


def other_core(value):
    return lax.ppermute(value, "gy", [(g, g ^ 1) for g in range(8)])


ORDER = (0, 2, 1, 3)


def exchanged(along, parts, order=ORDER):
    return [along(parts[m], m) if m else parts[0] for m in order]


def groups_of(rows, first):
    groups = [rows[at + first : at + first + 8] for at in range(0, rows.shape[0], 16)]
    return jnp.concatenate(groups, axis=0)


def prepare_kernel(tokens, stats, copy):
    copy[...] = tokens[...]
    rows = tokens[...].astype(F32)
    by_core = [groups_of(rows, 0), groups_of(rows, 8)]
    lines = []
    for power in range(2):
        sums = [
            jnp.sum(part if power == 0 else part * part, axis=1, keepdims=True) for part in by_core
        ]
        column = jnp.broadcast_to(jnp.concatenate(sums, axis=0), (128, 128))
        lines.append(column.T[0:1])
    line = jnp.concatenate(lines, axis=1)
    stats[...] = jnp.broadcast_to(line[:, None, :], stats.shape)


def prepare(tokens):
    return pl.pallas_call(
        prepare_kernel,
        out_shape=[
            jax.ShapeDtypeStruct((128, 1, 256), F32),
            jax.ShapeDtypeStruct(tokens.shape, tokens.dtype),
        ],
        in_specs=[VMEM],
        out_specs=[VMEM] * 2,
        compiler_params=params(8),
        cost_estimate=cost(1e8, 1e6),
        name="prepare",
    )(tokens)


def load_tiles(source, tiles, sems, at):
    loads = []
    wide = tiles.shape[2]
    for t in range(source.shape[1] // wide):
        load = pltpu.make_async_copy(
            source.at[:, pl.ds(t * wide, wide)], tiles.at[at + t], sems.at[at + t]
        )
        load.start()
        loads.append(load)
    return loads


def fill_left(place, gain, pieces, left):
    y, z, x, c = place[0], place[1], place[2], place[3]
    gains = gain[...].astype(F32)
    left[256:272] = jnp.broadcast_to(gain[...], (16, gain.shape[1]))
    along_y = c == 0
    for i, m in enumerate(ORDER):
        to_y = x ^ m ^ y
        for j in range(2):
            rows = pieces[j * 4 + i][...].astype(F32)
            rows = jnp.where(along_y, groups_of(rows, 0), groups_of(rows, 8))
            rows = rows - jnp.sum(rows, axis=1, keepdims=True) / rows.shape[1]
            rows = (rows * gains).astype(BF16)
            for b in range(2):
                to_z = ((c ^ j) * 2 + b) ^ z
                first = jnp.where(along_y, to_y, to_z)
                second = jnp.where(along_y, to_z, to_y)
                at = jnp.where(first % 2 == 1, first // 2 * 128, 400 - first // 2 * 128)
                at = pl.multiple_of(at + second * 32, 16)
                left[pl.ds(at, 32)] = rows[b * 32 : b * 32 + 32]


def multiply(left, tiles, loads, pairs, put):
    wide = tiles.shape[2]
    width = tiles.shape[0] * wide
    dims = (((1,), (1,)), ((), ()))
    part = lax.dot_general(left, pairs[...], dims, preferred_element_type=F32)
    put(part, width, pairs.shape[0])
    for t, load in enumerate(loads):
        load.wait()
        put(jnp.dot(left, tiles[t], preferred_element_type=F32), t * wide, wide)


def load_both(weights, tiles, sems):
    count = tiles.shape[0] // 2
    return load_tiles(weights[0], tiles, sems, 0) + load_tiles(weights[1], tiles, sems, count)


def project_kernel(place, gain, *refs):
    pieces, weights, pairs = refs[:8], refs[8:10], refs[10]
    out, gain_row, rest, left, tiles, sems = refs[11:]
    loads = load_both(weights, tiles, sems)
    fill_left(place, gain, pieces, left)
    rest[...] = left[272:]

    def put(part, at, size):
        out[:, at : at + size] = part[:256].astype(BF16)
        gain_row[:, at : at + size] = part[256:264]

    multiply(left[:272], tiles, loads, pairs, put)


def project_scratch(weights):
    depth, width = weights[0].shape
    count = 2 * width // 512
    return [
        pltpu.VMEM((count, depth, 512), BF16),
        pltpu.SemaphoreType.DMA((count,)),
    ]


def project(place, gain, pieces, weights, pairs):
    depth = weights[0].shape[0]
    total = 2 * weights[0].shape[1] + pairs.shape[0]
    return pl.pallas_call(
        project_kernel,
        out_shape=[
            jax.ShapeDtypeStruct((256, total), BF16),
            jax.ShapeDtypeStruct((8, total), F32),
            jax.ShapeDtypeStruct((256, depth), BF16),
        ],
        in_specs=[SMEM] + [VMEM] * 9 + [ANY] * 2 + [VMEM],
        out_specs=[VMEM] * 3,
        scratch_shapes=[pltpu.VMEM((528, depth), BF16)] + project_scratch(weights),
        compiler_params=params(48),
        cost_estimate=cost(4e9, 1e7),
        name="project",
    )(place, gain, *pieces, *weights, pairs)


def fill_columns(place, stats, shift_of, scale_of):
    y, z = place[0], place[1]
    total = stats[0:8, :]
    for g in range(1, 16):
        total = total + stats[g * 8 : g * 8 + 8, :]
    mean = total[:, :128] / D
    variance = total[:, 128:] / D - mean * mean
    here = stats[pl.ds(pl.multiple_of((y * 4 + z) * 8, 8), 8), :]
    shift_columns = (here[:, :128] / (D // 16) - mean).T
    scale_columns = lax.rsqrt(variance + 1e-05).T
    for s in range(8):
        shift_of[s] = shift_columns[:, s : s + 1]
        scale_of[s] = scale_columns[:, s : s + 1]


def columns_of(place, block, second):
    y, z, c = place[0], place[1], place[3]
    token_y = y ^ jnp.where(c == 0, block, second)
    token_z = z ^ jnp.where(c == 0, second, block)
    rows = pl.ds(pl.multiple_of(c * 64 + token_z % 2 * 32, 32), 32)
    return token_y * 2 + token_z // 2, rows


def scale_kernel(blocks, place, stats, gain_row, parts, *refs):
    outs, shift_of, scale_of = refs[:2], refs[2], refs[3]
    fill_columns(place, stats, shift_of, scale_of)
    line = gain_row[0:1, :]
    for i, out in enumerate(outs):
        for second in range(4):
            s, at = columns_of(place, blocks[i], second)
            rows = parts[i * 128 + second * 32 : i * 128 + second * 32 + 32, :]
            rows = (rows.astype(F32) + shift_of[s, at] * line) * scale_of[s, at]
            out[second * 32 : second * 32 + 32, :] = rows.astype(BF16)


def scale(blocks, place, stats, gain_row, parts):
    out = jax.ShapeDtypeStruct((128, parts.shape[1]), BF16)
    return pl.pallas_call(
        functools.partial(scale_kernel, blocks),
        out_shape=[out] * 2,
        in_specs=[SMEM] + [VMEM] * 3,
        out_specs=[VMEM] * 2,
        scratch_shapes=[pltpu.VMEM((8, 128, 1), F32)] * 2,
        compiler_params=params(12),
        cost_estimate=cost(1e9, 2e6),
        name="scale",
    )(place, stats, gain_row, parts)


def project_rest_kernel(blocks, place, stats, gain_row, left, *refs):
    weights, pairs, outs = refs[:2], refs[2], refs[3:5]
    tiles, sems, shift_of, scale_of, shift, factor = refs[5:]
    loads = load_both(weights, tiles, sems)
    fill_columns(place, stats, shift_of, scale_of)
    for k in range(8):
        s, at = columns_of(place, blocks[k // 4], k % 4)
        shift[k * 32 : k * 32 + 32] = shift_of[s, at]
        factor[k * 32 : k * 32 + 32] = scale_of[s, at]

    def put(part, at, size):
        line = gain_row[0:1, at : at + size]
        part = ((part + shift[...] * line) * factor[...]).astype(BF16)
        for i, out in enumerate(outs):
            out[:, at : at + size] = part[i * 128 : i * 128 + 128]

    multiply(left[...], tiles, loads, pairs, put)


def project_rest(blocks, place, stats, gain_row, left, weights, pairs):
    out = jax.ShapeDtypeStruct((128, gain_row.shape[1]), BF16)
    return pl.pallas_call(
        functools.partial(project_rest_kernel, blocks),
        out_shape=[out] * 2,
        in_specs=[SMEM] + [VMEM] * 3 + [ANY] * 2 + [VMEM],
        out_specs=[VMEM] * 2,
        scratch_shapes=project_scratch(weights)
        + [pltpu.VMEM((8, 128, 1), F32)] * 2
        + [pltpu.VMEM((256, 1), F32)] * 2,
        compiler_params=params(48),
        cost_estimate=cost(5e9, 1e7),
        name="project_rest",
    )(place, stats, gain_row, left, *weights, pairs)


def sum_of(refs):
    total = refs[0][...].astype(F32)
    for ref in refs[1:]:
        total = total + ref[...].astype(F32)
    return total


def add_and_cut_kernel(*refs):
    total = sum_of(refs[:4]).astype(BF16)
    rows = total.shape[0] // 4
    for k in range(4):
        refs[4 + k][...] = total[k * rows : k * rows + rows]


def add_and_cut(values):
    rows, width = values[0].shape
    out = jax.ShapeDtypeStruct((rows // 4, width), BF16)
    return pl.pallas_call(
        add_and_cut_kernel,
        out_shape=[out] * 4,
        in_specs=[VMEM] * 4,
        out_specs=[VMEM] * 4,
        compiler_params=params(12),
        cost_estimate=cost(1e8, 1e6),
        name="add_and_cut",
    )(*values)


def finish_kernel(place, *refs):
    ins, outs, blocks = refs[:4], refs[4:8], refs[8]
    total = sum_of(ins)
    for i in range(4):
        blocks[place[2] ^ i] = total[i * 8 : i * 8 + 8]
    for m in range(4):
        outs[m][...] = blocks[m].astype(BF16)


def finish(place, values):
    rows, width = values[0].shape
    out = jax.ShapeDtypeStruct((rows // 4, width), BF16)
    return pl.pallas_call(
        finish_kernel,
        out_shape=[out] * 4,
        in_specs=[SMEM] + [VMEM] * 4,
        out_specs=[VMEM] * 4,
        scratch_shapes=[pltpu.VMEM((4, rows // 4, width), F32)],
        compiler_params=params(8),
        cost_estimate=cost(1e8, 1e6),
        name="finish",
    )(place, *values)


def line_up_kernel(place, *refs):
    ins, out, blocks = refs[:4], refs[4], refs[5]
    for m, rows in zip(ORDER, ins):
        blocks[place[2] ^ m] = rows[...].astype(F32)
    out[...] = blocks[...].reshape(out.shape).astype(BF16)


def line_up(place, values):
    rows, width = values[0].shape
    return pl.pallas_call(
        line_up_kernel,
        out_shape=jax.ShapeDtypeStruct((4 * rows, width), BF16),
        in_specs=[SMEM] + [VMEM] * 4,
        out_specs=VMEM,
        scratch_shapes=[pltpu.VMEM((4, rows, width), F32)],
        compiler_params=params(8),
        cost_estimate=cost(1e8, 1e6),
        name="line_up",
    )(place, *values)


def attend_one(request, lengths, keys, values, count, query_rows, new_kv, result):
    per = STEPS * count
    start = request * per
    query = jnp.concatenate([query_rows[i, pl.ds(start, per), :] for i in range(2)], axis=-1)
    query = (query.astype(BF16).astype(F32) * HD ** (-0.5)).astype(BF16)
    dims = (((1,), (1,)), ((), ()))
    cached = lax.dot_general(query, keys[...], dims, preferred_element_type=F32)
    slots = lax.broadcasted_iota(jnp.int32, cached.shape, 1)
    cached = jnp.where(slots < lengths[request], cached, -jnp.inf)
    fresh = lax.dot_general(query, new_kv[0], dims, preferred_element_type=F32)
    row_step = lax.broadcasted_iota(jnp.int32, fresh.shape, 0) // count
    key_step = lax.broadcasted_iota(jnp.int32, fresh.shape, 1) - request * STEPS
    fresh = jnp.where((key_step >= 0) & (key_step <= row_step), fresh, -jnp.inf)
    top = jnp.maximum(
        jnp.max(cached, axis=-1, keepdims=True), jnp.max(fresh, axis=-1, keepdims=True)
    )
    cached = jnp.exp(cached - top)
    fresh = jnp.exp(fresh - top)
    denom = jnp.sum(cached, axis=-1, keepdims=True) + jnp.sum(fresh, axis=-1, keepdims=True)
    mixed = jnp.dot(cached.astype(BF16), values[...], preferred_element_type=F32)
    mixed = mixed + jnp.dot(fresh.astype(BF16), new_kv[1], preferred_element_type=F32)
    mixed = mixed / denom
    for i in range(2):
        result[i, pl.ds(start, per), :] = mixed[:, i * 128 : i * 128 + 128]


def attend_kernel(lengths, place, *refs):
    packed, (cosine, sine, keys, values), outs = refs[:4], refs[4:8], refs[8:12]
    query_rows, new_pieces, new_kv, result, key_rows, value_rows, sems = refs[12:]
    requests = keys.shape[0]
    loads = []
    for r in range(requests):
        loads.append(
            [
                pltpu.make_async_copy(source.at[r], target.at[r], sems.at[r, i])
                for i, (source, target) in enumerate(((keys, key_rows), (values, value_rows)))
            ]
        )
        for load in loads[r]:
            load.start()
    width = outs[0].shape[1]
    heads = width // HD
    count = 4 * heads
    x, c = place[2], place[3]
    cos, sin = cosine[...], sine[...]

    def rotated(first, second):
        return first * cos - second * sin, second * cos + first * sin

    for m, rows in zip(ORDER, packed):
        rows = rows[...].astype(F32)
        for h in range(heads):
            head = rows[:, h * HD : h * HD + HD]
            for i, half in enumerate(rotated(head[:, :128], head[:, 128:])):
                query_rows[i, pl.ds(m * heads + h, 8, stride=count), :] = half
        size = (rows.shape[1] - width) // 2
        for j in range(2):
            at = width + j * size
            new_pieces[(x ^ m) * 2 + (c ^ j)] = rows[:, at : at + size]
    halves = [jnp.concatenate([new_pieces[i], new_pieces[i + 1]], axis=-1) for i in range(0, 8, 2)]
    new_kv[0] = jnp.concatenate(rotated(halves[0], halves[1]), axis=-1).astype(BF16)
    new_kv[1] = jnp.concatenate(halves[2:], axis=-1).astype(BF16)
    for at in range(0, requests, GROUP):
        for r in range(at, at + GROUP):
            for load in loads[r]:
                load.wait()
        for r in range(at, at + GROUP):
            attend_one(
                r, lengths, key_rows.at[r], value_rows.at[r], count, query_rows, new_kv, result
            )
    for m, out in enumerate(outs):
        halves = [
            result[i, pl.ds(m * heads + h, 8, stride=count), :]
            for h in range(heads)
            for i in range(2)
        ]
        out[...] = jnp.concatenate(halves, axis=-1).astype(BF16)


def attend(place, packed, cosine, sine, cache_keys, cache_values, lengths, width):
    total = packed[0].shape[1]
    count = 4 * (width // HD)
    return pl.pallas_call(
        attend_kernel,
        out_shape=[jax.ShapeDtypeStruct((8, width), BF16)] * 4,
        in_specs=[SMEM] * 2 + [VMEM] * 6 + [ANY] * 2,
        out_specs=[VMEM] * 4,
        scratch_shapes=[
            pltpu.VMEM((2, 8 * count, 128), F32),
            pltpu.VMEM((8, 8, (total - width) // 2), F32),
            pltpu.VMEM((2, 8, HD), BF16),
            pltpu.VMEM((2, 8 * count, 128), F32),
            pltpu.VMEM(cache_keys.shape, BF16),
            pltpu.VMEM(cache_values.shape, BF16),
            pltpu.SemaphoreType.DMA((cache_keys.shape[0], 2)),
        ],
        compiler_params=params(52),
        cost_estimate=cost(6e9, 1.8e7),
        name="attend",
    )(lengths, place, *packed, cosine, sine, cache_keys, cache_values)


def multiply_rows(lefts, tiles, put, loads=None):
    left = jnp.concatenate([ref[...] for ref in lefts], axis=0)
    depth = left.shape[1] // 2
    count = tiles.shape[0] // 2
    wide = tiles.shape[2]
    for t in range(count):
        if loads:
            loads[t].wait()
        part = jnp.dot(left[:, :depth], tiles[t], preferred_element_type=F32)
        if loads:
            loads[count + t].wait()
        part = part + jnp.dot(left[:, depth:], tiles[count + t], preferred_element_type=F32)
        put(part.astype(BF16), t * wide, wide)


def mix_kernel(*refs):
    lefts, weights, (out, tiles, sems) = refs[:3], refs[3:5], refs[5:]
    loads = load_tiles(weights[0], tiles, sems, 0) + load_tiles(weights[1], tiles, sems, 3)

    def put(part, at, size):
        out[:, at : at + size] = part

    multiply_rows(lefts, tiles, put, loads)


def mix_rest_kernel(place, done, last, tiles, *refs):
    outs, result = refs[:4], refs[4]
    y, z, x, c = place[0], place[1], place[2], place[3]
    along_y = c == 0

    def slots(second, first):
        to_x = y ^ x ^ jnp.where(along_y, first, second)
        token_z = z ^ jnp.where(along_y, second, first)
        return to_x, (token_z // 2 ^ c) * 2 + token_z % 2

    for k in range(12):
        result[slots((0, 1, 3)[k // 4], ORDER[k % 4])] = done[k * 32 : k * 32 + 32, :]

    def put(part, at, size):
        for k in range(4):
            to_x, slot = slots(2, ORDER[k])
            result[to_x, slot, :, at : at + size] = part[k * 32 : k * 32 + 32]

    multiply_rows([last], tiles, put)
    for k, out in enumerate(outs):
        out[...] = result[k].reshape(out.shape)


def mix(lefts, weights):
    depth, width = weights[0].shape
    return pl.pallas_call(
        mix_kernel,
        out_shape=[
            jax.ShapeDtypeStruct((384, width), BF16),
            jax.ShapeDtypeStruct((6, depth, width // 3), BF16),
        ],
        in_specs=[VMEM] * 3 + [ANY] * 2,
        out_specs=[VMEM] * 2,
        scratch_shapes=[pltpu.SemaphoreType.DMA((6,))],
        compiler_params=params(24),
        cost_estimate=cost(4e9, 8e6),
        name="mix",
    )(*lefts, *weights)


def mix_rest(place, done, last, tiles):
    width = done.shape[1]
    return pl.pallas_call(
        mix_rest_kernel,
        out_shape=[jax.ShapeDtypeStruct((128, width), BF16)] * 4,
        in_specs=[SMEM] + [VMEM] * 3,
        out_specs=[VMEM] * 4,
        scratch_shapes=[pltpu.VMEM((4, 4, 32, width), BF16)],
        compiler_params=params(24),
        cost_estimate=cost(4e9, 8e6),
        name="mix_rest",
    )(place, done, last, tiles)


def last_sum_kernel(*refs):
    total = sum_of(refs[:4]).astype(BF16)
    refs[4][...] = total[:64]
    refs[5][...] = total[64:]


def last_sum(values):
    half = jax.ShapeDtypeStruct((64, values[0].shape[1]), BF16)
    return pl.pallas_call(
        last_sum_kernel,
        out_shape=[half] * 2,
        in_specs=[VMEM] * 4,
        out_specs=[VMEM] * 2,
        compiler_params=params(8),
        cost_estimate=cost(1e8, 1e6),
        name="last_sum",
    )(*values)


def per_device(tokens, norm_gain, w_query, w_keyvalue, w_out, cache_keys, cache_values, lengths):
    gx, gy = lax.axis_index("gx"), lax.axis_index("gy")
    place = jnp.stack([gx // 4, gx % 4, gy // 2, gy % 2]).astype(jnp.int32)

    stats, held = prepare(tokens)
    pieces = exchanged(along_x, [held] + [tokens] * 3)
    pieces += [other_core(piece) for piece in pieces]
    stats = lax.all_to_all(stats, ("gx", "gy"), 0, 0, tiled=True)
    w_pair = w_keyvalue.T
    weights = [w_query, other_core(w_query)]
    pairs = jnp.concatenate([w_pair, other_core(w_pair)], axis=0)
    gain = norm_gain[None]
    parts, gain_row, rest = project(place, gain, pieces, weights, pairs)
    gain_row, stats = lax.optimization_barrier((gain_row, stats))
    stats = stats.reshape(128, 256)
    sent = scale((1, 3), place, stats, gain_row, parts)
    kept = project_rest((2, 0), place, stats, gain_row, rest, weights, pairs)
    parts = [kept[1], sent[0], kept[0], sent[1]]

    parts = add_and_cut(exchanged(along_first, parts))
    parts = finish(place, exchanged(along_second, parts))
    packed = exchanged(along_x, parts)

    half_dim = HD // 2
    freqs = 10000.0 ** (-jnp.arange(half_dim, dtype=F32) / half_dim)
    positions = lengths[:, None] + jnp.arange(STEPS, dtype=jnp.int32)[None, :]
    angles = positions.reshape(-1).astype(F32)[:, None] * freqs
    attended = attend(
        place,
        packed,
        jnp.cos(angles),
        jnp.sin(angles),
        cache_keys,
        cache_values,
        lengths,
        2 * w_query.shape[1],
    )

    rows = line_up(place, exchanged(along_x, attended))
    rows = jnp.concatenate(exchanged(along_first, [rows] * 4), axis=0)
    near = [along_second(rows, 1), along_second(rows, 3)]
    late, near[0] = lax.optimization_barrier((rows, near[0]))
    blocks = [rows, near[0], along_second(late, 2), near[1]]
    weights = [w_out, other_core(w_out)]
    done, tiles = mix([blocks[0], blocks[1], blocks[3]], weights)
    parts = mix_rest(place, done, blocks[2], tiles)
    mine, theirs = last_sum(exchanged(along_x, parts))
    theirs, width = other_core(theirs), mine.shape[1]
    pair = jnp.stack([mine.reshape(8, 8, width), theirs.reshape(8, 8, width)], axis=1)
    swapped = jnp.stack([theirs.reshape(8, 8, width), mine.reshape(8, 8, width)], axis=1)
    return jnp.where(place[3] == 1, swapped, pair).reshape(128, width)


def solution(mesh):
    return jax.shard_map(
        per_device,
        mesh=mesh,
        in_specs=(
            P("gy", "gx"),
            P("gx"),
            P("gx", "gy"),
            P("gx", "gy"),
            P("gy", "gx"),
            P(("gx", "gy"), None, None),
            P(("gx", "gy"), None, None),
            P(("gx", "gy")),
        ),
        out_specs=P("gy", "gx"),
        check_vma=False,
    )
```

```python
import functools

import jax
import jax.numpy as jnp
from jax import lax
from jax.experimental import pallas as pl
from jax.experimental.pallas import tpu as pltpu
from jax.sharding import PartitionSpec as P

D = 18432
HD = 256
GROUP = 2
STEPS = 2
VMEM = pl.BlockSpec(memory_space=pltpu.VMEM)
SMEM = pl.BlockSpec(memory_space=pltpu.SMEM)
ANY = pl.BlockSpec(memory_space=pl.ANY)
F32 = jnp.float32
BF16 = jnp.bfloat16


def params(mib):
    return pltpu.CompilerParams(vmem_limit_bytes=mib * 1024 * 1024)


def cost(flops, size):
    return pl.CostEstimate(flops=int(flops), bytes_accessed=int(size), transcendentals=0)


def exchange_pairs(core_along_y, m):
    pairs = []
    for d in range(128):
        far = 32 * m if d % 2 == core_along_y else 8 * m
        pairs.append((d, d ^ far))
    return pairs


def along_first(value, m):
    return lax.ppermute(value, ("gx", "gy"), exchange_pairs(0, m))


def along_second(value, m):
    return lax.ppermute(value, ("gx", "gy"), exchange_pairs(1, m))


def along_x(value, m):
    return lax.ppermute(value, "gy", [(g, g ^ (2 * m)) for g in range(8)])


def other_core(value):
    return lax.ppermute(value, "gy", [(g, g ^ 1) for g in range(8)])


ORDER = (0, 2, 1, 3)


def exchanged(along, parts, order=ORDER):
    return [along(parts[m], m) if m else parts[0] for m in order]


def groups_of(rows, first):
    groups = [rows[at + first : at + first + 8] for at in range(0, rows.shape[0], 16)]
    return jnp.concatenate(groups, axis=0)


def prepare_kernel(tokens, stats, copy):
    copy[...] = tokens[...]
    rows = tokens[...].astype(F32)
    by_core = [groups_of(rows, 0), groups_of(rows, 8)]
    lines = []
    for power in range(2):
        sums = [
            jnp.sum(part if power == 0 else part * part, axis=1, keepdims=True) for part in by_core
        ]
        column = jnp.broadcast_to(jnp.concatenate(sums, axis=0), (128, 128))
        lines.append(column.T[0:1])
    line = jnp.concatenate(lines, axis=1)
    stats[...] = jnp.broadcast_to(line[:, None, :], stats.shape)


def prepare(tokens):
    return pl.pallas_call(
        prepare_kernel,
        out_shape=[
            jax.ShapeDtypeStruct((128, 1, 256), F32),
            jax.ShapeDtypeStruct(tokens.shape, tokens.dtype),
        ],
        in_specs=[VMEM],
        out_specs=[VMEM] * 2,
        compiler_params=params(8),
        cost_estimate=cost(1e8, 1e6),
        name="prepare",
    )(tokens)


def load_tiles(source, tiles, sems, at):
    loads = []
    wide = tiles.shape[2]
    for t in range(source.shape[1] // wide):
        load = pltpu.make_async_copy(
            source.at[:, pl.ds(t * wide, wide)], tiles.at[at + t], sems.at[at + t]
        )
        load.start()
        loads.append(load)
    return loads


def fill_left(place, gain, pieces, left):
    y, z, x, c = place[0], place[1], place[2], place[3]
    gains = gain[...].astype(F32)
    left[256:272] = jnp.broadcast_to(gain[...], (16, gain.shape[1]))
    along_y = c == 0
    for i, m in enumerate(ORDER):
        to_y = x ^ m ^ y
        for j in range(2):
            rows = pieces[j * 4 + i][...].astype(F32)
            rows = jnp.where(along_y, groups_of(rows, 0), groups_of(rows, 8))
            rows = rows - jnp.sum(rows, axis=1, keepdims=True) / rows.shape[1]
            rows = (rows * gains).astype(BF16)
            for b in range(2):
                to_z = ((c ^ j) * 2 + b) ^ z
                first = jnp.where(along_y, to_y, to_z)
                second = jnp.where(along_y, to_z, to_y)
                at = jnp.where(first % 2 == 1, first // 2 * 128, 400 - first // 2 * 128)
                at = pl.multiple_of(at + second * 32, 16)
                left[pl.ds(at, 32)] = rows[b * 32 : b * 32 + 32]


def multiply(left, tiles, loads, pairs, put):
    wide = tiles.shape[2]
    width = tiles.shape[0] * wide
    dims = (((1,), (1,)), ((), ()))
    part = lax.dot_general(left, pairs[...], dims, preferred_element_type=F32)
    put(part, width, pairs.shape[0])
    for t, load in enumerate(loads):
        load.wait()
        put(jnp.dot(left, tiles[t], preferred_element_type=F32), t * wide, wide)


def load_both(weights, tiles, sems):
    count = tiles.shape[0] // 2
    return load_tiles(weights[0], tiles, sems, 0) + load_tiles(weights[1], tiles, sems, count)


def project_kernel(place, gain, *refs):
    pieces, weights, pairs = refs[:8], refs[8:10], refs[10]
    out, gain_row, rest, left, tiles, sems = refs[11:]
    loads = load_both(weights, tiles, sems)
    fill_left(place, gain, pieces, left)
    rest[...] = left[272:]

    def put(part, at, size):
        out[:, at : at + size] = part[:256].astype(BF16)
        gain_row[:, at : at + size] = part[256:264]

    multiply(left[:272], tiles, loads, pairs, put)


def project_scratch(weights):
    depth, width = weights[0].shape
    count = 2 * width // 512
    return [
        pltpu.VMEM((count, depth, 512), BF16),
        pltpu.SemaphoreType.DMA((count,)),
    ]


def project(place, gain, pieces, weights, pairs):
    depth = weights[0].shape[0]
    total = 2 * weights[0].shape[1] + pairs.shape[0]
    return pl.pallas_call(
        project_kernel,
        out_shape=[
            jax.ShapeDtypeStruct((256, total), BF16),
            jax.ShapeDtypeStruct((8, total), F32),
            jax.ShapeDtypeStruct((256, depth), BF16),
        ],
        in_specs=[SMEM] + [VMEM] * 9 + [ANY] * 2 + [VMEM],
        out_specs=[VMEM] * 3,
        scratch_shapes=[pltpu.VMEM((528, depth), BF16)] + project_scratch(weights),
        compiler_params=params(48),
        cost_estimate=cost(4e9, 1e7),
        name="project",
    )(place, gain, *pieces, *weights, pairs)


def fill_columns(place, stats, shift_of, scale_of):
    y, z = place[0], place[1]
    total = stats[0:8, :]
    for g in range(1, 16):
        total = total + stats[g * 8 : g * 8 + 8, :]
    mean = total[:, :128] / D
    variance = total[:, 128:] / D - mean * mean
    here = stats[pl.ds(pl.multiple_of((y * 4 + z) * 8, 8), 8), :]
    shift_columns = (here[:, :128] / (D // 16) - mean).T
    scale_columns = lax.rsqrt(variance + 1e-05).T
    for s in range(8):
        shift_of[s] = shift_columns[:, s : s + 1]
        scale_of[s] = scale_columns[:, s : s + 1]


def columns_of(place, block, second):
    y, z, c = place[0], place[1], place[3]
    token_y = y ^ jnp.where(c == 0, block, second)
    token_z = z ^ jnp.where(c == 0, second, block)
    rows = pl.ds(pl.multiple_of(c * 64 + token_z % 2 * 32, 32), 32)
    return token_y * 2 + token_z // 2, rows


def scale_kernel(blocks, place, stats, gain_row, parts, *refs):
    outs, shift_of, scale_of = refs[:2], refs[2], refs[3]
    fill_columns(place, stats, shift_of, scale_of)
    line = gain_row[0:1, :]
    for i, out in enumerate(outs):
        for second in range(4):
            s, at = columns_of(place, blocks[i], second)
            rows = parts[i * 128 + second * 32 : i * 128 + second * 32 + 32, :]
            rows = (rows.astype(F32) + shift_of[s, at] * line) * scale_of[s, at]
            out[second * 32 : second * 32 + 32, :] = rows.astype(BF16)


def scale(blocks, place, stats, gain_row, parts):
    out = jax.ShapeDtypeStruct((128, parts.shape[1]), BF16)
    return pl.pallas_call(
        functools.partial(scale_kernel, blocks),
        out_shape=[out] * 2,
        in_specs=[SMEM] + [VMEM] * 3,
        out_specs=[VMEM] * 2,
        scratch_shapes=[pltpu.VMEM((8, 128, 1), F32)] * 2,
        compiler_params=params(12),
        cost_estimate=cost(1e9, 2e6),
        name="scale",
    )(place, stats, gain_row, parts)


def project_rest_kernel(blocks, place, stats, gain_row, left, *refs):
    weights, pairs, outs = refs[:2], refs[2], refs[3:5]
    tiles, sems, shift_of, scale_of, shift, factor = refs[5:]
    loads = load_both(weights, tiles, sems)
    fill_columns(place, stats, shift_of, scale_of)
    for k in range(8):
        s, at = columns_of(place, blocks[k // 4], k % 4)
        shift[k * 32 : k * 32 + 32] = shift_of[s, at]
        factor[k * 32 : k * 32 + 32] = scale_of[s, at]

    def put(part, at, size):
        line = gain_row[0:1, at : at + size]
        part = ((part + shift[...] * line) * factor[...]).astype(BF16)
        for i, out in enumerate(outs):
            out[:, at : at + size] = part[i * 128 : i * 128 + 128]

    multiply(left[...], tiles, loads, pairs, put)


def project_rest(blocks, place, stats, gain_row, left, weights, pairs):
    out = jax.ShapeDtypeStruct((128, gain_row.shape[1]), BF16)
    return pl.pallas_call(
        functools.partial(project_rest_kernel, blocks),
        out_shape=[out] * 2,
        in_specs=[SMEM] + [VMEM] * 3 + [ANY] * 2 + [VMEM],
        out_specs=[VMEM] * 2,
        scratch_shapes=project_scratch(weights)
        + [pltpu.VMEM((8, 128, 1), F32)] * 2
        + [pltpu.VMEM((256, 1), F32)] * 2,
        compiler_params=params(48),
        cost_estimate=cost(5e9, 1e7),
        name="project_rest",
    )(place, stats, gain_row, left, *weights, pairs)


def sum_of(refs):
    total = refs[0][...].astype(F32)
    for ref in refs[1:]:
        total = total + ref[...].astype(F32)
    return total


def add_and_cut_kernel(*refs):
    total = sum_of(refs[:4]).astype(BF16)
    rows = total.shape[0] // 4
    for k in range(4):
        refs[4 + k][...] = total[k * rows : k * rows + rows]


def add_and_cut(values):
    rows, width = values[0].shape
    out = jax.ShapeDtypeStruct((rows // 4, width), BF16)
    return pl.pallas_call(
        add_and_cut_kernel,
        out_shape=[out] * 4,
        in_specs=[VMEM] * 4,
        out_specs=[VMEM] * 4,
        compiler_params=params(12),
        cost_estimate=cost(1e8, 1e6),
        name="add_and_cut",
    )(*values)


def finish_kernel(place, *refs):
    ins, outs, blocks = refs[:4], refs[4:8], refs[8]
    total = sum_of(ins)
    for i in range(4):
        blocks[place[2] ^ i] = total[i * 8 : i * 8 + 8]
    for m in range(4):
        outs[m][...] = blocks[m].astype(BF16)


def finish(place, values):
    rows, width = values[0].shape
    out = jax.ShapeDtypeStruct((rows // 4, width), BF16)
    return pl.pallas_call(
        finish_kernel,
        out_shape=[out] * 4,
        in_specs=[SMEM] + [VMEM] * 4,
        out_specs=[VMEM] * 4,
        scratch_shapes=[pltpu.VMEM((4, rows // 4, width), F32)],
        compiler_params=params(8),
        cost_estimate=cost(1e8, 1e6),
        name="finish",
    )(place, *values)


def line_up_kernel(place, *refs):
    ins, out, blocks = refs[:4], refs[4], refs[5]
    for m, rows in zip(ORDER, ins):
        blocks[place[2] ^ m] = rows[...].astype(F32)
    out[...] = blocks[...].reshape(out.shape).astype(BF16)


def line_up(place, values):
    rows, width = values[0].shape
    return pl.pallas_call(
        line_up_kernel,
        out_shape=jax.ShapeDtypeStruct((4 * rows, width), BF16),
        in_specs=[SMEM] + [VMEM] * 4,
        out_specs=VMEM,
        scratch_shapes=[pltpu.VMEM((4, rows, width), F32)],
        compiler_params=params(8),
        cost_estimate=cost(1e8, 1e6),
        name="line_up",
    )(place, *values)


def attend_one(request, lengths, keys, values, count, query_rows, new_kv, result):
    per = STEPS * count
    start = request * per
    query = jnp.concatenate([query_rows[i, pl.ds(start, per), :] for i in range(2)], axis=-1)
    query = (query.astype(BF16).astype(F32) * HD ** (-0.5)).astype(BF16)
    dims = (((1,), (1,)), ((), ()))
    cached = lax.dot_general(query, keys[...], dims, preferred_element_type=F32)
    half = cached.shape[1] // 2
    slots = lax.broadcasted_iota(jnp.int32, (per, half), 1) + half
    masked = jnp.where(slots < lengths[request], cached[:, half:], -jnp.inf)
    cached = jnp.concatenate([cached[:, :half], masked], axis=1)
    fresh = lax.dot_general(query, new_kv[0], dims, preferred_element_type=F32)
    row_step = lax.broadcasted_iota(jnp.int32, fresh.shape, 0) // count
    key_step = lax.broadcasted_iota(jnp.int32, fresh.shape, 1) - request * STEPS
    fresh = jnp.where((key_step >= 0) & (key_step <= row_step), fresh, -jnp.inf)
    top = jnp.maximum(
        jnp.max(cached, axis=-1, keepdims=True), jnp.max(fresh, axis=-1, keepdims=True)
    )
    cached = jnp.exp(cached - top)
    fresh = jnp.exp(fresh - top)
    denom = jnp.sum(cached, axis=-1, keepdims=True) + jnp.sum(fresh, axis=-1, keepdims=True)
    mixed = jnp.dot(cached.astype(BF16), values[...], preferred_element_type=F32)
    mixed = mixed + jnp.dot(fresh.astype(BF16), new_kv[1], preferred_element_type=F32)
    mixed = mixed / denom
    for i in range(2):
        result[i, pl.ds(start, per), :] = mixed[:, i * 128 : i * 128 + 128]


def attend_kernel(lengths, place, *refs):
    packed, (cosine, sine, keys, values), outs = refs[:4], refs[4:8], refs[8:12]
    query_rows, new_pieces, new_kv, result, key_rows, value_rows, sems = refs[12:]
    requests = keys.shape[0]
    loads = []
    for r in range(requests):
        loads.append(
            [
                pltpu.make_async_copy(source.at[r], target.at[r], sems.at[r, i])
                for i, (source, target) in enumerate(((keys, key_rows), (values, value_rows)))
            ]
        )
        for load in loads[r]:
            load.start()
    width = outs[0].shape[1]
    heads = width // HD
    count = 4 * heads
    x, c = place[2], place[3]
    cos, sin = cosine[...], sine[...]

    def rotated(first, second):
        return first * cos - second * sin, second * cos + first * sin

    for m, rows in zip(ORDER, packed):
        rows = rows[...].astype(F32)
        for h in range(heads):
            head = rows[:, h * HD : h * HD + HD]
            for i, half in enumerate(rotated(head[:, :128], head[:, 128:])):
                query_rows[i, pl.ds(m * heads + h, 8, stride=count), :] = half
        size = (rows.shape[1] - width) // 2
        for j in range(2):
            at = width + j * size
            new_pieces[(x ^ m) * 2 + (c ^ j)] = rows[:, at : at + size]
    halves = [jnp.concatenate([new_pieces[i], new_pieces[i + 1]], axis=-1) for i in range(0, 8, 2)]
    new_kv[0] = jnp.concatenate(rotated(halves[0], halves[1]), axis=-1).astype(BF16)
    new_kv[1] = jnp.concatenate(halves[2:], axis=-1).astype(BF16)
    for at in range(0, requests, GROUP):
        for r in range(at, at + GROUP):
            for load in loads[r]:
                load.wait()
        for r in range(at, at + GROUP):
            attend_one(
                r, lengths, key_rows.at[r], value_rows.at[r], count, query_rows, new_kv, result
            )
    for m, out in enumerate(outs):
        halves = [
            result[i, pl.ds(m * heads + h, 8, stride=count), :]
            for h in range(heads)
            for i in range(2)
        ]
        out[...] = jnp.concatenate(halves, axis=-1).astype(BF16)


def attend(place, packed, cosine, sine, cache_keys, cache_values, lengths, width):
    total = packed[0].shape[1]
    count = 4 * (width // HD)
    return pl.pallas_call(
        attend_kernel,
        out_shape=[jax.ShapeDtypeStruct((8, width), BF16)] * 4,
        in_specs=[SMEM] * 2 + [VMEM] * 6 + [ANY] * 2,
        out_specs=[VMEM] * 4,
        scratch_shapes=[
            pltpu.VMEM((2, 8 * count, 128), F32),
            pltpu.VMEM((8, 8, (total - width) // 2), F32),
            pltpu.VMEM((2, 8, HD), BF16),
            pltpu.VMEM((2, 8 * count, 128), F32),
            pltpu.VMEM(cache_keys.shape, BF16),
            pltpu.VMEM(cache_values.shape, BF16),
            pltpu.SemaphoreType.DMA((cache_keys.shape[0], 2)),
        ],
        compiler_params=params(52),
        cost_estimate=cost(6e9, 1.8e7),
        name="attend",
    )(lengths, place, *packed, cosine, sine, cache_keys, cache_values)


def multiply_rows(lefts, tiles, put, loads=None):
    left = jnp.concatenate([ref[...] for ref in lefts], axis=0)
    depth = left.shape[1] // 2
    count = tiles.shape[0] // 2
    wide = tiles.shape[2]
    for t in range(count):
        if loads:
            loads[t].wait()
        part = jnp.dot(left[:, :depth], tiles[t], preferred_element_type=F32)
        if loads:
            loads[count + t].wait()
        part = part + jnp.dot(left[:, depth:], tiles[count + t], preferred_element_type=F32)
        put(part.astype(BF16), t * wide, wide)


def mix_kernel(*refs):
    lefts, weights, (out, tiles, sems) = refs[:3], refs[3:5], refs[5:]
    loads = load_tiles(weights[0], tiles, sems, 0) + load_tiles(weights[1], tiles, sems, 3)

    def put(part, at, size):
        out[:, at : at + size] = part

    multiply_rows(lefts, tiles, put, loads)


def mix_rest_kernel(place, done, last, tiles, *refs):
    outs, result = refs[:4], refs[4]
    y, z, x, c = place[0], place[1], place[2], place[3]
    along_y = c == 0

    def slots(second, first):
        to_x = y ^ x ^ jnp.where(along_y, first, second)
        token_z = z ^ jnp.where(along_y, second, first)
        return to_x, (token_z // 2 ^ c) * 2 + token_z % 2

    for k in range(12):
        result[slots((0, 1, 3)[k // 4], ORDER[k % 4])] = done[k * 32 : k * 32 + 32, :]

    def put(part, at, size):
        for k in range(4):
            to_x, slot = slots(2, ORDER[k])
            result[to_x, slot, :, at : at + size] = part[k * 32 : k * 32 + 32]

    multiply_rows([last], tiles, put)
    for k, out in enumerate(outs):
        out[...] = result[k].reshape(out.shape)


def mix(lefts, weights):
    depth, width = weights[0].shape
    return pl.pallas_call(
        mix_kernel,
        out_shape=[
            jax.ShapeDtypeStruct((384, width), BF16),
            jax.ShapeDtypeStruct((6, depth, width // 3), BF16),
        ],
        in_specs=[VMEM] * 3 + [ANY] * 2,
        out_specs=[VMEM] * 2,
        scratch_shapes=[pltpu.SemaphoreType.DMA((6,))],
        compiler_params=params(24),
        cost_estimate=cost(4e9, 8e6),
        name="mix",
    )(*lefts, *weights)


def mix_rest(place, done, last, tiles):
    width = done.shape[1]
    return pl.pallas_call(
        mix_rest_kernel,
        out_shape=[jax.ShapeDtypeStruct((128, width), BF16)] * 4,
        in_specs=[SMEM] + [VMEM] * 3,
        out_specs=[VMEM] * 4,
        scratch_shapes=[pltpu.VMEM((4, 4, 32, width), BF16)],
        compiler_params=params(24),
        cost_estimate=cost(4e9, 8e6),
        name="mix_rest",
    )(place, done, last, tiles)


def last_sum_kernel(*refs):
    total = sum_of(refs[:4]).astype(BF16)
    refs[4][...] = total[:64]
    refs[5][...] = total[64:]


def last_sum(values):
    half = jax.ShapeDtypeStruct((64, values[0].shape[1]), BF16)
    return pl.pallas_call(
        last_sum_kernel,
        out_shape=[half] * 2,
        in_specs=[VMEM] * 4,
        out_specs=[VMEM] * 2,
        compiler_params=params(8),
        cost_estimate=cost(1e8, 1e6),
        name="last_sum",
    )(*values)


def per_device(tokens, norm_gain, w_query, w_keyvalue, w_out, cache_keys, cache_values, lengths):
    gx, gy = lax.axis_index("gx"), lax.axis_index("gy")
    place = jnp.stack([gx // 4, gx % 4, gy // 2, gy % 2]).astype(jnp.int32)

    stats, held = prepare(tokens)
    pieces = exchanged(along_x, [held] + [tokens] * 3)
    pieces += [other_core(piece) for piece in pieces]
    stats = lax.all_to_all(stats, ("gx", "gy"), 0, 0, tiled=True)
    w_pair = w_keyvalue.T
    weights = [w_query, other_core(w_query)]
    pairs = jnp.concatenate([w_pair, other_core(w_pair)], axis=0)
    gain = norm_gain[None]
    parts, gain_row, rest = project(place, gain, pieces, weights, pairs)
    gain_row, stats = lax.optimization_barrier((gain_row, stats))
    stats = stats.reshape(128, 256)
    sent = scale((1, 3), place, stats, gain_row, parts)
    kept = project_rest((2, 0), place, stats, gain_row, rest, weights, pairs)
    parts = [kept[1], sent[0], kept[0], sent[1]]

    parts = add_and_cut(exchanged(along_first, parts))
    parts = finish(place, exchanged(along_second, parts))
    packed = exchanged(along_x, parts)

    half_dim = HD // 2
    freqs = 10000.0 ** (-jnp.arange(half_dim, dtype=F32) / half_dim)
    positions = lengths[:, None] + jnp.arange(STEPS, dtype=jnp.int32)[None, :]
    angles = positions.reshape(-1).astype(F32)[:, None] * freqs
    attended = attend(
        place,
        packed,
        jnp.cos(angles),
        jnp.sin(angles),
        cache_keys,
        cache_values,
        lengths,
        2 * w_query.shape[1],
    )

    rows = line_up(place, exchanged(along_x, attended))
    rows = jnp.concatenate(exchanged(along_first, [rows] * 4), axis=0)
    near = [along_second(rows, 1), along_second(rows, 3)]
    late, near[0] = lax.optimization_barrier((rows, near[0]))
    blocks = [rows, near[0], along_second(late, 2), near[1]]
    weights = [w_out, other_core(w_out)]
    done, tiles = mix([blocks[0], blocks[1], blocks[3]], weights)
    parts = mix_rest(place, done, blocks[2], tiles)
    mine, theirs = last_sum(exchanged(along_x, parts))
    theirs, width = other_core(theirs), mine.shape[1]
    pair = jnp.stack([mine.reshape(8, 8, width), theirs.reshape(8, 8, width)], axis=1)
    swapped = jnp.stack([theirs.reshape(8, 8, width), mine.reshape(8, 8, width)], axis=1)
    return jnp.where(place[3] == 1, swapped, pair).reshape(128, width)


def solution(mesh):
    return jax.shard_map(
        per_device,
        mesh=mesh,
        in_specs=(
            P("gy", "gx"),
            P("gx"),
            P("gx", "gy"),
            P("gx", "gy"),
            P("gy", "gx"),
            P(("gx", "gy"), None, None),
            P(("gx", "gy"), None, None),
            P(("gx", "gy")),
        ),
        out_specs=P("gy", "gx"),
        check_vma=False,
    )
```
